128 devices in a mesh: section: 2 (over core), dp: 32 (over x, y, z_lo), tensor: 2 (over z_hi).
Axes of the slice: x: 4, y: 4, z: 4 (z_hi: 2, z_lo: 2; z = z_hi * 2 + z_lo), core: 2. Of those that a mesh axis runs over, the one named last changes fastest.
Arguments:
- embeddings: bfloat16 [128, 256, 768], P('dp'), may hold values from -6 to 6
- species: int32 [128], P('dp'), may hold values from 0 to 1
- ln1_gain: float32 [2, 768], P('section'), may hold values from 0.1 to 1.9
- ln1_bias: float32 [2, 768], P('section'), may hold values from -1.5 to 1.5
- qkv_weight: bfloat16 [2, 768, 3, 768], P('section', None, None, 'tensor'), may hold values from -0.21875 to 0.21875
- out_weight: bfloat16 [2, 768, 768], P('section', 'tensor'), may hold values from -0.625 to 0.625
- ln2_gain: float32 [2, 768], P('section'), may hold values from 0.1 to 1.9
- ln2_bias: float32 [2, 768], P('section'), may hold values from -1.5 to 1.5
- up_weight: bfloat16 [2, 768, 3072], P('section', None, 'tensor'), may hold values from -0.21875 to 0.21875
- up_bias: float32 [2, 3072], P('section', 'tensor'), may hold values from -3 to 3
- down_weight: bfloat16 [2, 3072, 768], P('section', 'tensor'), may hold values from -0.109375 to 0.109375
- species_bias: float32 [2, 2, 768], P('section'), may hold values from -3 to 3
- out_cotangent: float32 [128, 256, 768], P('dp'), may hold values from -6 to 6
Outputs:
- layer_out: float32 [2, 128, 256, 768], P('section', 'dp')
- input_grad: float32 [2, 128, 256, 768], P('section', 'dp')
- grad_ln1_gain: float32 [2, 768], P('section')
- grad_ln1_bias: float32 [2, 768], P('section')
- grad_qkv: float32 [2, 768, 3, 768], P('section', None, None, 'tensor')
- grad_out: float32 [2, 768, 768], P('section', 'tensor')
- grad_ln2_gain: float32 [2, 768], P('section')
- grad_ln2_bias: float32 [2, 768], P('section')
- grad_up: float32 [2, 768, 3072], P('section', None, 'tensor')
- grad_up_bias: float32 [2, 3072], P('section', 'tensor')
- grad_down: float32 [2, 3072, 768], P('section', 'tensor')
- grad_species: float32 [2, 2, 768], P('section')
The draws below stay inside these ranges and needn't reach their ends.
All inputs are finite; a program needn't handle non-finite values.
Results may differ from the reference program's by a relative error of at most 0.024.
Values may be sent and summed in bfloat16 or wider, within the bound.
A program may use at most 320 MiB of HBM per device.

```python
import jax
import jax.numpy as jnp
from jax import lax

D = 768
FF = 3072
HEAD = 64
LEN = 256
LAYERS = 2
SPECIES = 2
CELLS = 128
N_TENSOR = 2


def touch_ends(values, stream_key, least, high):
    spot = [jax.random.randint(jax.random.fold_in(stream_key, axis), (), 0, length) for axis, length in enumerate(values.shape)]
    widest = values.shape.index(max(values.shape))
    next_to = spot[:widest] + [(spot[widest] + 1) % values.shape[widest]] + spot[widest + 1:]
    return values.at[tuple(spot)].set(least).at[tuple(next_to)].set(high)


def block_levels(own_key, shape, shards, least, largest):
    def one(position, parts):
        steps = jax.random.uniform(jax.random.fold_in(jax.random.fold_in(own_key, 6), position), (parts,), jnp.float32, least / len(shards), largest / len(shards))
        return jnp.repeat(jnp.exp(steps), shape[position] // parts).reshape((-1,) + (1,) * (len(shape) - position - 1))

    factor_of = one(*shards[0])
    for cut in shards[1:]:
        factor_of = factor_of * one(*cut)
    return factor_of


def centred(own_key, extent, scale, reach, cuts=(), kind=jnp.bfloat16):
    result = scale * jax.random.normal(own_key, extent, jnp.float32)
    if cuts:
        result = result * block_levels(own_key, extent, cuts, -0.22, 0.18)
    return jnp.clip(result, -reach, reach).astype(kind)


def setup_inputs(seed: int = 0) -> dict:
    splits = jax.random.split(jax.random.key(seed), 14)
    embeddings = centred(splits[0], (CELLS, LEN, D), 1.0, 6.0, ((0, 32),))
    species = touch_ends(jax.random.randint(splits[1], (CELLS,), 0, SPECIES), jax.random.fold_in(splits[1], 1), 0, SPECIES - 1).astype(jnp.int32)
    ln1_gain = jnp.clip(1.0 + 0.18 * jax.random.normal(splits[2], (LAYERS, D), jnp.float32), 0.1, 1.9)
    ln1_bias = centred(splits[3], (LAYERS, D), 0.3, 1.5, ((0, 2),), jnp.float32)
    qkv_weight = centred(splits[4], (LAYERS, D, 3, D), D ** -0.5, 0.21875, ((0, 2), (3, 2)))
    out_weight = centred(splits[5], (LAYERS, D, D), (D // 8) ** -0.5, 0.625, ((0, 2), (1, 2)))
    ln2_gain = jnp.clip(1.0 + 0.18 * jax.random.normal(splits[6], (LAYERS, D), jnp.float32), 0.1, 1.9)
    ln2_bias = centred(splits[7], (LAYERS, D), 0.3, 1.5, ((0, 2),), jnp.float32)
    up_weight = centred(splits[8], (LAYERS, D, FF), D ** -0.5, 0.21875, ((0, 2), (2, 2)))
    up_bias = centred(splits[9], (LAYERS, FF), 0.5, 3.0, ((0, 2), (1, 2)), jnp.float32)
    down_weight = centred(splits[10], (LAYERS, FF, D), FF ** -0.5, 0.109375, ((0, 2), (1, 2)))
    species_bias = centred(splits[11], (LAYERS, SPECIES, D), 0.5, 3.0, ((0, 2),), jnp.float32)
    out_cotangent = centred(splits[12], (CELLS, LEN, D), 1.0, 6.0, ((0, 32),), jnp.float32)
    return dict(embeddings=embeddings, species=species, ln1_gain=ln1_gain, ln1_bias=ln1_bias, qkv_weight=qkv_weight, out_weight=out_weight, ln2_gain=ln2_gain, ln2_bias=ln2_bias, up_weight=up_weight, up_bias=up_bias, down_weight=down_weight, species_bias=species_bias, out_cotangent=out_cotangent)


@jax.custom_vjp
def low(v):
    return lax.optimization_barrier(v.astype(jnp.bfloat16)).astype(jnp.float32)

@jax.custom_vjp
def low_back(v):
    return v

def low_keep(v):
    return (low(v), None)

def low_pass(kept, grad):
    return (grad,)

def back_keep(v):
    return (v, None)

def back_low(kept, grad):
    return (low(grad),)
low.defvjp(low_keep, low_pass)
low_back.defvjp(back_keep, back_low)
highest = lax.Precision.HIGHEST
epsilon = 1e-05

def matmul(operand, against):
    return jnp.dot(operand, against, precision=highest, preferred_element_type=jnp.float32)

def normalize(values):
    center = values - lax.optimization_barrier(jnp.mean(values, axis=-1, keepdims=True))
    return center * lax.rsqrt(lax.optimization_barrier(jnp.mean(center * center, axis=-1, keepdims=True)) + epsilon)

def encoder_layer(inputs, species_flag, params):
    gain_one, bias_one, qkv_w, out_w, gain_two, bias_two, up_w, up_b, down_w, table = params
    row_count = inputs.shape[0]
    half_width = D // N_TENSOR
    head_count = half_width // HEAD
    unit_width = FF // N_TENSOR
    shifted = inputs + table[species_flag]
    act_one = low(normalize(shifted) * gain_one + bias_one)
    attn_total = jnp.zeros(inputs.shape, jnp.float32)
    for part_index in range(N_TENSOR):
        head_cols = slice(part_index * half_width, (part_index + 1) * half_width)
        part_input = low_back(act_one)
        projected = matmul(part_input, qkv_w[:, :, head_cols].reshape(D, 3 * half_width))
        projected = projected.reshape(row_count, 3, head_count, HEAD)
        queries = low(low_back(projected[:, 0]))
        key_vectors = low(low_back(projected[:, 1]))
        value_vectors = low(low_back(projected[:, 2]))
        scores = jnp.einsum('qhd,khd->hqk', queries, key_vectors, precision=highest) * HEAD ** (-0.5)
        attn_probs = jax.nn.softmax(low_back(scores), axis=-1)
        head_mix = jnp.einsum('hqk,khd->qhd', low(attn_probs), value_vectors, precision=highest)
        head_mix = low(low_back(head_mix)).reshape(row_count, half_width)
        attn_total = attn_total + low(matmul(head_mix, out_w[head_cols]))
    residual = shifted + low_back(attn_total)
    act_two = low(normalize(residual) * gain_two + bias_two)
    unit_total = jnp.zeros(inputs.shape, jnp.float32)
    for part_index in range(N_TENSOR):
        unit_cols = slice(part_index * unit_width, (part_index + 1) * unit_width)
        part_input = low_back(act_two)
        pre_act = low_back(matmul(part_input, up_w[:, unit_cols]) + up_b[unit_cols])
        hidden = low(jax.nn.gelu(pre_act, approximate=False))
        unit_total = unit_total + low(matmul(hidden, down_w[unit_cols]))
    return residual + low_back(unit_total)

def reference(embeddings, species, ln1_gain, ln1_bias, qkv_weight, out_weight, ln2_gain, ln2_bias, up_weight, up_bias, down_weight, species_bias, out_cotangent):
    params = tuple((source_array.astype(jnp.float32) for source_array in (ln1_gain, ln1_bias, qkv_weight, out_weight, ln2_gain, ln2_bias, up_weight, up_bias, down_weight, species_bias)))
    embedded = embeddings.astype(jnp.float32)
    probe = jnp.zeros(embedded.shape, jnp.float32)
    group_cells = max((candidate for candidate in range(1, CELLS + 1) if CELLS % candidate == 0 and candidate * LEN <= max(4096, LEN)))
    block_count = CELLS // group_cells

    def run(weights, embed_in, probe_in):
        first_params = tuple((stacked[0] for stacked in weights))
        second_params = tuple((stacked[1] for stacked in weights))

        def block_step(block_data):
            block_embed, block_probe, block_species = block_data
            first_out = jax.vmap(encoder_layer, in_axes=(0, 0, None))(block_embed, block_species, first_params)
            second_in = low_back(low(first_out)) + block_probe
            second_out = jax.vmap(encoder_layer, in_axes=(0, 0, None))(second_in, block_species, second_params)
            return (first_out, second_out)
        blocks = (embed_in.reshape(block_count, group_cells, LEN, D), probe_in.reshape(block_count, group_cells, LEN, D), species.reshape(block_count, group_cells))
        out_pair = lax.map(jax.checkpoint(block_step), blocks)
        return (out_pair[0].reshape(CELLS, LEN, D), out_pair[1].reshape(CELLS, LEN, D))
    (first_out, second_out), pullback = jax.vjp(run, params, embedded, probe)
    param_grads, embed_grad, probe_grad = pullback((jnp.zeros_like(first_out), out_cotangent.astype(jnp.float32)))
    return (jnp.stack([first_out, second_out]), jnp.stack([embed_grad, probe_grad]), param_grads[0], param_grads[1], param_grads[2], param_grads[3], param_grads[4], param_grads[5], param_grads[6], param_grads[7], param_grads[8], param_grads[9])
```

```python
import functools

import jax
import jax.numpy as jnp
from jax import lax
from jax.experimental import pallas as pl
from jax.experimental.pallas import tpu as pltpu
from jax.sharding import PartitionSpec as P

HEAD = 64
BR, BC = 96, 384
MESH = pl.DeviceIdType.MESH
BF = jnp.bfloat16
F32 = jnp.float32

epsilon = 1e-05
root_half = 0.7071067811865476
density_scale = 0.3989422804014327


def place():
    dp = lax.axis_index("dp")
    z = lax.axis_index("tensor") * 2 + lax.rem(dp, 2)
    return dp // 8, lax.rem(dp // 2, 4), z, lax.axis_index("section")


def device(x, y, z, core):
    return (core, (x * 4 + y) * 2 + lax.rem(z, 2), z // 2)


def wrap(v):
    return lax.rem(v, 4)


def sum_kernel(g_ref, s_ref, full_ref, small_ref, r1, r2, r3, o1, s1, s2, s3, q1, q2, q3, ss, rs, qs, qr, ls, gs, gr, ws):
    x, y, z, c = place()
    t, zl = z // 2, lax.rem(z, 2)
    peers = []
    for k in (1, 2, 3):
        zk = wrap(z + k)
        other = lax.rem(zk // 2 + t, 2)
        peers.append(
            (
                (wrap(x + k), y, z, c),
                (x, wrap(y + k), z, c),
                (x, y, zk, lax.rem(c + other, 2)),
                other,
                wrap(x + k),
                wrap(y + k),
                lax.rem(zk, 2),
            )
        )
    barrier = pltpu.get_barrier_semaphore()
    for px, py, pz, *_ in peers:
        for p in (px, py, pz):
            pl.semaphore_signal(barrier, inc=1, device_id=device(*p), device_id_type=MESH)
    pl.semaphore_wait(barrier, 9)

    def send(src, dst, sems, rsems, idx, peer):
        cp = pltpu.make_async_remote_copy(
            src_ref=src, dst_ref=dst, send_sem=sems.at[idx], recv_sem=rsems.at[idx], device_id=device(*peer), device_id_type=MESH
        )
        cp.start()
        return cp

    own = c
    first = [[], [], []]
    for k in (1, 2, 3):
        px, py, pz, other, xk, yk, zlk = peers[k - 1]
        which = lax.rem(own + other, 2)
        first[0].append(
            [send(g_ref.at[which, 0, pl.ds(zlk * 16, 16)], r1.at[0, k - 1], ss, rs, (0, 0, k - 1, 0), pz)]
        )
        first[1].append(
            [send(g_ref.at[i, 1, pl.ds(xk * 8, 8)], r1.at[1, k - 1, pl.ds(i * 8, 8)], ss, rs, (0, 1, k - 1, i), px) for i in (0, 1)]
        )
        first[2].append(
            [send(g_ref.at[i, 2, pl.ds(yk * 8, 8)], r1.at[2, k - 1, pl.ds(i * 8, 8)], ss, rs, (0, 2, k - 1, i), py) for i in (0, 1)]
        )
    q1[pl.ds(x, 1)] = s_ref[...][None]
    small = [send(q1.at[x], q1.at[x], qs, qr, (0, k - 1), peers[k - 1][0]) for k in (1, 2, 3)]
    mine = [
        pltpu.make_async_copy(g_ref.at[own, 0, pl.ds(zl * 16, 16)], o1.at[0], ls.at[0]),
        pltpu.make_async_copy(g_ref.at[0, 1, pl.ds(x * 8, 8)], o1.at[1, pl.ds(0, 8)], ls.at[1]),
        pltpu.make_async_copy(g_ref.at[1, 1, pl.ds(x * 8, 8)], o1.at[1, pl.ds(8, 8)], ls.at[2]),
        pltpu.make_async_copy(g_ref.at[0, 2, pl.ds(y * 8, 8)], o1.at[2, pl.ds(0, 8)], ls.at[3]),
        pltpu.make_async_copy(g_ref.at[1, 2, pl.ds(y * 8, 8)], o1.at[2, pl.ds(8, 8)], ls.at[4]),
    ]
    for cp in mine:
        cp.start()
    for cp in mine:
        cp.wait()

    def add(dst, part, base, recv, count):
        @pl.loop(0, count)
        def _(i):
            total = base(i).astype(F32)
            for k in range(3):
                total += recv[part, k, pl.ds(i, 1)][0].astype(F32)
            dst[part, pl.ds(i, 1)] = total.astype(BF)[None]

    for cp in small:
        cp.wait()
    q2[pl.ds(y, 1)] = (((q1[0] + q1[1]) + q1[2]) + q1[3])[None]
    small = [send(q2.at[y], q2.at[y], qs, qr, (1, k - 1), peers[k - 1][1]) for k in (1, 2, 3)]
    second = [[], [], []]
    for p in range(3):
        for group in first[p]:
            for cp in group:
                cp.wait()
        add(s1, p, lambda i, p=p: o1[p, pl.ds(i, 1)][0], r1, 16)
        for k in (1, 2, 3):
            px, py, pz, other, xk, yk, zlk = peers[k - 1]
            which = lax.rem(own + other, 2)
            if p == 0:
                second[0].append([send(s1.at[0, pl.ds(xk * 4, 4)], r2.at[0, k - 1], ss, rs, (1, 0, k - 1, 0), px)])
            elif p == 1:
                second[1].append(
                    [
                        send(s1.at[1, pl.ds(i * 8 + yk * 2, 2)], r2.at[1, k - 1, pl.ds(i * 2, 2)], ss, rs, (1, 1, k - 1, i), py)
                        for i in (0, 1)
                    ]
                )
            else:
                second[2].append([send(s1.at[2, pl.ds(which * 8 + zlk * 4, 4)], r2.at[2, k - 1], ss, rs, (1, 2, k - 1, 0), pz)])
    for cp in small:
        cp.wait()
    q2sum = ((q2[0] + q2[1]) + q2[2]) + q2[3]
    q2[pl.ds(4, 1)] = q2sum[None]
    q3[pl.ds(z, 1)] = q2[4, pl.ds(own, 1)]
    small = []
    for k in (1, 2, 3):
        which = lax.rem(own + peers[k - 1][3], 2)
        small.append(send(q2.at[4, which], q3.at[z], qs, qr, (2, k - 1), peers[k - 1][2]))
    third = [[], [], []]
    bases = [
        lambda i: s1[0, pl.ds(x * 4 + i, 1)][0],
        lambda i: s1[1, pl.ds((i // 2) * 8 + y * 2 + lax.rem(i, 2), 1)][0],
        lambda i: s1[2, pl.ds(own * 8 + zl * 4 + i, 1)][0],
    ]
    for p in range(3):
        for group in second[p]:
            for cp in group:
                cp.wait()
        add(s2, p, bases[p], r2, 4)
        for k in (1, 2, 3):
            px, py, pz, other, xk, yk, zlk = peers[k - 1]
            which = lax.rem(own + other, 2)
            if p == 0:
                third[0].append(send(s2.at[0, yk], r3.at[0, k - 1, 0], ss, rs, (2, 0, k - 1, 0), py))
            elif p == 1:
                third[1].append(send(s2.at[1, which * 2 + zlk], r3.at[1, k - 1, 0], ss, rs, (2, 1, k - 1, 0), pz))
            else:
                third[2].append(send(s2.at[2, xk], r3.at[2, k - 1, 0], ss, rs, (2, 2, k - 1, 0), px))
    for cp in small:
        cp.wait()
    small_ref[...] = ((q3[0] + q3[1]) + q3[2]) + q3[3]
    bases = [
        lambda i: s2[0, pl.ds(y, 1)][0],
        lambda i: s2[1, pl.ds(own * 2 + zl, 1)][0],
        lambda i: s2[2, pl.ds(x, 1)][0],
    ]
    number = (zl * 16 + x * 4 + y, x * 8 + y * 2 + zl, y * 8 + zl * 4 + x)
    gather = [[], [], []]
    local = []

    def spread(p, step, start, count, axis):
        out = []
        for k in (1, 2, 3):
            if axis == 2 and k != 2:
                continue
            peer = peers[k - 1][axis] if axis < 2 else (x, y, t * 2 + 1 - zl, c)
            part = full_ref.at[p, pl.ds(start, count)]
            out.append(send(part, part, gs, gr, (p, step, k - 1), peer))
        return out

    for p in range(3):
        for cp in third[p]:
            cp.wait()
        add(s3, p, bases[p], r3, 1)
        cp = pltpu.make_async_copy(s3.at[p], full_ref.at[p, pl.ds(number[p], 1)], ws.at[p])
        cp.start()
        local.append(cp)
    orders = (
        ((1, number[0], 1), (0, zl * 16 + x * 4, 4), (2, zl * 16, 16)),
        ((2, number[1], 1), (1, x * 8 + y * 2, 2), (0, x * 8, 8)),
        ((0, number[2], 1), (2, y * 8 + zl * 4, 4), (1, y * 8, 8)),
    )
    for step in range(3):
        for p in range(3):
            if step == 0:
                local[p].wait()
            else:
                for cp in gather[p]:
                    cp.wait()
            axis, start, count = orders[p][step]
            gather[p] = spread(p, step, start, count, axis)
    for p in range(3):
        for cp in gather[p]:
            cp.wait()


def summed(grads, small):
    dma = pltpu.SemaphoreType.DMA
    blocks = lambda *lead: pltpu.VMEM((*lead, BR, BC), BF)
    anywhere = pl.BlockSpec(memory_space=pl.ANY)
    return pl.pallas_call(
        sum_kernel,
        out_shape=(jax.ShapeDtypeStruct((3, 32, BR, BC), BF), jax.ShapeDtypeStruct((8, 768), F32)),
        in_specs=[anywhere, pl.BlockSpec(memory_space=pltpu.VMEM)],
        out_specs=(anywhere, pl.BlockSpec(memory_space=pltpu.VMEM)),
        scratch_shapes=[
            blocks(3, 3, 16),
            blocks(3, 3, 4),
            blocks(3, 3, 1),
            blocks(3, 16),
            blocks(3, 16),
            blocks(3, 4),
            blocks(3, 1),
            pltpu.VMEM((4, 2, 8, 768), F32),
            pltpu.VMEM((5, 2, 8, 768), F32),
            pltpu.VMEM((4, 8, 768), F32),
            dma((3, 3, 3, 2)),
            dma((3, 3, 3, 2)),
            dma((3, 3)),
            dma((3, 3)),
            dma((5,)),
            dma((3, 3, 3)),
            dma((3, 3, 3)),
            dma((3,)),
        ],
        compiler_params=pltpu.CompilerParams(collective_id=0, has_side_effects=True, vmem_limit_bytes=48 * 2**20),
        name="gradient_sums",
    )(grads, small)


def normalize(values):
    center = values - jnp.mean(values, axis=-1, keepdims=True)
    inverse = lax.rsqrt(jnp.mean(center * center, axis=-1, keepdims=True) + epsilon)
    return (center * inverse, inverse)


def norm_back(grad_normed, normed, inverse):
    return inverse * (
        grad_normed
        - jnp.mean(grad_normed, axis=-1, keepdims=True)
        - normed * jnp.mean(grad_normed * normed, axis=-1, keepdims=True)
    )


def gelu_slope(values):
    return 0.5 * (1.0 + lax.erf(values * root_half)) + values * density_scale * jnp.exp(-0.5 * values * values)


def dot(a, b):
    return jnp.dot(a, b, preferred_element_type=F32)


def row_inner(a, b):
    return lax.dot_general(a, b, (((0,), (0,)), ((), ())), preferred_element_type=F32).astype(BF)


def back_product(a, b):
    return lax.dot_general(a, b, (((1,), (1,)), ((), ())), preferred_element_type=F32)


def both_cores(part):
    return part.astype(F32) + lax.ppermute(part, "section", [(0, 1), (1, 0)]).astype(F32)


def heads(a):
    return a.reshape(2, 256, 6, HEAD)


def layer_forward(x, flags, w):
    g1, b1, qkv_w, out_w, g2, b2, up_w, up_b, down_w, table = w
    bias = jnp.where(flags[:, None] == 0, table[0][None], table[1][None])
    shifted = (x.reshape(2, 256, -1) + bias[:, None]).reshape(512, -1)
    n1, i1 = normalize(shifted)
    a1 = (n1 * g1 + b1).astype(BF)
    q, k, v = (heads(dot(a1, qkv_w[i]).astype(BF)) for i in range(3))
    scores = jnp.einsum("bqhd,bkhd->bhqk", q, k, preferred_element_type=F32) * HEAD**-0.5
    top = jnp.max(scores, axis=-1, keepdims=True)
    lse = top + jnp.log(jnp.sum(jnp.exp(scores - top), axis=-1, keepdims=True))
    probs = jnp.exp(scores - lse)
    o = jnp.einsum("bhqk,bkhd->bqhd", probs.astype(BF), v, preferred_element_type=F32).astype(BF).reshape(512, -1)
    r = shifted + both_cores(dot(o, out_w).astype(BF))
    n2, i2 = normalize(r)
    a2 = (n2 * g2 + b2).astype(BF)
    u = dot(a2, up_w) + up_b
    g = jax.nn.gelu(u, approximate=False).astype(BF)
    out = r + both_cores(dot(g, down_w).astype(BF))
    return out, (n1, i1, a1, q, k, v, lse, o, n2, i2, a2, u, g)


def columns(a):
    return a.reshape(a.shape[0], -1, BC).transpose(1, 0, 2).reshape(-1, BR, BC)


def layer_backward(dy, kept, flags, w):
    g1, b1, qkv_w, out_w, g2, b2, up_w, up_b, down_w, table = w
    n1, i1, a1, q, k, v, lse, o, n2, i2, a2, u, g = kept
    dz = dy.astype(BF)
    grad_down = row_inner(g, dz)
    du = (back_product(dz, down_w) * gelu_slope(u)).astype(BF)
    grad_up_b = jnp.sum(du, axis=0, dtype=F32)
    grad_up = row_inner(a2, du)
    da2 = both_cores(back_product(du, up_w).astype(BF))
    grad_g2 = jnp.sum(da2 * n2, axis=0)
    grad_b2 = jnp.sum(da2, axis=0)
    dr = dy + norm_back(da2 * g2, n2, i2)
    dattn = dr.astype(BF)
    grad_out = row_inner(o, dattn)
    do = heads(back_product(dattn, out_w).astype(BF))
    scores = jnp.einsum("bqhd,bkhd->bhqk", q, k, preferred_element_type=F32) * HEAD**-0.5
    probs = jnp.exp(scores - lse)
    dprobs = jnp.einsum("bqhd,bkhd->bhqk", do, v, preferred_element_type=F32)
    dv = jnp.einsum("bhqk,bqhd->bkhd", probs.astype(BF), do, preferred_element_type=F32).astype(BF).reshape(512, -1)
    ds = (probs * (dprobs - jnp.sum(probs * dprobs, axis=-1, keepdims=True))).astype(BF)
    dq = (jnp.einsum("bhqk,bkhd->bqhd", ds, k, preferred_element_type=F32) * HEAD**-0.5).astype(BF).reshape(512, -1)
    dk = (jnp.einsum("bhqk,bqhd->bkhd", ds, q, preferred_element_type=F32) * HEAD**-0.5).astype(BF).reshape(512, -1)
    grad_qkv = [row_inner(a1, d) for d in (dq, dk, dv)]
    da1 = both_cores((back_product(dq, qkv_w[0]) + back_product(dk, qkv_w[1]) + back_product(dv, qkv_w[2])).astype(BF))
    grad_g1 = jnp.sum(da1 * n1, axis=0)
    grad_b1 = jnp.sum(da1, axis=0)
    dx = dr + norm_back(da1 * g1, n1, i1)
    cells = jnp.sum(dx.reshape(2, 256, -1), axis=1)
    grad_table = [jnp.sum(jnp.where(flags[:, None] == s, cells, 0.0), axis=0) for s in (0, 1)]
    small = jnp.concatenate([jnp.stack([grad_g1, grad_b1, grad_g2, grad_b2, *grad_table]), grad_up_b.reshape(2, 768)])
    blocks = jnp.stack(
        [
            columns(grad_down),
            columns(grad_up),
            jnp.concatenate([columns(d) for d in grad_qkv] + [columns(grad_out)]),
        ]
    )
    return dx, blocks, small


def shards(
    embeddings,
    species,
    ln1_gain,
    ln1_bias,
    qkv_weight,
    out_weight,
    ln2_gain,
    ln2_bias,
    up_weight,
    up_bias,
    down_weight,
    species_bias,
    out_cotangent,
):
    core = lax.axis_index("section")
    half = lax.axis_index("tensor")
    swap_cores = [(0, 1), (1, 0)]
    cross = [(0, 3), (1, 2), (2, 1), (3, 0)]
    own = (
        ln1_gain[0],
        ln1_bias[0],
        qkv_weight[0].transpose(1, 0, 2),
        out_weight[0],
        ln2_gain[0],
        ln2_bias[0],
        up_weight[0],
        up_bias[0],
        down_weight[0],
        species_bias[0],
    )
    split = (False, False, True, True, False, False, True, True, True, False)
    other = tuple(
        lax.ppermute(a, ("section", "tensor"), cross) if cut else lax.ppermute(a, "section", swap_cores)
        for a, cut in zip(own, split)
    )
    first = core == 0
    weights = (
        tuple(jnp.where(first, a, b) for a, b in zip(own, other)),
        tuple(jnp.where(first, b, a) for a, b in zip(own, other)),
    )
    cells = lax.dynamic_slice_in_dim(embeddings, half * 2, 2, 0).reshape(512, -1)
    flags = lax.dynamic_slice_in_dim(species, half * 2, 2, 0)
    cotangent = lax.dynamic_slice_in_dim(out_cotangent, half * 2, 2, 0).reshape(512, -1)
    out0, kept0 = layer_forward(cells.astype(F32), flags, weights[0])
    out1, kept1 = layer_forward(out0.astype(BF).astype(F32), flags, weights[1])
    dx1, blocks1, small1 = layer_backward(cotangent, kept1, flags, weights[1])
    dx0, blocks0, small0 = layer_backward(dx1.astype(BF).astype(F32), kept0, flags, weights[0])

    def four_cells(a0, a1):
        mine = jnp.where(first, a0, a1).astype(BF).reshape(2, 256, -1)
        theirs = lax.ppermute(mine, "tensor", swap_cores)
        low = half == 0
        return jnp.concatenate([jnp.where(low, mine, theirs), jnp.where(low, theirs, mine)]).astype(F32)[None]

    layer_out = four_cells(out0, out1)
    input_grad = four_cells(dx0, dx1)
    full, small = summed(jnp.stack([blocks0, blocks1]), jnp.stack([small0, small1]))

    def whole(blocks, rows):
        return blocks.reshape(-1, rows, BC).transpose(1, 0, 2).reshape(rows, -1).astype(F32)[None]

    grad_down = whole(full[0], 1536)
    grad_up = whole(full[1], 768)
    grad_qkv = full[2, :24].reshape(3, 768, BC).transpose(1, 0, 2).astype(F32)[None]
    grad_out = whole(full[2, 24:], 384)
    return (
        layer_out,
        input_grad,
        small[0:1],
        small[1:2],
        grad_qkv,
        grad_out,
        small[2:3],
        small[3:4],
        grad_up,
        small[6:8].reshape(1, 1536),
        grad_down,
        small[4:6][None],
    )


def solution(mesh):
    placed = (
        P("dp", None, None),
        P("dp"),
        P("section", None),
        P("section", None),
        P("section", None, None, "tensor"),
        P("section", "tensor", None),
        P("section", None),
        P("section", None),
        P("section", None, "tensor"),
        P("section", "tensor"),
        P("section", "tensor", None),
        P("section", None, None),
        P("dp", None, None),
    )
    return jax.shard_map(
        shards,
        mesh=mesh,
        in_specs=placed,
        out_specs=(
            P("section", "dp", None, None),
            P("section", "dp", None, None),
            P("section", None),
            P("section", None),
            P("section", None, None, "tensor"),
            P("section", "tensor", None),
            P("section", None),
            P("section", None),
            P("section", None, "tensor"),
            P("section", "tensor"),
            P("section", "tensor", None),
            P("section", None, None),
        ),
        check_vma=False,
    )
```

```python
import functools

import jax
import jax.numpy as jnp
from jax import lax
from jax.experimental import pallas as pl
from jax.experimental.pallas import tpu as pltpu
from jax.sharding import PartitionSpec as P

HEAD = 64
BR, BC = 96, 384
MESH = pl.DeviceIdType.MESH
BF = jnp.bfloat16
F32 = jnp.float32

epsilon = 1e-05
root_half = 0.7071067811865476
density_scale = 0.3989422804014327


def place():
    dp = lax.axis_index("dp")
    z = lax.axis_index("tensor") * 2 + lax.rem(dp, 2)
    return dp // 8, lax.rem(dp // 2, 4), z, lax.axis_index("section")


def device(x, y, z, core):
    return (core, (x * 4 + y) * 2 + lax.rem(z, 2), z // 2)


def wrap(v):
    return lax.rem(v, 4)


def sum_kernel(g_ref, s_ref, full0, full1, full2, small_ref, r1, r2, r3, o1, s1, s2, s3, q1, q2, q3, ss, rs, qs, qr, ls, gs, gr, ws):
    full_ref = (full0, full1, full2)
    x, y, z, c = place()
    t, zl = z // 2, lax.rem(z, 2)
    peers = []
    for k in (1, 2, 3):
        zk = wrap(z + k)
        other = lax.rem(zk // 2 + t, 2)
        peers.append(
            (
                (wrap(x + k), y, z, c),
                (x, wrap(y + k), z, c),
                (x, y, zk, lax.rem(c + other, 2)),
                other,
                wrap(x + k),
                wrap(y + k),
                lax.rem(zk, 2),
            )
        )
    barrier = pltpu.get_barrier_semaphore()
    for px, py, pz, *_ in peers:
        for p in (px, py, pz):
            pl.semaphore_signal(barrier, inc=1, device_id=device(*p), device_id_type=MESH)
    pl.semaphore_wait(barrier, 9)

    def send(src, dst, sems, rsems, idx, peer):
        cp = pltpu.make_async_remote_copy(
            src_ref=src, dst_ref=dst, send_sem=sems.at[idx], recv_sem=rsems.at[idx], device_id=device(*peer), device_id_type=MESH
        )
        cp.start()
        return cp

    own = c
    first = [[], [], []]
    for k in (1, 2, 3):
        px, py, pz, other, xk, yk, zlk = peers[k - 1]
        which = lax.rem(own + other, 2)
        first[0].append(
            [send(g_ref.at[which, 0, pl.ds(zlk * 16, 16)], r1.at[0, k - 1], ss, rs, (0, 0, k - 1, 0), pz)]
        )
        first[1].append(
            [send(g_ref.at[i, 1, pl.ds(xk * 8, 8)], r1.at[1, k - 1, pl.ds(i * 8, 8)], ss, rs, (0, 1, k - 1, i), px) for i in (0, 1)]
        )
        first[2].append(
            [send(g_ref.at[i, 2, pl.ds(yk * 8, 8)], r1.at[2, k - 1, pl.ds(i * 8, 8)], ss, rs, (0, 2, k - 1, i), py) for i in (0, 1)]
        )
    q1[pl.ds(x, 1)] = s_ref[...][None]
    small = [send(q1.at[x], q1.at[x], qs, qr, (0, k - 1), peers[k - 1][0]) for k in (1, 2, 3)]
    mine = [
        pltpu.make_async_copy(g_ref.at[own, 0, pl.ds(zl * 16, 16)], o1.at[0], ls.at[0]),
        pltpu.make_async_copy(g_ref.at[0, 1, pl.ds(x * 8, 8)], o1.at[1, pl.ds(0, 8)], ls.at[1]),
        pltpu.make_async_copy(g_ref.at[1, 1, pl.ds(x * 8, 8)], o1.at[1, pl.ds(8, 8)], ls.at[2]),
        pltpu.make_async_copy(g_ref.at[0, 2, pl.ds(y * 8, 8)], o1.at[2, pl.ds(0, 8)], ls.at[3]),
        pltpu.make_async_copy(g_ref.at[1, 2, pl.ds(y * 8, 8)], o1.at[2, pl.ds(8, 8)], ls.at[4]),
    ]
    for cp in mine:
        cp.start()
    for cp in mine:
        cp.wait()

    def add(dst, part, base, recv, count):
        @pl.loop(0, count)
        def _(i):
            total = base(i).astype(F32)
            for k in range(3):
                total += recv[part, k, pl.ds(i, 1)][0].astype(F32)
            dst[part, pl.ds(i, 1)] = total.astype(BF)[None]

    for cp in small:
        cp.wait()
    q2[pl.ds(y, 1)] = (((q1[0] + q1[1]) + q1[2]) + q1[3])[None]
    small = [send(q2.at[y], q2.at[y], qs, qr, (1, k - 1), peers[k - 1][1]) for k in (1, 2, 3)]
    second = [[], [], []]
    for p in range(3):
        for group in first[p]:
            for cp in group:
                cp.wait()
        add(s1, p, lambda i, p=p: o1[p, pl.ds(i, 1)][0], r1, 16)
        for k in (1, 2, 3):
            px, py, pz, other, xk, yk, zlk = peers[k - 1]
            which = lax.rem(own + other, 2)
            if p == 0:
                second[0].append([send(s1.at[0, pl.ds(xk * 4, 4)], r2.at[0, k - 1], ss, rs, (1, 0, k - 1, 0), px)])
            elif p == 1:
                second[1].append(
                    [
                        send(s1.at[1, pl.ds(i * 8 + yk * 2, 2)], r2.at[1, k - 1, pl.ds(i * 2, 2)], ss, rs, (1, 1, k - 1, i), py)
                        for i in (0, 1)
                    ]
                )
            else:
                second[2].append([send(s1.at[2, pl.ds(which * 8 + zlk * 4, 4)], r2.at[2, k - 1], ss, rs, (1, 2, k - 1, 0), pz)])
    for cp in small:
        cp.wait()
    q2sum = ((q2[0] + q2[1]) + q2[2]) + q2[3]
    q2[pl.ds(4, 1)] = q2sum[None]
    q3[pl.ds(z, 1)] = q2[4, pl.ds(own, 1)]
    small = []
    for k in (1, 2, 3):
        which = lax.rem(own + peers[k - 1][3], 2)
        small.append(send(q2.at[4, which], q3.at[z], qs, qr, (2, k - 1), peers[k - 1][2]))
    third = [[], [], []]
    bases = [
        lambda i: s1[0, pl.ds(x * 4 + i, 1)][0],
        lambda i: s1[1, pl.ds((i // 2) * 8 + y * 2 + lax.rem(i, 2), 1)][0],
        lambda i: s1[2, pl.ds(own * 8 + zl * 4 + i, 1)][0],
    ]
    for p in range(3):
        for group in second[p]:
            for cp in group:
                cp.wait()
        add(s2, p, bases[p], r2, 4)
        for k in (1, 2, 3):
            px, py, pz, other, xk, yk, zlk = peers[k - 1]
            which = lax.rem(own + other, 2)
            if p == 0:
                third[0].append(send(s2.at[0, yk], r3.at[0, k - 1, 0], ss, rs, (2, 0, k - 1, 0), py))
            elif p == 1:
                third[1].append(send(s2.at[1, which * 2 + zlk], r3.at[1, k - 1, 0], ss, rs, (2, 1, k - 1, 0), pz))
            else:
                third[2].append(send(s2.at[2, xk], r3.at[2, k - 1, 0], ss, rs, (2, 2, k - 1, 0), px))
    for cp in small:
        cp.wait()
    small_ref[...] = ((q3[0] + q3[1]) + q3[2]) + q3[3]
    bases = [
        lambda i: s2[0, pl.ds(y, 1)][0],
        lambda i: s2[1, pl.ds(own * 2 + zl, 1)][0],
        lambda i: s2[2, pl.ds(x, 1)][0],
    ]
    number = (zl * 16 + x * 4 + y, x * 8 + y * 2 + zl, y * 8 + zl * 4 + x)
    gather = [[], [], []]
    local = []

    def spread(p, step, start, count, axis):
        out = []
        for k in (1, 2, 3):
            if axis == 2 and k != 2:
                continue
            peer = peers[k - 1][axis] if axis < 2 else (x, y, t * 2 + 1 - zl, c)
            part = full_ref[p].at[pl.ds(start, count)]
            out.append(send(part, part, gs, gr, (p, step, k - 1), peer))
        return out

    for p in range(3):
        for cp in third[p]:
            cp.wait()
        add(s3, p, bases[p], r3, 1)
        cp = pltpu.make_async_copy(s3.at[p], full_ref[p].at[pl.ds(number[p], 1)], ws.at[p])
        cp.start()
        local.append(cp)
    orders = (
        ((1, number[0], 1), (0, zl * 16 + x * 4, 4), (2, zl * 16, 16)),
        ((2, number[1], 1), (1, x * 8 + y * 2, 2), (0, x * 8, 8)),
        ((0, number[2], 1), (2, y * 8 + zl * 4, 4), (1, y * 8, 8)),
    )
    for step in range(3):
        for p in range(3):
            if step == 0:
                local[p].wait()
            else:
                for cp in gather[p]:
                    cp.wait()
            axis, start, count = orders[p][step]
            gather[p] = spread(p, step, start, count, axis)
    for p in range(3):
        for cp in gather[p]:
            cp.wait()


def summed(grads, small):
    dma = pltpu.SemaphoreType.DMA
    blocks = lambda *lead: pltpu.VMEM((*lead, BR, BC), BF)
    anywhere = pl.BlockSpec(memory_space=pl.ANY)
    return pl.pallas_call(
        sum_kernel,
        out_shape=(jax.ShapeDtypeStruct((32, BR, BC), BF),) * 3 + (jax.ShapeDtypeStruct((8, 768), F32),),
        in_specs=[anywhere, pl.BlockSpec(memory_space=pltpu.VMEM)],
        out_specs=(anywhere, anywhere, anywhere, pl.BlockSpec(memory_space=pltpu.VMEM)),
        scratch_shapes=[
            blocks(3, 3, 16),
            blocks(3, 3, 4),
            blocks(3, 3, 1),
            blocks(3, 16),
            blocks(3, 16),
            blocks(3, 4),
            blocks(3, 1),
            pltpu.VMEM((4, 2, 8, 768), F32),
            pltpu.VMEM((5, 2, 8, 768), F32),
            pltpu.VMEM((4, 8, 768), F32),
            dma((3, 3, 3, 2)),
            dma((3, 3, 3, 2)),
            dma((3, 3)),
            dma((3, 3)),
            dma((5,)),
            dma((3, 3, 3)),
            dma((3, 3, 3)),
            dma((3,)),
        ],
        compiler_params=pltpu.CompilerParams(collective_id=0, has_side_effects=True, vmem_limit_bytes=48 * 2**20),
        name="gradient_sums",
    )(grads, small)


def norm(values):
    center = values - jnp.mean(values, axis=-1, keepdims=True)
    inverse = lax.rsqrt(jnp.mean(center * center, axis=-1, keepdims=True) + epsilon)
    return (center * inverse, inverse)


def norm_back(grad_normed, normed, inverse):
    return inverse * (
        grad_normed
        - jnp.mean(grad_normed, axis=-1, keepdims=True)
        - normed * jnp.mean(grad_normed * normed, axis=-1, keepdims=True)
    )


def dot(a, b):
    return jnp.dot(a, b, preferred_element_type=F32)


def dot_rows(a, b):
    return lax.dot_general(a, b, (((0,), (0,)), ((), ())), preferred_element_type=F32)


def dot_back(a, b):
    return lax.dot_general(a, b, (((1,), (1,)), ((), ())), preferred_element_type=F32)


def column_sum(a):
    return jnp.sum(a, axis=0, keepdims=True)


def layers_kernel(
    species, emb, cot, pk_own, pk_other, *refs
):
    own_w, other_w = refs[:4], refs[4:8]
    lo4, dx4, g_out, small = refs[8:12]
    (qkv_w, out_w, up_w, down_w, pk, emb_v, cot_v, S, A1, Q, K, V, LSE, O, R, A2, G, SL, LO, DX, DR, DU, DZ, DO, DQ, DK, DV, PB, DS, X, Y, GS) = refs[12:44]
    load_sem, x_send, x_recv, out_local, out_send, out_recv, g_sem = refs[44:]
    x, y, z, c = place()
    t = z // 2
    sibling = device(x, y, z, 1 - c)
    far = device(x, y, lax.rem(z + 2, 4), c)
    barrier = pltpu.get_barrier_semaphore()
    for p in (sibling, far):
        pl.semaphore_signal(barrier, inc=1, device_id=p, device_id_type=MESH)
    weights = (qkv_w, out_w, up_w, down_w)
    loads = []

    def load(src, dst, i):
        cp = pltpu.make_async_copy(src, dst, load_sem.at[i])
        cp.start()
        return cp

    start = [
        load(emb.at[pl.ds(2 * t, 2)], emb_v, 0),
        load(pk_own, pk.at[c], 1),
        load(pk_other, pk.at[1 - c], 2),
    ]
    w_loads = []
    for i, w in enumerate(weights):
        w_loads.append((load(own_w[i], w.at[c], 3 + 2 * i), load(other_w[i], w.at[1 - c], 4 + 2 * i)))
    cot_load = load(cot.at[pl.ds(2 * t, 2)], cot_v, 11)
    for cp in start:
        cp.wait()
    pl.semaphore_wait(barrier, 2)

    flying = {}

    def push(kind, b):
        cp = pltpu.make_async_remote_copy(
            src_ref=X.at[kind, b],
            dst_ref=Y.at[kind, b],
            send_sem=x_send.at[kind, b],
            recv_sem=x_recv.at[kind, b],
            device_id=sibling,
            device_id_type=MESH,
        )
        cp.start()
        flying[kind, b] = cp

    def both(kind, b):
        flying.pop((kind, b)).wait()
        return X[kind, b].astype(F32) + Y[kind, b].astype(F32)

    ready = [False] * 4

    def need(i):
        if not ready[i]:
            for cp in w_loads[i]:
                cp.wait()
            ready[i] = True

    def flag(b):
        return species[2 * t + b]

    def heads_forward(l, b):
        if l == 0:
            xin = emb_v[b].astype(F32)
        else:
            low = (R[0, b] + both(1, b)).astype(BF)
            LO[0, b] = low
            xin = low.astype(F32)
        s = xin + jnp.where(flag(b) == 0, pk[l, 4:5], pk[l, 5:6])
        S[l, b] = s
        n1, _ = norm(s)
        a1 = (n1 * pk[l, 0:1] + pk[l, 1:2]).astype(BF)
        A1[l, b] = a1
        need(0)
        for i, part in enumerate((Q, K, V)):
            part[l, b] = dot(a1, qkv_w[l, i]).astype(BF)
        for h in range(6):
            hs = slice(h * HEAD, h * HEAD + HEAD)
            sc = dot_back(K[l, b, :, hs], Q[l, b, :, hs]) * HEAD**-0.5
            top = jnp.max(sc, axis=0, keepdims=True)
            e = jnp.exp(sc - top)
            total = jnp.sum(e, axis=0, keepdims=True)
            PB[h] = (e * (1.0 / total)).astype(BF)
            LSE[l, b, h : h + 1] = top + jnp.log(total)
        for h in range(6):
            hs = slice(h * HEAD, h * HEAD + HEAD)
            O[l, b, :, hs] = dot_rows(PB[h], V[l, b, :, hs]).astype(BF)
        need(1)
        X[0, b] = dot(O[l, b], out_w[l]).astype(BF)
        push(0, b)

    def units_forward(l, b):
        r = S[l, b] + both(0, b)
        R[l, b] = r
        n2, _ = norm(r)
        a2 = (n2 * pk[l, 2:3] + pk[l, 3:4]).astype(BF)
        A2[l, b] = a2
        need(2)
        for j in range(2):
            cols = slice(j * 768, j * 768 + 768)
            u = dot(a2, up_w[l, :, cols]) + pk[l, 6 + j : 7 + j]
            cdf = 0.5 * (1.0 + lax.erf(u * root_half))
            G[l, b, :, cols] = (u * cdf).astype(BF)
            SL[l, b, :, cols] = (cdf + u * density_scale * jnp.exp(-0.5 * u * u)).astype(BF)
        need(3)
        X[1, b] = dot(G[l, b], down_w[l]).astype(BF)
        push(1, b)

    def rows(ref, *lead):
        a = ref[lead] if lead else ref[...]
        return a.reshape(512, a.shape[-1])

    def put(part, number, value):
        for i in range(value.shape[0] // BR):
            GS[part, number + i] = value[i * BR : (i + 1) * BR]

    g_copies = {}

    def flush(l, part):
        cp = pltpu.make_async_copy(GS.at[part], g_out.at[l, part], g_sem.at[part])
        cp.start()
        g_copies[part] = cp

    def free(part):
        if part in g_copies:
            g_copies.pop(part).wait()

    def dy(l, b):
        return cot_v[b] if l == 1 else DX[1, b].astype(F32)

    def units_backward(l):
        for b in range(2):
            DZ[b] = dy(l, b).astype(BF) if l == 1 else DX[1, b]
            for j in range(2):
                cols = slice(j * 768, j * 768 + 768)
                DU[b, :, cols] = (dot_back(DZ[b], down_w[l, cols]) * SL[l, b, :, cols].astype(F32)).astype(BF)
            X[0, b] = dot_back(DU[b], up_w[l]).astype(BF)
            push(0, b)
        free(0)
        dz = rows(DZ)
        for j in range(2):
            gd = dot_rows(rows(G, l)[:, j * 768 : j * 768 + 768], dz).astype(BF)
            for h in range(2):
                put(0, h * 16 + j * 8, gd[:, h * BC : (h + 1) * BC])
        flush(l, 0)
        free(1)
        a2 = rows(A2, l)
        for j in range(2):
            du = rows(DU)[:, j * 768 : j * 768 + 768]
            gu = dot_rows(a2, du).astype(BF)
            for h in range(2):
                put(1, (2 * j + h) * 8, gu[:, h * BC : (h + 1) * BC])
            small[l, 6 + j : 7 + j] = column_sum(du.astype(F32))
        flush(l, 1)
        gain = bias = 0.0
        for b in range(2):
            da2 = both(0, b)
            n2, inv = norm(R[l, b])
            gain += column_sum(da2 * n2)
            bias += column_sum(da2)
            dr = dy(l, b) + norm_back(da2 * pk[l, 2:3], n2, inv)
            DR[b] = dr
            DZ[b] = dr.astype(BF)
        small[l, 2:3] = gain
        small[l, 3:4] = bias

    def heads_backward(l):
        for b in range(2):
            DO[b] = dot_back(DZ[b], out_w[l]).astype(BF)
            for h in range(6):
                hs = slice(h * HEAD, h * HEAD + HEAD)
                sc = dot_back(K[l, b, :, hs], Q[l, b, :, hs]) * HEAD**-0.5
                p = jnp.exp(sc - LSE[l, b, h : h + 1])
                dp = dot_back(V[l, b, :, hs], DO[b, :, hs])
                pdp = p * dp
                PB[h] = p.astype(BF)
                DS[h] = (pdp - p * jnp.sum(pdp, axis=0, keepdims=True)).astype(BF)
            for h in range(6):
                hs = slice(h * HEAD, h * HEAD + HEAD)
                DV[b, :, hs] = dot(PB[h], DO[b, :, hs]).astype(BF)
                DK[b, :, hs] = (dot(DS[h], Q[l, b, :, hs]) * HEAD**-0.5).astype(BF)
                DQ[b, :, hs] = (dot_rows(DS[h], K[l, b, :, hs]) * HEAD**-0.5).astype(BF)
            X[1, b] = (
                dot_back(DQ[b], qkv_w[l, 0]) + dot_back(DK[b], qkv_w[l, 1]) + dot_back(DV[b], qkv_w[l, 2])
            ).astype(BF)
            push(1, b)
        free(2)
        go = dot_rows(rows(O, l), rows(DZ)).astype(BF)
        for h in range(2):
            put(2, 24 + h * 4, go[:, h * BC : (h + 1) * BC])
        a1 = rows(A1, l)
        for i, d in enumerate((DQ, DK, DV)):
            put(2, i * 8, dot_rows(a1, rows(d)).astype(BF))
        flush(l, 2)
        gain = bias = 0.0
        table = [0.0, 0.0]
        for b in range(2):
            da1 = both(1, b)
            n1, inv = norm(S[l, b])
            gain += column_sum(da1 * n1)
            bias += column_sum(da1)
            dx = DR[b] + norm_back(da1 * pk[l, 0:1], n1, inv)
            DX[l, b] = dx.astype(BF)
            total = column_sum(dx)
            for k in range(2):
                table[k] += jnp.where(flag(b) == k, total, 0.0)
        small[l, 0:1] = gain
        small[l, 1:2] = bias
        small[l, 4:5] = table[0]
        small[l, 5:6] = table[1]

    def share(src, dst, i):
        part = dst.at[pl.ds(2 * t, 2)]
        here = pltpu.make_async_copy(src, part, out_local.at[i])
        here.start()
        there = pltpu.make_async_remote_copy(
            src_ref=src, dst_ref=part, send_sem=out_send.at[i], recv_sem=out_recv.at[i], device_id=far, device_id_type=MESH
        )
        there.start()
        return here, there

    for l in range(2):
        for b in range(2):
            heads_forward(l, b)
        for b in range(2):
            units_forward(l, b)
    for b in range(2):
        LO[1, b] = (R[1, b] + both(1, b)).astype(BF)
    finish = list(share(LO.at[c], lo4, 0))
    cot_load.wait()
    for l in (1, 0):
        units_backward(l)
        heads_backward(l)
    finish += share(DX.at[c], dx4, 1)
    for part in range(3):
        free(part)
    for cp in finish:
        cp.wait()


def run_layers(species, emb, cot, pk_own, pk_other, own_w, other_w):
    anywhere = pl.BlockSpec(memory_space=pl.ANY)
    dma = pltpu.SemaphoreType.DMA
    vm = lambda *shape: pltpu.VMEM(shape, BF)
    vf = lambda *shape: pltpu.VMEM(shape, F32)
    cells = (2, 256, 768)
    scratch = dict(
        qkv_w=vm(2, 3, 768, 384),
        out_w=vm(2, 384, 768),
        up_w=vm(2, 768, 1536),
        down_w=vm(2, 1536, 768),
        pk=vf(2, 8, 768),
        emb_v=vm(*cells),
        cot_v=vf(*cells),
        S=vf(2, *cells),
        A1=vm(2, *cells),
        Q=vm(2, 2, 256, 384),
        K=vm(2, 2, 256, 384),
        V=vm(2, 2, 256, 384),
        LSE=vf(2, 2, 8, 256),
        O=vm(2, 2, 256, 384),
        R=vf(2, *cells),
        A2=vm(2, *cells),
        G=vm(2, 2, 256, 1536),
        SL=vm(2, 2, 256, 1536),
        LO=vm(2, *cells),
        DX=vm(2, *cells),
        DR=vf(*cells),
        DU=vm(2, 256, 1536),
        DZ=vm(*cells),
        DO=vm(2, 256, 384),
        DQ=vm(2, 256, 384),
        DK=vm(2, 256, 384),
        DV=vm(2, 256, 384),
        PB=vm(6, 256, 256),
        DS=vm(6, 256, 256),
        X=vm(2, *cells),
        Y=vm(2, *cells),
        GS=vm(3, 32, BR, BC),
    )
    sems = [dma((12,)), dma((2, 2)), dma((2, 2)), dma((2,)), dma((2,)), dma((2,)), dma((3,))]
    return pl.pallas_call(
        layers_kernel,
        out_shape=(
            jax.ShapeDtypeStruct((4, 256, 768), BF),
            jax.ShapeDtypeStruct((4, 256, 768), BF),
            jax.ShapeDtypeStruct((2, 3, 32, BR, BC), BF),
            jax.ShapeDtypeStruct((2, 8, 768), F32),
        ),
        in_specs=[pl.BlockSpec(memory_space=pltpu.SMEM)] + [anywhere] * 12,
        out_specs=(anywhere, anywhere, anywhere, pl.BlockSpec(memory_space=pltpu.VMEM)),
        scratch_shapes=list(scratch.values()) + sems,
        compiler_params=pltpu.CompilerParams(collective_id=1, has_side_effects=True, vmem_limit_bytes=63 * 2**20),
        name="layers",
    )(species, emb, cot, pk_own, pk_other, *own_w, *other_w)


def widen_kernel(down, up, heads, down_out, up_out, qkv_out, out_out):
    for h in range(2):
        down_out[:, h * BC : (h + 1) * BC] = down[h].astype(F32)
    for h in range(4):
        up_out[:, h * BC : (h + 1) * BC] = up[h].astype(F32)
    qkv_out[...] = heads[:3].astype(F32)
    out_out[...] = heads[3].astype(F32)


def widen(down, up, heads):
    return pl.pallas_call(
        widen_kernel,
        grid=(8,),
        in_specs=[
            pl.BlockSpec((2, 192, BC), lambda i: (0, i, 0)),
            pl.BlockSpec((4, 96, BC), lambda i: (0, i, 0)),
            pl.BlockSpec((4, 96, BC), lambda i: (0, i, 0)),
        ],
        out_specs=[
            pl.BlockSpec((192, 768), lambda i: (i, 0)),
            pl.BlockSpec((96, 1536), lambda i: (i, 0)),
            pl.BlockSpec((3, 96, BC), lambda i: (0, i, 0)),
            pl.BlockSpec((96, BC), lambda i: (lax.rem(i, 4), i // 4)),
        ],
        out_shape=[
            jax.ShapeDtypeStruct((1536, 768), F32),
            jax.ShapeDtypeStruct((768, 1536), F32),
            jax.ShapeDtypeStruct((3, 768, BC), F32),
            jax.ShapeDtypeStruct((384, 768), F32),
        ],
        name="widen",
    )(down.reshape(2, 1536, BC), up.reshape(4, 768, BC), heads.reshape(4, 768, BC))


def shards(
    embeddings,
    species,
    ln1_gain,
    ln1_bias,
    qkv_weight,
    out_weight,
    ln2_gain,
    ln2_bias,
    up_weight,
    up_bias,
    down_weight,
    species_bias,
    out_cotangent,
):
    cross = [(0, 3), (1, 2), (2, 1), (3, 0)]
    own_w = (qkv_weight[0].transpose(1, 0, 2), out_weight[0], up_weight[0], down_weight[0])
    pk = jnp.concatenate([ln1_gain, ln1_bias, ln2_gain, ln2_bias, species_bias[0], up_bias.reshape(2, 768)])
    other = lambda a: lax.ppermute(a, ("section", "tensor"), cross)
    lo4, dx4, grads, small = run_layers(
        species, embeddings, out_cotangent, pk, other(pk), own_w, tuple(other(w) for w in own_w)
    )
    down, up, heads, small = summed(grads, small)
    grad_down, grad_up, grad_qkv, grad_out = widen(down, up, heads)
    return (
        lo4.astype(F32)[None],
        dx4.astype(F32)[None],
        small[0:1],
        small[1:2],
        grad_qkv.transpose(1, 0, 2)[None],
        grad_out[None],
        small[2:3],
        small[3:4],
        grad_up[None],
        small[6:8].reshape(1, 1536),
        grad_down[None],
        small[4:6][None],
    )


def solution(mesh):
    placed = (
        P("dp", None, None),
        P("dp"),
        P("section", None),
        P("section", None),
        P("section", None, None, "tensor"),
        P("section", "tensor", None),
        P("section", None),
        P("section", None),
        P("section", None, "tensor"),
        P("section", "tensor"),
        P("section", "tensor", None),
        P("section", None, None),
        P("dp", None, None),
    )
    return jax.shard_map(
        shards,
        mesh=mesh,
        in_specs=placed,
        out_specs=(
            P("section", "dp", None, None),
            P("section", "dp", None, None),
            P("section", None),
            P("section", None),
            P("section", None, None, "tensor"),
            P("section", "tensor", None),
            P("section", None),
            P("section", None),
            P("section", None, "tensor"),
            P("section", "tensor"),
            P("section", "tensor", None),
            P("section", None, None),
        ),
        check_vma=False,
    )
```

```python
import functools

import jax
import jax.numpy as jnp
from jax import lax
from jax.experimental import pallas as pl
from jax.experimental.pallas import tpu as pltpu
from jax.sharding import PartitionSpec as P

HEAD = 64
BR, BC = 96, 384
MESH = pl.DeviceIdType.MESH
BF = jnp.bfloat16
F32 = jnp.float32

epsilon = 1e-05
root_half = 0.7071067811865476
density_scale = 0.3989422804014327


def place():
    dp = lax.axis_index("dp")
    z = lax.axis_index("tensor") * 2 + lax.rem(dp, 2)
    return dp // 8, lax.rem(dp // 2, 4), z, lax.axis_index("section")


def device(x, y, z, core):
    return (core, (x * 4 + y) * 2 + lax.rem(z, 2), z // 2)


def wrap(v):
    return lax.rem(v, 4)


def sum_kernel(g_ref, s_ref, full0, full1, full2, small_ref, r1, r2, r3, o1, s1, s2, s3, q1, q2, q3, ss, rs, qs, qr, ls, gs, gr, ws):
    full_ref = (full0, full1, full2)
    x, y, z, c = place()
    t, zl = z // 2, lax.rem(z, 2)
    peers = []
    for k in (1, 2, 3):
        zk = wrap(z + k)
        other = lax.rem(zk // 2 + t, 2)
        peers.append(
            (
                (wrap(x + k), y, z, c),
                (x, wrap(y + k), z, c),
                (x, y, zk, lax.rem(c + other, 2)),
                other,
                wrap(x + k),
                wrap(y + k),
                lax.rem(zk, 2),
            )
        )
    barrier = pltpu.get_barrier_semaphore()
    for px, py, pz, *_ in peers:
        for p in (px, py, pz):
            pl.semaphore_signal(barrier, inc=1, device_id=device(*p), device_id_type=MESH)
    pl.semaphore_wait(barrier, 9)

    def send(src, dst, sems, rsems, idx, peer):
        cp = pltpu.make_async_remote_copy(
            src_ref=src, dst_ref=dst, send_sem=sems.at[idx], recv_sem=rsems.at[idx], device_id=device(*peer), device_id_type=MESH
        )
        cp.start()
        return cp

    own = c
    first = [[], [], []]
    for k in (1, 2, 3):
        px, py, pz, other, xk, yk, zlk = peers[k - 1]
        which = lax.rem(own + other, 2)
        first[0].append(
            [send(g_ref.at[which, 0, pl.ds(zlk * 16, 16)], r1.at[0, k - 1], ss, rs, (0, 0, k - 1, 0), pz)]
        )
        first[1].append(
            [send(g_ref.at[i, 1, pl.ds(xk * 8, 8)], r1.at[1, k - 1, pl.ds(i * 8, 8)], ss, rs, (0, 1, k - 1, i), px) for i in (0, 1)]
        )
        first[2].append(
            [send(g_ref.at[i, 2, pl.ds(yk * 8, 8)], r1.at[2, k - 1, pl.ds(i * 8, 8)], ss, rs, (0, 2, k - 1, i), py) for i in (0, 1)]
        )
    q1[pl.ds(x, 1)] = s_ref[...][None]
    small = [send(q1.at[x], q1.at[x], qs, qr, (0, k - 1), peers[k - 1][0]) for k in (1, 2, 3)]
    mine = [
        pltpu.make_async_copy(g_ref.at[own, 0, pl.ds(zl * 16, 16)], o1.at[0], ls.at[0]),
        pltpu.make_async_copy(g_ref.at[0, 1, pl.ds(x * 8, 8)], o1.at[1, pl.ds(0, 8)], ls.at[1]),
        pltpu.make_async_copy(g_ref.at[1, 1, pl.ds(x * 8, 8)], o1.at[1, pl.ds(8, 8)], ls.at[2]),
        pltpu.make_async_copy(g_ref.at[0, 2, pl.ds(y * 8, 8)], o1.at[2, pl.ds(0, 8)], ls.at[3]),
        pltpu.make_async_copy(g_ref.at[1, 2, pl.ds(y * 8, 8)], o1.at[2, pl.ds(8, 8)], ls.at[4]),
    ]
    for cp in mine:
        cp.start()
    for cp in mine:
        cp.wait()

    def add(dst, part, base, recv, count):
        @pl.loop(0, count)
        def _(i):
            total = base(i).astype(F32)
            for k in range(3):
                total += recv[part, k, pl.ds(i, 1)][0].astype(F32)
            dst[part, pl.ds(i, 1)] = total.astype(BF)[None]

    for cp in small:
        cp.wait()
    q2[pl.ds(y, 1)] = (((q1[0] + q1[1]) + q1[2]) + q1[3])[None]
    small = [send(q2.at[y], q2.at[y], qs, qr, (1, k - 1), peers[k - 1][1]) for k in (1, 2, 3)]
    second = [[], [], []]
    for p in range(3):
        for group in first[p]:
            for cp in group:
                cp.wait()
        add(s1, p, lambda i, p=p: o1[p, pl.ds(i, 1)][0], r1, 16)
        for k in (1, 2, 3):
            px, py, pz, other, xk, yk, zlk = peers[k - 1]
            which = lax.rem(own + other, 2)
            if p == 0:
                second[0].append([send(s1.at[0, pl.ds(xk * 4, 4)], r2.at[0, k - 1], ss, rs, (1, 0, k - 1, 0), px)])
            elif p == 1:
                second[1].append(
                    [
                        send(s1.at[1, pl.ds(i * 8 + yk * 2, 2)], r2.at[1, k - 1, pl.ds(i * 2, 2)], ss, rs, (1, 1, k - 1, i), py)
                        for i in (0, 1)
                    ]
                )
            else:
                second[2].append([send(s1.at[2, pl.ds(which * 8 + zlk * 4, 4)], r2.at[2, k - 1], ss, rs, (1, 2, k - 1, 0), pz)])
    for cp in small:
        cp.wait()
    q2sum = ((q2[0] + q2[1]) + q2[2]) + q2[3]
    q2[pl.ds(4, 1)] = q2sum[None]
    q3[pl.ds(z, 1)] = q2[4, pl.ds(own, 1)]
    small = []
    for k in (1, 2, 3):
        which = lax.rem(own + peers[k - 1][3], 2)
        small.append(send(q2.at[4, which], q3.at[z], qs, qr, (2, k - 1), peers[k - 1][2]))
    third = [[], [], []]
    bases = [
        lambda i: s1[0, pl.ds(x * 4 + i, 1)][0],
        lambda i: s1[1, pl.ds((i // 2) * 8 + y * 2 + lax.rem(i, 2), 1)][0],
        lambda i: s1[2, pl.ds(own * 8 + zl * 4 + i, 1)][0],
    ]
    for p in range(3):
        for group in second[p]:
            for cp in group:
                cp.wait()
        add(s2, p, bases[p], r2, 4)
        for k in (1, 2, 3):
            px, py, pz, other, xk, yk, zlk = peers[k - 1]
            which = lax.rem(own + other, 2)
            if p == 0:
                third[0].append(send(s2.at[0, yk], r3.at[0, k - 1, 0], ss, rs, (2, 0, k - 1, 0), py))
            elif p == 1:
                third[1].append(send(s2.at[1, which * 2 + zlk], r3.at[1, k - 1, 0], ss, rs, (2, 1, k - 1, 0), pz))
            else:
                third[2].append(send(s2.at[2, xk], r3.at[2, k - 1, 0], ss, rs, (2, 2, k - 1, 0), px))
    for cp in small:
        cp.wait()
    small_ref[...] = ((q3[0] + q3[1]) + q3[2]) + q3[3]
    bases = [
        lambda i: s2[0, pl.ds(y, 1)][0],
        lambda i: s2[1, pl.ds(own * 2 + zl, 1)][0],
        lambda i: s2[2, pl.ds(x, 1)][0],
    ]
    number = (zl * 16 + x * 4 + y, x * 8 + y * 2 + zl, y * 8 + zl * 4 + x)
    gather = [[], [], []]
    local = []

    def spread(p, step, start, count, axis):
        out = []
        for k in (1, 2, 3):
            if axis == 2 and k != 2:
                continue
            peer = peers[k - 1][axis] if axis < 2 else (x, y, t * 2 + 1 - zl, c)
            part = full_ref[p].at[pl.ds(start, count)]
            out.append(send(part, part, gs, gr, (p, step, k - 1), peer))
        return out

    for p in range(3):
        for cp in third[p]:
            cp.wait()
        add(s3, p, bases[p], r3, 1)
        cp = pltpu.make_async_copy(s3.at[p], full_ref[p].at[pl.ds(number[p], 1)], ws.at[p])
        cp.start()
        local.append(cp)
    orders = (
        ((1, number[0], 1), (0, zl * 16 + x * 4, 4), (2, zl * 16, 16)),
        ((2, number[1], 1), (1, x * 8 + y * 2, 2), (0, x * 8, 8)),
        ((0, number[2], 1), (2, y * 8 + zl * 4, 4), (1, y * 8, 8)),
    )
    for step in range(3):
        for p in range(3):
            if step == 0:
                local[p].wait()
            else:
                for cp in gather[p]:
                    cp.wait()
            axis, start, count = orders[p][step]
            gather[p] = spread(p, step, start, count, axis)
    for p in range(3):
        for cp in gather[p]:
            cp.wait()


def summed(grads, small):
    dma = pltpu.SemaphoreType.DMA
    blocks = lambda *lead: pltpu.VMEM((*lead, BR, BC), BF)
    anywhere = pl.BlockSpec(memory_space=pl.ANY)
    return pl.pallas_call(
        sum_kernel,
        out_shape=(jax.ShapeDtypeStruct((32, BR, BC), BF),) * 3 + (jax.ShapeDtypeStruct((8, 768), F32),),
        in_specs=[anywhere, pl.BlockSpec(memory_space=pltpu.VMEM)],
        out_specs=(anywhere, anywhere, anywhere, pl.BlockSpec(memory_space=pltpu.VMEM)),
        scratch_shapes=[
            blocks(3, 3, 16),
            blocks(3, 3, 4),
            blocks(3, 3, 1),
            blocks(3, 16),
            blocks(3, 16),
            blocks(3, 4),
            blocks(3, 1),
            pltpu.VMEM((4, 2, 8, 768), F32),
            pltpu.VMEM((5, 2, 8, 768), F32),
            pltpu.VMEM((4, 8, 768), F32),
            dma((3, 3, 3, 2)),
            dma((3, 3, 3, 2)),
            dma((3, 3)),
            dma((3, 3)),
            dma((5,)),
            dma((3, 3, 3)),
            dma((3, 3, 3)),
            dma((3,)),
        ],
        compiler_params=pltpu.CompilerParams(collective_id=0, has_side_effects=True, vmem_limit_bytes=48 * 2**20),
        name="gradient_sums",
    )(grads, small)


def norm(values):
    center = values - jnp.mean(values, axis=-1, keepdims=True)
    inverse = lax.rsqrt(jnp.mean(center * center, axis=-1, keepdims=True) + epsilon)
    return (center * inverse, inverse)


def norm_back(grad_normed, normed, inverse):
    return inverse * (
        grad_normed
        - jnp.mean(grad_normed, axis=-1, keepdims=True)
        - normed * jnp.mean(grad_normed * normed, axis=-1, keepdims=True)
    )


def dot(a, b):
    return jnp.dot(a, b, preferred_element_type=F32)


def dot_rows(a, b):
    return lax.dot_general(a, b, (((0,), (0,)), ((), ())), preferred_element_type=F32)


def dot_back(a, b):
    return lax.dot_general(a, b, (((1,), (1,)), ((), ())), preferred_element_type=F32)


def column_sum(a):
    return jnp.sum(a, axis=0, keepdims=True)


def layers_kernel(
    species, emb, cot, pk_own, *refs
):
    own_w = refs[:4]
    lo4, dx4, g_out, small = refs[4:8]
    (qkv_w, out_w, up_w, down_w, pk, emb_v, cot_v, S, A1, Q, K, V, LSE, O, R, A2, G, SL, LO, DX, DR, DU, DZ, DO, DQ, DK, DV, PB, DS, X, Y, GS) = refs[8:40]
    load_sem, x_send, x_recv, out_local, out_send, out_recv, g_sem, w_send, w_recv = refs[40:]
    x, y, z, c = place()
    t = z // 2
    zl = lax.rem(z, 2)
    sibling = device(x, y, z, 1 - c)
    far = device(x, y, lax.rem(z + 2, 4), c)
    cross = device(x, y, 3 - z, 1 - c)
    pair = device(x, y, 2 * t + 1 - zl, c)
    along_x = [device(wrap(x + k), y, z, c) for k in (1, 2, 3)]
    along_y = [device(x, wrap(y + k), z, c) for k in (1, 2, 3)]
    barrier = pltpu.get_barrier_semaphore()
    for p in (sibling, far, cross, pair, *along_x, *along_y):
        pl.semaphore_signal(barrier, inc=1, device_id=p, device_id_type=MESH)
    weights = (qkv_w, out_w, up_w, down_w)

    def load(src, dst, i):
        cp = pltpu.make_async_copy(src, dst, load_sem.at[i])
        cp.start()
        return cp

    w_loads = [load(own_w[i], w.at[c], i) for i, w in enumerate(weights)]
    start = [load(emb.at[pl.ds(2 * t, 2)], emb_v, 4), load(pk_own, pk.at[c], 5)]
    cot_load = load(cot.at[pl.ds(2 * t, 2)], cot_v, 6)
    pl.semaphore_wait(barrier, 10)

    moves = []

    def move(src, dst, peer):
        i = len(moves)
        cp = pltpu.make_async_remote_copy(
            src_ref=src, dst_ref=dst, send_sem=w_send.at[i], recv_sem=w_recv.at[i], device_id=peer, device_id_type=MESH
        )
        moves.append(cp)
        return cp

    def start_all(copies):
        for cp in copies:
            cp.start()

    def arrived(copies):
        for cp in copies:
            cp.wait_recv()

    pk_move = move(pk_own, pk.at[c], cross)
    up_hop = move(own_w[2].at[pl.ds(x * 192 + y * 48, 48)], up_w.at[c, pl.ds(x * 192 + y * 48, 48)], cross)
    down_hop = move(own_w[3].at[pl.ds(y * 384 + x * 96, 96)], down_w.at[c, pl.ds(y * 384 + x * 96, 96)], cross)
    start_all((pk_move, up_hop, down_hop))
    direct = [
        move(own_w[0].at[i, pl.ds((1 - zl) * 384, 384)], qkv_w.at[c, i, pl.ds((1 - zl) * 384, 384)], cross) for i in range(3)
    ]
    direct.append(move(own_w[1].at[pl.ds((1 - zl) * 192, 192)], out_w.at[c, pl.ds((1 - zl) * 192, 192)], cross))
    pl.when(c == 0)(lambda: start_all(direct))

    def onward(ref, rows, count, peers):
        part = ref.at[1 - c, pl.ds(rows, count)]
        return [move(part, part, p) for p in peers]

    up_y = onward(up_w, x * 192 + y * 48, 48, along_y)
    down_x = onward(down_w, y * 384 + x * 96, 96, along_x)
    up_x = onward(up_w, x * 192, 192, along_x)
    down_y = onward(down_w, y * 384, 384, along_y)
    trade = []
    for i in range(3):
        part = qkv_w.at[1 - c, i, pl.ds(zl * 384, 384)]
        trade.append(move(part, part, pair))
    part = out_w.at[1 - c, pl.ds(zl * 192, 192)]
    trade.append(move(part, part, pair))

    arrived([up_hop])
    start_all(up_y)
    arrived([down_hop])
    start_all(down_x)
    arrived(up_y)
    start_all(up_x)
    arrived(down_x)
    start_all(down_y)

    def hand_on():
        for i in range(4):
            arrived([direct[i]])
            trade[i].start()

    @pl.when(c == 1)
    def _():
        hand_on()
        start_all(direct)

    arrived([pk_move])
    for cp in start:
        cp.wait()

    def need(l, i):
        incoming = ([*trade[:3]], [trade[3]], up_x, down_y)[i]
        if l == 0:
            w_loads[i].wait()
        pl.when(c == 1 - l)(lambda: arrived(incoming))

    flying = {}

    def push(kind, b):
        cp = pltpu.make_async_remote_copy(
            src_ref=X.at[kind, b],
            dst_ref=Y.at[kind, b],
            send_sem=x_send.at[kind, b],
            recv_sem=x_recv.at[kind, b],
            device_id=sibling,
            device_id_type=MESH,
        )
        cp.start()
        flying[kind, b] = cp

    def both(kind, b):
        flying.pop((kind, b)).wait()
        return X[kind, b].astype(F32) + Y[kind, b].astype(F32)

    def flag(b):
        return species[2 * t + b]

    def heads_forward(l, b):
        if l == 0:
            xin = emb_v[b].astype(F32)
        else:
            low = (R[0, b] + both(1, b)).astype(BF)
            LO[0, b] = low
            xin = low.astype(F32)
        s = xin + jnp.where(flag(b) == 0, pk[l, 4:5], pk[l, 5:6])
        S[l, b] = s
        n1, _ = norm(s)
        a1 = (n1 * pk[l, 0:1] + pk[l, 1:2]).astype(BF)
        A1[l, b] = a1
        if b == 0:
            need(l, 0)
        for i, part in enumerate((Q, K, V)):
            part[l, b] = dot(a1, qkv_w[l, i]).astype(BF)
        for h in range(6):
            hs = slice(h * HEAD, h * HEAD + HEAD)
            sc = dot_back(K[l, b, :, hs], Q[l, b, :, hs]) * HEAD**-0.5
            top = jnp.max(sc, axis=0, keepdims=True)
            e = jnp.exp(sc - top)
            total = jnp.sum(e, axis=0, keepdims=True)
            PB[h] = (e * (1.0 / total)).astype(BF)
            LSE[l, b, h : h + 1] = top + jnp.log(total)
        for h in range(6):
            hs = slice(h * HEAD, h * HEAD + HEAD)
            O[l, b, :, hs] = dot_rows(PB[h], V[l, b, :, hs]).astype(BF)
        if b == 0:
            need(l, 1)
        X[0, b] = dot(O[l, b], out_w[l]).astype(BF)
        push(0, b)

    def units_forward(l, b):
        r = S[l, b] + both(0, b)
        R[l, b] = r
        n2, _ = norm(r)
        a2 = (n2 * pk[l, 2:3] + pk[l, 3:4]).astype(BF)
        A2[l, b] = a2
        if b == 0:
            need(l, 2)
        for j in range(2):
            cols = slice(j * 768, j * 768 + 768)
            u = dot(a2, up_w[l, :, cols]) + pk[l, 6 + j : 7 + j]
            cdf = 0.5 * (1.0 + lax.erf(u * root_half))
            G[l, b, :, cols] = (u * cdf).astype(BF)
            SL[l, b, :, cols] = (cdf + u * density_scale * jnp.exp(-0.5 * u * u)).astype(BF)
        if b == 0:
            need(l, 3)
        X[1, b] = dot(G[l, b], down_w[l]).astype(BF)
        push(1, b)

    def rows(ref, *lead):
        a = ref[lead] if lead else ref[...]
        return a.reshape(512, a.shape[-1])

    def put(part, number, value):
        for i in range(value.shape[0] // BR):
            GS[part, number + i] = value[i * BR : (i + 1) * BR]

    g_copies = {}

    def flush(l, part):
        cp = pltpu.make_async_copy(GS.at[part], g_out.at[l, part], g_sem.at[part])
        cp.start()
        g_copies[part] = cp

    def free(part):
        if part in g_copies:
            g_copies.pop(part).wait()

    def dy(l, b):
        return cot_v[b] if l == 1 else DX[1, b].astype(F32)

    def units_backward(l):
        for b in range(2):
            DZ[b] = dy(l, b).astype(BF) if l == 1 else DX[1, b]
            for j in range(2):
                cols = slice(j * 768, j * 768 + 768)
                DU[b, :, cols] = (dot_back(DZ[b], down_w[l, cols]) * SL[l, b, :, cols].astype(F32)).astype(BF)
            X[0, b] = dot_back(DU[b], up_w[l]).astype(BF)
            push(0, b)
        free(0)
        dz = rows(DZ)
        for j in range(2):
            gd = dot_rows(rows(G, l)[:, j * 768 : j * 768 + 768], dz).astype(BF)
            for h in range(2):
                put(0, h * 16 + j * 8, gd[:, h * BC : (h + 1) * BC])
        flush(l, 0)
        free(1)
        a2 = rows(A2, l)
        for j in range(2):
            du = rows(DU)[:, j * 768 : j * 768 + 768]
            gu = dot_rows(a2, du).astype(BF)
            for h in range(2):
                put(1, (2 * j + h) * 8, gu[:, h * BC : (h + 1) * BC])
            small[l, 6 + j : 7 + j] = column_sum(du.astype(F32))
        flush(l, 1)
        gain = bias = 0.0
        for b in range(2):
            da2 = both(0, b)
            n2, inv = norm(R[l, b])
            gain += column_sum(da2 * n2)
            bias += column_sum(da2)
            dr = dy(l, b) + norm_back(da2 * pk[l, 2:3], n2, inv)
            DR[b] = dr
            DZ[b] = dr.astype(BF)
        small[l, 2:3] = gain
        small[l, 3:4] = bias

    def heads_backward(l):
        for b in range(2):
            DO[b] = dot_back(DZ[b], out_w[l]).astype(BF)
            for h in range(6):
                hs = slice(h * HEAD, h * HEAD + HEAD)
                sc = dot_back(K[l, b, :, hs], Q[l, b, :, hs]) * HEAD**-0.5
                p = jnp.exp(sc - LSE[l, b, h : h + 1])
                dp = dot_back(V[l, b, :, hs], DO[b, :, hs])
                pdp = p * dp
                PB[h] = p.astype(BF)
                DS[h] = (pdp - p * jnp.sum(pdp, axis=0, keepdims=True)).astype(BF)
            for h in range(6):
                hs = slice(h * HEAD, h * HEAD + HEAD)
                DV[b, :, hs] = dot(PB[h], DO[b, :, hs]).astype(BF)
                DK[b, :, hs] = (dot(DS[h], Q[l, b, :, hs]) * HEAD**-0.5).astype(BF)
                DQ[b, :, hs] = (dot_rows(DS[h], K[l, b, :, hs]) * HEAD**-0.5).astype(BF)
            X[1, b] = (
                dot_back(DQ[b], qkv_w[l, 0]) + dot_back(DK[b], qkv_w[l, 1]) + dot_back(DV[b], qkv_w[l, 2])
            ).astype(BF)
            push(1, b)
        free(2)
        go = dot_rows(rows(O, l), rows(DZ)).astype(BF)
        for h in range(2):
            put(2, 24 + h * 4, go[:, h * BC : (h + 1) * BC])
        a1 = rows(A1, l)
        for i, d in enumerate((DQ, DK, DV)):
            put(2, i * 8, dot_rows(a1, rows(d)).astype(BF))
        flush(l, 2)
        gain = bias = 0.0
        table = [0.0, 0.0]
        for b in range(2):
            da1 = both(1, b)
            n1, inv = norm(S[l, b])
            gain += column_sum(da1 * n1)
            bias += column_sum(da1)
            dx = DR[b] + norm_back(da1 * pk[l, 0:1], n1, inv)
            DX[l, b] = dx.astype(BF)
            total = column_sum(dx)
            for k in range(2):
                table[k] += jnp.where(flag(b) == k, total, 0.0)
        small[l, 0:1] = gain
        small[l, 1:2] = bias
        small[l, 4:5] = table[0]
        small[l, 5:6] = table[1]

    def share(src, dst, i):
        part = dst.at[pl.ds(2 * t, 2)]
        here = pltpu.make_async_copy(src, part, out_local.at[i])
        here.start()
        there = pltpu.make_async_remote_copy(
            src_ref=src, dst_ref=part, send_sem=out_send.at[i], recv_sem=out_recv.at[i], device_id=far, device_id_type=MESH
        )
        there.start()
        return here, there

    for l in range(2):
        for b in range(2):
            heads_forward(l, b)
        if l == 0:
            pl.when(c == 0)(hand_on)
        for b in range(2):
            units_forward(l, b)
    for b in range(2):
        LO[1, b] = (R[1, b] + both(1, b)).astype(BF)
    finish = list(share(LO.at[c], lo4, 0))
    cot_load.wait()
    for l in (1, 0):
        units_backward(l)
        heads_backward(l)
    finish += share(DX.at[c], dx4, 1)
    for part in range(3):
        free(part)
    for cp in finish:
        cp.wait()
    for cp in moves:
        cp.wait_send()


def run_layers(species, emb, cot, pk_own, own_w):
    anywhere = pl.BlockSpec(memory_space=pl.ANY)
    dma = pltpu.SemaphoreType.DMA
    vm = lambda *shape: pltpu.VMEM(shape, BF)
    vf = lambda *shape: pltpu.VMEM(shape, F32)
    cells = (2, 256, 768)
    scratch = dict(
        qkv_w=vm(2, 3, 768, 384),
        out_w=vm(2, 384, 768),
        up_w=vm(2, 768, 1536),
        down_w=vm(2, 1536, 768),
        pk=vf(2, 8, 768),
        emb_v=vm(*cells),
        cot_v=vf(*cells),
        S=vf(2, *cells),
        A1=vm(2, *cells),
        Q=vm(2, 2, 256, 384),
        K=vm(2, 2, 256, 384),
        V=vm(2, 2, 256, 384),
        LSE=vf(2, 2, 8, 256),
        O=vm(2, 2, 256, 384),
        R=vf(2, *cells),
        A2=vm(2, *cells),
        G=vm(2, 2, 256, 1536),
        SL=vm(2, 2, 256, 1536),
        LO=vm(2, *cells),
        DX=vm(2, *cells),
        DR=vf(*cells),
        DU=vm(2, 256, 1536),
        DZ=vm(*cells),
        DO=vm(2, 256, 384),
        DQ=vm(2, 256, 384),
        DK=vm(2, 256, 384),
        DV=vm(2, 256, 384),
        PB=vm(6, 256, 256),
        DS=vm(6, 256, 256),
        X=vm(2, *cells),
        Y=vm(2, *cells),
        GS=vm(3, 32, BR, BC),
    )
    sems = [dma((7,)), dma((2, 2)), dma((2, 2)), dma((2,)), dma((2,)), dma((2,)), dma((3,)), dma((23,)), dma((23,))]
    return pl.pallas_call(
        layers_kernel,
        out_shape=(
            jax.ShapeDtypeStruct((4, 256, 768), BF),
            jax.ShapeDtypeStruct((4, 256, 768), BF),
            jax.ShapeDtypeStruct((2, 3, 32, BR, BC), BF),
            jax.ShapeDtypeStruct((2, 8, 768), F32),
        ),
        in_specs=[pl.BlockSpec(memory_space=pltpu.SMEM)] + [anywhere] * 7,
        out_specs=(anywhere, anywhere, anywhere, pl.BlockSpec(memory_space=pltpu.VMEM)),
        scratch_shapes=list(scratch.values()) + sems,
        compiler_params=pltpu.CompilerParams(collective_id=1, has_side_effects=True, vmem_limit_bytes=63 * 2**20),
        name="layers",
    )(species, emb, cot, pk_own, *own_w)


def widen_kernel(down, up, heads, down_out, up_out, qkv_out, out_out):
    for h in range(2):
        down_out[:, h * BC : (h + 1) * BC] = down[h].astype(F32)
    for h in range(4):
        up_out[:, h * BC : (h + 1) * BC] = up[h].astype(F32)
    qkv_out[...] = heads[:3].astype(F32)
    out_out[...] = heads[3].astype(F32)


def widen(down, up, heads):
    return pl.pallas_call(
        widen_kernel,
        grid=(8,),
        in_specs=[
            pl.BlockSpec((2, 192, BC), lambda i: (0, i, 0)),
            pl.BlockSpec((4, 96, BC), lambda i: (0, i, 0)),
            pl.BlockSpec((4, 96, BC), lambda i: (0, i, 0)),
        ],
        out_specs=[
            pl.BlockSpec((192, 768), lambda i: (i, 0)),
            pl.BlockSpec((96, 1536), lambda i: (i, 0)),
            pl.BlockSpec((3, 96, BC), lambda i: (0, i, 0)),
            pl.BlockSpec((96, BC), lambda i: (lax.rem(i, 4), i // 4)),
        ],
        out_shape=[
            jax.ShapeDtypeStruct((1536, 768), F32),
            jax.ShapeDtypeStruct((768, 1536), F32),
            jax.ShapeDtypeStruct((3, 768, BC), F32),
            jax.ShapeDtypeStruct((384, 768), F32),
        ],
        name="widen",
    )(down.reshape(2, 1536, BC), up.reshape(4, 768, BC), heads.reshape(4, 768, BC))


def shards(
    embeddings,
    species,
    ln1_gain,
    ln1_bias,
    qkv_weight,
    out_weight,
    ln2_gain,
    ln2_bias,
    up_weight,
    up_bias,
    down_weight,
    species_bias,
    out_cotangent,
):
    own_w = (qkv_weight[0].transpose(1, 0, 2), out_weight[0], up_weight[0], down_weight[0])
    pk = jnp.concatenate([ln1_gain, ln1_bias, ln2_gain, ln2_bias, species_bias[0], up_bias.reshape(2, 768)])
    lo4, dx4, grads, small = run_layers(species, embeddings, out_cotangent, pk, own_w)
    down, up, heads, small = summed(grads, small)
    grad_down, grad_up, grad_qkv, grad_out = widen(down, up, heads)
    return (
        lo4.astype(F32)[None],
        dx4.astype(F32)[None],
        small[0:1],
        small[1:2],
        grad_qkv.transpose(1, 0, 2)[None],
        grad_out[None],
        small[2:3],
        small[3:4],
        grad_up[None],
        small[6:8].reshape(1, 1536),
        grad_down[None],
        small[4:6][None],
    )


def solution(mesh):
    placed = (
        P("dp", None, None),
        P("dp"),
        P("section", None),
        P("section", None),
        P("section", None, None, "tensor"),
        P("section", "tensor", None),
        P("section", None),
        P("section", None),
        P("section", None, "tensor"),
        P("section", "tensor"),
        P("section", "tensor", None),
        P("section", None, None),
        P("dp", None, None),
    )
    return jax.shard_map(
        shards,
        mesh=mesh,
        in_specs=placed,
        out_specs=(
            P("section", "dp", None, None),
            P("section", "dp", None, None),
            P("section", None),
            P("section", None),
            P("section", None, None, "tensor"),
            P("section", "tensor", None),
            P("section", None),
            P("section", None),
            P("section", None, "tensor"),
            P("section", "tensor"),
            P("section", "tensor", None),
            P("section", None, None),
        ),
        check_vma=False,
    )
```

```python
import functools

import jax
import jax.numpy as jnp
from jax import lax
from jax.experimental import pallas as pl
from jax.experimental.pallas import tpu as pltpu
from jax.sharding import PartitionSpec as P

HEAD = 64
MOVES = 180
UR, UC = 48, 384
MESH = pl.DeviceIdType.MESH
BF = jnp.bfloat16
F32 = jnp.float32

epsilon = 1e-05
root_half = 0.7071067811865476
density_scale = 0.3989422804014327


def place():
    dp = lax.axis_index("dp")
    z = lax.axis_index("tensor") * 2 + lax.rem(dp, 2)
    return dp // 8, lax.rem(dp // 2, 4), z, lax.axis_index("section")


def device(x, y, z, core):
    return (core, (x * 4 + y) * 2 + lax.rem(z, 2), z // 2)


def flip(v):
    return v + 1 - 2 * lax.rem(v, 2)


def wrap(v):
    return lax.rem(v, 4)


def norm(values):
    center = values - jnp.mean(values, axis=-1, keepdims=True)
    inverse = lax.rsqrt(jnp.mean(center * center, axis=-1, keepdims=True) + epsilon)
    return (center * inverse, inverse)


def norm_back(grad_normed, normed, inverse):
    return inverse * (
        grad_normed
        - jnp.mean(grad_normed, axis=-1, keepdims=True)
        - normed * jnp.mean(grad_normed * normed, axis=-1, keepdims=True)
    )


def dot(a, b):
    return jnp.dot(a, b, preferred_element_type=F32)


def dot_rows(a, b):
    return lax.dot_general(a, b, (((0,), (0,)), ((), ())), preferred_element_type=F32)


def dot_back(a, b):
    return lax.dot_general(a, b, (((1,), (1,)), ((), ())), preferred_element_type=F32)


def column_sum(a):
    return jnp.sum(a, axis=0, keepdims=True)


def split_refs(refs, counts):
    out, at = [], 0
    for n in counts:
        out.append(refs[at : at + n])
        at += n
    return out


def layers_kernel(
    species, emb, cot, pk_own, *refs
):
    own_w = refs[:4]
    lo4, dx4, g_out, r1o, r1f, r1x, r1y, full0, full1, full2, small_out = refs[4:15]
    full = (full0, full1, full2)
    (
        (qkv_w, out_w, up_w, down_w, pk),
        (S, A1, Q, K, V, LSE, O, R, A2, G, SL, LO, DX, DR, DZ, DO, PB, DS, X, Y),
        (GS, PAD, SM, SMR, s1a, s1f, s1x, s1y, s2a, s2b, s2c, s2f, s3, s3f, r2a, r2b, r2o, r2f, r3a, r3o, r3f, r3c),
        (load_sem, x_send, x_recv, out_local, out_send, out_recv, g_sem, w_send, w_recv, pull_sem, keep_sem),
    ) = split_refs(refs[15:], (5, 20, 22, 11))
    x, y, z, c = place()
    t = z // 2
    zl = lax.rem(z, 2)
    sibling = device(x, y, z, 1 - c)
    far = device(x, y, lax.rem(z + 2, 4), c)
    cross = device(x, y, 3 - z, 1 - c)
    pair = device(x, y, 2 * t + 1 - zl, c)
    along_x = [device(wrap(x + k), y, z, c) for k in (1, 2, 3)]
    along_y = [device(x, wrap(y + k), z, c) for k in (1, 2, 3)]
    barrier = pltpu.get_barrier_semaphore()
    for p in (sibling, far, cross, pair, *along_x, *along_y):
        pl.semaphore_signal(barrier, inc=1, device_id=p, device_id_type=MESH)
    weights = (qkv_w, out_w, up_w, down_w)

    def load(src, dst, i):
        cp = pltpu.make_async_copy(src, dst, load_sem.at[i])
        cp.start()
        return cp

    w_loads = [load(own_w[i], w.at[c], i) for i, w in enumerate(weights)]
    start = [load(emb.at[pl.ds(2 * t, 2)], DZ, 4), load(pk_own, pk.at[c], 5)]
    cot_load = load(cot.at[pl.ds(2 * t, 2)], DR, 6)
    pl.semaphore_wait(barrier, 10)
    near_x, wrap_x = device(flip(x), y, z, c), device(3 - x, y, z, c)
    near_y, wrap_y = device(x, flip(y), z, c), device(x, 3 - y, z, c)

    moves = []

    def move(src, dst, peer):
        i = len(moves)
        cp = pltpu.make_async_remote_copy(
            src_ref=src, dst_ref=dst, send_sem=w_send.at[i], recv_sem=w_recv.at[i], device_id=peer, device_id_type=MESH
        )
        moves.append(cp)
        return cp

    def start_all(copies):
        for cp in copies:
            cp.start()

    def arrived(copies):
        for cp in copies:
            cp.wait_recv()

    def sent(copies):
        for cp in copies:
            cp.wait_send()

    pk_move = move(pk_own, pk.at[c], cross)
    up_hop = move(own_w[2].at[pl.ds(x * 192 + y * 48, 48)], up_w.at[c, pl.ds(x * 192 + y * 48, 48)], cross)
    down_hop = move(own_w[3].at[pl.ds(y * 384 + x * 96, 96)], down_w.at[c, pl.ds(y * 384 + x * 96, 96)], cross)
    start_all((pk_move, up_hop, down_hop))
    direct = [
        move(own_w[0].at[i, pl.ds((1 - zl) * 384, 384)], qkv_w.at[c, i, pl.ds((1 - zl) * 384, 384)], cross) for i in range(3)
    ]
    direct.append(move(own_w[1].at[pl.ds((1 - zl) * 192, 192)], out_w.at[c, pl.ds((1 - zl) * 192, 192)], cross))
    pl.when(c == 0)(lambda: start_all(direct))

    def onward(ref, rows, count, peers):
        part = ref.at[1 - c, pl.ds(rows, count)]
        return [move(part, part, p) for p in peers]

    up_y = onward(up_w, x * 192 + y * 48, 48, along_y)
    down_x = onward(down_w, y * 384 + x * 96, 96, along_x)
    up_x = onward(up_w, x * 192, 192, along_x)
    down_y = onward(down_w, y * 384, 384, along_y)
    trade = []
    for i in range(3):
        part = qkv_w.at[1 - c, i, pl.ds(zl * 384, 384)]
        trade.append(move(part, part, pair))
    part = out_w.at[1 - c, pl.ds(zl * 192, 192)]
    trade.append(move(part, part, pair))

    w_count = len(moves)
    arrived([up_hop])
    start_all(up_y)
    arrived([down_hop])
    start_all(down_x)
    arrived(up_y)
    start_all(up_x)
    arrived(down_x)
    start_all(down_y)

    def hand_on():
        for i in range(4):
            arrived([direct[i]])
            trade[i].start()

    @pl.when(c == 1)
    def _():
        hand_on()
        start_all(direct)

    arrived([pk_move])
    for cp in start:
        cp.wait()

    def need(l, i):
        incoming = ([*trade[:3]], [trade[3]], up_x, down_y)[i]
        if l == 0:
            w_loads[i].wait()
        pl.when(c == 1 - l)(lambda: arrived(incoming))

    flying = {}

    def push(kind, b):
        cp = pltpu.make_async_remote_copy(
            src_ref=X.at[kind, b],
            dst_ref=Y.at[kind, b],
            send_sem=x_send.at[kind, b],
            recv_sem=x_recv.at[kind, b],
            device_id=sibling,
            device_id_type=MESH,
        )
        cp.start()
        flying[kind, b] = cp

    def both(kind, b):
        flying.pop((kind, b)).wait()
        return X[kind, b].astype(F32) + Y[kind, b].astype(F32)

    def flag(b):
        return species[2 * t + b]

    def heads_forward(l, b):
        if l == 0:
            xin = DZ[b].astype(F32)
        else:
            low = (R[0, b] + both(1, b)).astype(BF)
            LO[0, b] = low
            xin = low.astype(F32)
        s = xin + jnp.where(flag(b) == 0, pk[l, 4:5], pk[l, 5:6])
        S[l, b] = s
        n1, _ = norm(s)
        a1 = (n1 * pk[l, 0:1] + pk[l, 1:2]).astype(BF)
        A1[l, b] = a1
        if b == 0:
            need(l, 0)
        for i, part in enumerate((Q, K, V)):
            part[l, b] = dot(a1, qkv_w[l, i]).astype(BF)
        for h in range(6):
            hs = slice(h * HEAD, h * HEAD + HEAD)
            sc = dot_back(K[l, b, :, hs], Q[l, b, :, hs]) * HEAD**-0.5
            top = jnp.max(sc, axis=0, keepdims=True)
            e = jnp.exp(sc - top)
            total = jnp.sum(e, axis=0, keepdims=True)
            PB[h] = (e * (1.0 / total)).astype(BF)
            LSE[l, b, h : h + 1] = top + jnp.log(total)
        for h in range(6):
            hs = slice(h * HEAD, h * HEAD + HEAD)
            O[l, b, :, hs] = dot_rows(PB[h], V[l, b, :, hs]).astype(BF)
        if b == 0:
            need(l, 1)
        X[0, b] = dot(O[l, b], out_w[l]).astype(BF)
        push(0, b)

    def units_forward(l, b):
        r = S[l, b] + both(0, b)
        R[l, b] = r
        n2, _ = norm(r)
        a2 = (n2 * pk[l, 2:3] + pk[l, 3:4]).astype(BF)
        A2[l, b] = a2
        if b == 0:
            need(l, 2)
        for j in range(2):
            cols = slice(j * 768, j * 768 + 768)
            u = dot(a2, up_w[l, :, cols]) + pk[l, 6 + j : 7 + j]
            cdf = 0.5 * (1.0 + lax.erf(u * root_half))
            G[l, b, :, cols] = (u * cdf).astype(BF)
            SL[l, b, :, cols] = (cdf + u * density_scale * jnp.exp(-0.5 * u * u)).astype(BF)
        if b == 0:
            need(l, 3)
        X[1, b] = dot(G[l, b], down_w[l]).astype(BF)
        push(1, b)

    def rows(ref, *lead):
        a = ref[lead] if lead else ref[...]
        return a.reshape(512, a.shape[-1])

    def put(slot, number, value):
        for i in range(value.shape[0] // UR):
            GS[slot, number + i] = value[i * UR : (i + 1) * UR]

    g_copies = {}

    def flush(l, part):
        cp = pltpu.make_async_copy(GS.at[part % 2], g_out.at[l, part], g_sem.at[part % 2])
        cp.start()
        g_copies[part % 2] = cp

    def free(slot):
        if slot in g_copies:
            g_copies.pop(slot).wait()

    def dy(l, b):
        return DR[b] if l == 1 else DX[1, b].astype(F32)


    def at(ref, start, count):
        return ref.at[pl.ds(start, count)]

    def add_up(jobs, far_off):
        if far_off:
            pulls, where = [], 0
            for dst, pieces, count in jobs:
                for i, piece in enumerate(pieces):
                    cp = pltpu.make_async_copy(piece, at(PAD, where, count), pull_sem.at[len(pulls)])
                    cp.start()
                    pulls.append(cp)
                    pieces[i] = at(PAD, where, count)
                    where += count
            for cp in pulls:
                cp.wait()
        for dst, pieces, count in jobs:
            total = pieces[0][...].astype(F32)
            for piece in pieces[1:]:
                total += piece[...].astype(F32)
            dst[...] = total.astype(BF)

    class Ring:
        def __init__(self, i, near_dev, wrap_dev, src, rcv, out, n, far_off=False):
            h = n // 2
            near, other, opposite = flip(i), 3 - i, 3 - flip(i)
            self.far_off = far_off
            of = lambda k, lo: at(src, k * n + lo, h)
            got = lambda k: at(rcv, k * h, h)
            self.first = [
                move(of(near, 0), got(0), near_dev),
                move(of(other, h), got(2), wrap_dev),
                move(of(opposite, 0), got(1), near_dev),
                move(of(opposite, h), got(3), wrap_dev),
            ]
            low, high = at(out, 0, h), at(out, h, h)
            self.second = [move(low, got(4), wrap_dev), move(high, got(5), near_dev)]
            self.mid_jobs = lambda: [(low, [of(other, 0), got(1)], h), (high, [of(near, h), got(3)], h)]
            self.end_jobs = lambda: [
                (low, [of(i, 0), got(0), got(4)], h),
                (high, [of(i, h), got(2), got(5)], h),
            ]

        def start(self):
            start_all(self.first[2:])
            start_all(self.first[:2])

        def mid(self):
            arrived(self.first[2:])
            add_up(self.mid_jobs(), self.far_off)
            start_all(self.second)

        def end(self):
            arrived(self.first[:2])
            arrived(self.second)
            sent(self.second)
            add_up(self.end_jobs(), self.far_off)

        def close(self):
            sent(self.first)

    class Column:
        def __init__(self, l, src, rcv_own, rcv_far, out_own, out_far, n, far_off=False):
            h = n // 2
            self.l, self.far_off = l, far_off
            of = lambda k, lo: at(src, k * n + lo, h)
            got = lambda k: at(rcv_own, k * h, h)
            kept = at(rcv_far, 0, h)
            low, high = at(out_own, 0, h), at(out_own, h, h)
            passed = at(out_far, 0, h)
            self.own_pair = move(of(1 - zl, 0), got(0), pair)
            self.far_pair = move(of(zl, 0), kept, pair)
            self.far_cross = [move(of(0, h), got(1), cross), move(of(1, h), got(2), cross)]
            self.own_second = move(high, got(4), pair)
            self.far_second = move(passed, got(3), cross)
            self.own_mid = lambda: [(high, [of(1 - zl, h), got(2 - zl)], h)]
            self.far_mid = lambda: [(passed, [of(1 - zl, 0), kept], h)]
            self.own_end = lambda: [
                (low, [of(zl, 0), got(0), got(3)], h),
                (high, [of(zl, h), got(1 + zl), got(4)], h),
            ]

        def start(self):
            @pl.when(c == self.l)
            def _():
                self.own_pair.start()

            @pl.when(c != self.l)
            def _():
                start_all((self.far_pair, *self.far_cross))

        def mid(self):
            @pl.when(c == self.l)
            def _():
                arrived(self.far_cross)
                add_up(self.own_mid(), self.far_off)
                self.own_second.start()

            @pl.when(c != self.l)
            def _():
                arrived([self.far_pair])
                add_up(self.far_mid(), self.far_off)
                self.far_second.start()

        def end(self):
            @pl.when(c == self.l)
            def _():
                arrived((self.own_pair, self.own_second, self.far_second))
                sent([self.own_second])
                add_up(self.own_end(), self.far_off)

        def close(self):
            @pl.when(c == self.l)
            def _():
                sent([self.own_pair])

            @pl.when(c != self.l)
            def _():
                sent((self.far_pair, *self.far_cross, self.far_second))

    class OnOwn:
        def __init__(self, l, phase):
            self.l, self.phase = l, phase

        def start(self):
            pl.when(c == self.l)(self.phase.start)

        def mid(self):
            pl.when(c == self.l)(self.phase.mid)

        def end(self):
            pl.when(c == self.l)(self.phase.end)

        def close(self):
            pl.when(c == self.l)(self.phase.close)

    chain = []
    for l in range(2):
        by_x, by_y = (x, near_x, wrap_x), (y, near_y, wrap_y)
        g = g_out.at[l]
        chain.append(
            (
                (
                    Column(l, g.at[0], r1o, r1f, s1a, s1f, 32, True),
                    OnOwn(l, Ring(*by_x, s1a, r2a, s2a, 8)),
                    OnOwn(l, Ring(*by_y, s2a, r3a, s3.at[0], 2)),
                ),
                (
                    Ring(*by_x, g.at[1], r1x.at[l], s1x.at[l], 16, True),
                    Ring(*by_y, s1x.at[l], r2b.at[l], s2b.at[l], 4),
                    Column(l, s2b.at[l], r3o, r3f, s3.at[1], s3f, 2),
                ),
                (
                    Ring(*by_y, g.at[2], r1y.at[l], s1y.at[l], 16, True),
                    Column(l, s1y.at[l], r2o, r2f, s2c, s2f, 8),
                    OnOwn(l, Ring(*by_x, s2c, r3c, s3.at[2], 2)),
                ),
            )
        )

    def launch(l, part):
        free(part % 2)
        chain[l][part][0].start()

    def units_backward(l):
        for b in range(2):
            DZ[b] = dy(l, b).astype(BF) if l == 1 else DX[1, b]
            for j in range(2):
                cols = slice(j * 768, j * 768 + 768)
                SL[l, b, :, cols] = (dot_back(DZ[b], down_w[l, cols]) * SL[l, b, :, cols].astype(F32)).astype(BF)
            X[0, b] = dot_back(SL[l, b], up_w[l]).astype(BF)
            push(0, b)
        free(0)
        dz = rows(DZ)
        for j in range(2):
            gd = dot_rows(rows(G, l)[:, j * 768 : j * 768 + 768], dz).astype(BF)
            for h in range(2):
                put(0, h * 32 + j * 16, gd[:, h * UC : (h + 1) * UC])
        flush(l, 0)
        if l == 0:
            chain[1][0][0].mid()
        free(1)
        a2 = rows(A2, l)
        for j in range(2):
            du = rows(SL, l)[:, j * 768 : j * 768 + 768]
            gu = dot_rows(a2, du).astype(BF)
            for h in range(2):
                put(1, (2 * j + h) * 16, gu[:, h * UC : (h + 1) * UC])
            SM[0, l, 6 + j : 7 + j] = column_sum(du.astype(F32))
        flush(l, 1)
        launch(l, 0)
        if l == 0:
            chain[1][1][0].mid()
        gain = bias = 0.0
        for b in range(2):
            da2 = both(0, b)
            n2, inv = norm(R[l, b])
            gain += column_sum(da2 * n2)
            bias += column_sum(da2)
            dr = dy(l, b) + norm_back(da2 * pk[l, 2:3], n2, inv)
            DR[b] = dr
            DZ[b] = dr.astype(BF)
        SM[0, l, 2:3] = gain
        SM[0, l, 3:4] = bias
        launch(l, 1)

    def heads_backward(l):
        for b in range(2):
            DO[b] = dot_back(DZ[b], out_w[l]).astype(BF)
            for h in range(6):
                hs = slice(h * HEAD, h * HEAD + HEAD)
                sc = dot_back(K[l, b, :, hs], Q[l, b, :, hs]) * HEAD**-0.5
                p = jnp.exp(sc - LSE[l, b, h : h + 1])
                dp = dot_back(V[l, b, :, hs], DO[b, :, hs])
                pdp = p * dp
                PB[h] = p.astype(BF)
                DS[h] = (pdp - p * jnp.sum(pdp, axis=0, keepdims=True)).astype(BF)
            for h in range(6):
                hs = slice(h * HEAD, h * HEAD + HEAD)
                V[l, b, :, hs] = dot(PB[h], DO[b, :, hs]).astype(BF)
                dk = (dot(DS[h], Q[l, b, :, hs]) * HEAD**-0.5).astype(BF)
                dq = (dot_rows(DS[h], K[l, b, :, hs]) * HEAD**-0.5).astype(BF)
                K[l, b, :, hs] = dk
                Q[l, b, :, hs] = dq
            X[1, b] = (
                dot_back(Q[l, b], qkv_w[l, 0]) + dot_back(K[l, b], qkv_w[l, 1]) + dot_back(V[l, b], qkv_w[l, 2])
            ).astype(BF)
            push(1, b)
        if l == 0:
            chain[1][2][0].mid()
        free(0)
        go = dot_rows(rows(O, l), rows(DZ)).astype(BF)
        for h in range(2):
            put(0, 48 + h * 8, go[:, h * UC : (h + 1) * UC])
        a1 = rows(A1, l)
        for i, d in enumerate((Q, K, V)):
            put(0, i * 16, dot_rows(a1, rows(d, l)).astype(BF))
        flush(l, 2)
        gain = bias = 0.0
        table = [0.0, 0.0]
        for b in range(2):
            da1 = both(1, b)
            n1, inv = norm(S[l, b])
            gain += column_sum(da1 * n1)
            bias += column_sum(da1)
            dx = DR[b] + norm_back(da1 * pk[l, 0:1], n1, inv)
            DX[l, b] = dx.astype(BF)
            total = column_sum(dx)
            for k in range(2):
                table[k] += jnp.where(flag(b) == k, total, 0.0)
        SM[0, l, 0:1] = gain
        SM[0, l, 1:2] = bias
        SM[0, l, 4:5] = table[0]
        SM[0, l, 5:6] = table[1]
        launch(l, 2)

    def share(src, dst, i):
        part = dst.at[pl.ds(2 * t, 2)]
        here = pltpu.make_async_copy(src, part, out_local.at[i])
        here.start()
        there = pltpu.make_async_remote_copy(
            src_ref=src, dst_ref=part, send_sem=out_send.at[i], recv_sem=out_recv.at[i], device_id=far, device_id_type=MESH
        )
        there.start()
        return here, there

    for l in range(2):
        for b in range(2):
            heads_forward(l, b)
        if l == 0:
            pl.when(c == 0)(hand_on)
        for b in range(2):
            units_forward(l, b)
    for b in range(2):
        LO[1, b] = (R[1, b] + both(1, b)).astype(BF)
    finish = list(share(LO.at[c], lo4, 0))
    cot_load.wait()
    for l in (1, 0):
        units_backward(l)
        heads_backward(l)
    finish += share(DX.at[c], dx4, 1)

    small_steps = []

    def small_step(k, peer, both_layers=True):
        src = SM.at[k] if both_layers else SM.at[k, pl.ds(1 - c, 1)]
        dst = SMR.at[k] if both_layers else SMR.at[k, pl.ds(1 - c, 1)]
        cp = move(src, dst, peer)

        def begin():
            cp.start()

        def finish_step():
            cp.wait_recv()
            if both_layers:
                SM[k + 1] = SM[k] + SMR[k]
            else:
                small_out[...] = SM[k, pl.ds(c, 1)][0] + SMR[k, pl.ds(c, 1)][0]

        small_steps.append((begin, finish_step))

    small_from = len(moves)
    for k, peer in enumerate((near_x, wrap_x, near_y, wrap_y, pair)):
        small_step(k, peer)
    small_step(5, cross, False)

    def small_next(k):
        if k:
            small_steps[k - 1][1]()
        if k < 6:
            small_steps[k][0]()

    def advance(l, part, phase):
        chain[l][part][phase].end()
        if phase < 2:
            chain[l][part][phase + 1].start()

    small_next(0)
    advance(1, 0, 0)
    advance(1, 1, 0)
    small_next(1)
    chain[0][0][0].mid()
    chain[0][1][0].mid()
    advance(1, 2, 0)
    small_next(2)
    for part in range(3):
        chain[1][part][1].mid()
    chain[0][2][0].mid()
    small_next(3)
    advance(0, 0, 0)
    advance(0, 1, 0)
    for part in range(3):
        advance(1, part, 1)
    small_next(4)
    advance(0, 2, 0)
    for part in range(3):
        chain[1][part][2].mid()
    for part in range(3):
        chain[0][part][1].mid()
    small_next(5)
    for part in range(3):
        advance(1, part, 2)
    for part in range(3):
        advance(0, part, 1)
    small_next(6)
    for part in range(3):
        chain[0][part][2].mid()
    for part in range(3):
        advance(0, part, 2)

    def unit(p, start, count):
        return full[p].at[pl.ds(start, count)]

    class Spread:
        def __init__(self, p, base, n, i, near_dev, wrap_dev):
            h = n // 2
            near, other = flip(i), 3 - i
            piece = lambda k, lo: unit(p, base + k * n + lo, h)
            self.first = [move(piece(i, 0), piece(i, 0), wrap_dev), move(piece(i, h), piece(i, h), near_dev)]
            self.second = [
                move(piece(i, 0), piece(i, 0), near_dev),
                move(piece(i, h), piece(i, h), wrap_dev),
                move(piece(other, 0), piece(other, 0), near_dev),
                move(piece(near, h), piece(near, h), wrap_dev),
            ]

        def start(self):
            start_all(self.first)
            start_all(self.second[:2])

        def mid(self):
            arrived(self.first)
            start_all(self.second[2:])

        def end(self):
            arrived(self.second)

        def close(self):
            sent(self.first)
            sent(self.second)

    class Trade:
        def __init__(self, p, base, n):
            part = unit(p, base + zl * n, n)
            self.copy = move(part, part, pair)

        def start(self):
            self.copy.start()

        def mid(self):
            pass

        def end(self):
            arrived([self.copy])

        def close(self):
            sent([self.copy])

    spread_x, spread_y = (x, near_x, wrap_x), (y, near_y, wrap_y)
    gathers = (
        (Spread(0, zl * 32 + x * 8, 2, *spread_y), Spread(0, zl * 32, 8, *spread_x), Trade(0, 0, 32)),
        (Trade(1, x * 16 + y * 4, 2), Spread(1, x * 16, 4, *spread_y), Spread(1, 0, 16, *spread_x)),
        (Spread(2, y * 16 + zl * 8, 2, *spread_x), Trade(2, y * 16, 8), Spread(2, 0, 16, *spread_y)),
    )
    number = (zl * 32 + x * 8 + y * 2, x * 16 + y * 4 + zl * 2, y * 16 + zl * 8 + x * 2)
    kept = []
    for p in range(3):
        cp = pltpu.make_async_copy(s3.at[p], unit(p, number[p], 2), keep_sem.at[p])
        cp.start()
        kept.append(cp)
    for p in range(3):
        kept[p].wait()
        gathers[p][0].start()
    for step in range(3):
        for p in range(3):
            gathers[p][step].mid()
        for p in range(3):
            gathers[p][step].end()
            if step < 2:
                gathers[p][step + 1].start()

    for cp in finish:
        cp.wait()
    sent(moves[:w_count])
    for l in range(2):
        for part in range(3):
            for phase in range(3):
                chain[l][part][phase].close()
    for steps in gathers:
        for step in steps:
            step.close()
    sent(moves[small_from : small_from + 6])


def run_layers(species, emb, cot, pk_own, own_w):
    anywhere = pl.BlockSpec(memory_space=pl.ANY)
    dma = pltpu.SemaphoreType.DMA
    vm = lambda *shape: pltpu.VMEM(shape, BF)
    vf = lambda *shape: pltpu.VMEM(shape, F32)
    cells = (2, 256, 768)
    units = lambda *shape: pltpu.VMEM((*shape, UR, UC), BF)
    scratch = [
        vm(2, 3, 768, 384),
        vm(2, 384, 768),
        vm(2, 768, 1536),
        vm(2, 1536, 768),
        vf(2, 8, 768),
        vf(2, *cells),
        vm(2, *cells),
        vm(2, 2, 256, 384),
        vm(2, 2, 256, 384),
        vm(2, 2, 256, 384),
        vf(2, 2, 8, 256),
        vm(2, 2, 256, 384),
        vf(2, *cells),
        vm(2, *cells),
        vm(2, 2, 256, 1536),
        vm(2, 2, 256, 1536),
        vm(2, *cells),
        vm(2, *cells),
        vf(*cells),
        vm(*cells),
        vm(2, 256, 384),
        vm(6, 256, 256),
        vm(6, 256, 256),
        vm(2, *cells),
        vm(2, *cells),
        units(2, 64),
        units(96),
        vf(6, 2, 8, 768),
        vf(6, 2, 8, 768),
        units(32),
        units(16),
        units(2, 16),
        units(2, 16),
        units(8),
        units(2, 4),
        units(8),
        units(4),
        units(3, 2),
        units(1),
        units(24),
        units(2, 12),
        units(20),
        units(4),
        units(6),
        units(5),
        units(1),
        units(6),
        dma((7,)),
        dma((2, 2)),
        dma((2, 2)),
        dma((2,)),
        dma((2,)),
        dma((2,)),
        dma((2,)),
        dma((MOVES,)),
        dma((MOVES,)),
        dma((6,)),
        dma((3,)),
    ]
    hbm = lambda *shape: jax.ShapeDtypeStruct((*shape, UR, UC), BF)
    return pl.pallas_call(
        layers_kernel,
        out_shape=(
            jax.ShapeDtypeStruct((4, 256, 768), BF),
            jax.ShapeDtypeStruct((4, 256, 768), BF),
            hbm(2, 3, 64),
            hbm(80),
            hbm(16),
            hbm(2, 48),
            hbm(2, 48),
            hbm(64),
            hbm(64),
            hbm(64),
            jax.ShapeDtypeStruct((8, 768), F32),
        ),
        in_specs=[pl.BlockSpec(memory_space=pltpu.SMEM)] + [anywhere] * 7,
        out_specs=(*[anywhere] * 10, pl.BlockSpec(memory_space=pltpu.VMEM)),
        scratch_shapes=scratch,
        compiler_params=pltpu.CompilerParams(collective_id=1, has_side_effects=True, vmem_limit_bytes=63 * 2**20),
        name="layers",
    )(species, emb, cot, pk_own, *own_w)


def widen_kernel(down, up, heads, down_out, up_out, qkv_out, out_out):
    for h in range(2):
        down_out[:, h * UC : (h + 1) * UC] = down[h].astype(F32)
    for h in range(4):
        up_out[:, h * UC : (h + 1) * UC] = up[h].astype(F32)
    qkv_out[...] = heads[:3].astype(F32)
    out_out[...] = heads[3].astype(F32)


def widen(down, up, heads):
    return pl.pallas_call(
        widen_kernel,
        grid=(8,),
        in_specs=[
            pl.BlockSpec((2, 192, UC), lambda i: (0, i, 0)),
            pl.BlockSpec((4, 96, UC), lambda i: (0, i, 0)),
            pl.BlockSpec((4, 96, UC), lambda i: (0, i, 0)),
        ],
        out_specs=[
            pl.BlockSpec((192, 768), lambda i: (i, 0)),
            pl.BlockSpec((96, 1536), lambda i: (i, 0)),
            pl.BlockSpec((3, 96, UC), lambda i: (0, i, 0)),
            pl.BlockSpec((96, UC), lambda i: (lax.rem(i, 4), i // 4)),
        ],
        out_shape=[
            jax.ShapeDtypeStruct((1536, 768), F32),
            jax.ShapeDtypeStruct((768, 1536), F32),
            jax.ShapeDtypeStruct((3, 768, UC), F32),
            jax.ShapeDtypeStruct((384, 768), F32),
        ],
        name="widen",
    )(down.reshape(2, 1536, UC), up.reshape(4, 768, UC), heads.reshape(4, 768, UC))


def shards(
    embeddings,
    species,
    ln1_gain,
    ln1_bias,
    qkv_weight,
    out_weight,
    ln2_gain,
    ln2_bias,
    up_weight,
    up_bias,
    down_weight,
    species_bias,
    out_cotangent,
):
    own_w = (qkv_weight[0].transpose(1, 0, 2), out_weight[0], up_weight[0], down_weight[0])
    pk = jnp.concatenate([ln1_gain, ln1_bias, ln2_gain, ln2_bias, species_bias[0], up_bias.reshape(2, 768)])
    results = run_layers(species, embeddings, out_cotangent, pk, own_w)
    lo4, dx4 = results[:2]
    down, up, heads, small = results[7:]
    grad_down, grad_up, grad_qkv, grad_out = widen(down, up, heads)
    return (
        lo4.astype(F32)[None],
        dx4.astype(F32)[None],
        small[0:1],
        small[1:2],
        grad_qkv.transpose(1, 0, 2)[None],
        grad_out[None],
        small[2:3],
        small[3:4],
        grad_up[None],
        small[6:8].reshape(1, 1536),
        grad_down[None],
        small[4:6][None],
    )


def solution(mesh):
    placed = (
        P("dp", None, None),
        P("dp"),
        P("section", None),
        P("section", None),
        P("section", None, None, "tensor"),
        P("section", "tensor", None),
        P("section", None),
        P("section", None),
        P("section", None, "tensor"),
        P("section", "tensor"),
        P("section", "tensor", None),
        P("section", None, None),
        P("dp", None, None),
    )
    return jax.shard_map(
        shards,
        mesh=mesh,
        in_specs=placed,
        out_specs=(
            P("section", "dp", None, None),
            P("section", "dp", None, None),
            P("section", None),
            P("section", None),
            P("section", None, None, "tensor"),
            P("section", "tensor", None),
            P("section", None),
            P("section", None),
            P("section", None, "tensor"),
            P("section", "tensor"),
            P("section", "tensor", None),
            P("section", None, None),
        ),
        check_vma=False,
    )
```

```python
import functools

import jax
import jax.numpy as jnp
from jax import lax
from jax.experimental import pallas as pl
from jax.experimental.pallas import tpu as pltpu
from jax.sharding import PartitionSpec as P

HEAD = 64
MOVES = 256
UR, UC = 48, 384
MESH = pl.DeviceIdType.MESH
BF = jnp.bfloat16
F32 = jnp.float32

epsilon = 1e-05
root_half = 0.7071067811865476
density_scale = 0.3989422804014327


def place():
    dp = lax.axis_index("dp")
    z = lax.axis_index("tensor") * 2 + lax.rem(dp, 2)
    return dp // 8, lax.rem(dp // 2, 4), z, lax.axis_index("section")


def device(x, y, z, core):
    return (core, (x * 4 + y) * 2 + lax.rem(z, 2), z // 2)


def flip(v):
    return v + 1 - 2 * lax.rem(v, 2)


def wrap(v):
    return lax.rem(v, 4)


def norm(values):
    center = values - jnp.mean(values, axis=-1, keepdims=True)
    inverse = lax.rsqrt(jnp.mean(center * center, axis=-1, keepdims=True) + epsilon)
    return (center * inverse, inverse)


def norm_back(grad_normed, normed, inverse):
    return inverse * (
        grad_normed
        - jnp.mean(grad_normed, axis=-1, keepdims=True)
        - normed * jnp.mean(grad_normed * normed, axis=-1, keepdims=True)
    )


def dot(a, b):
    return jnp.dot(a, b, preferred_element_type=F32)


def dot_rows(a, b):
    return lax.dot_general(a, b, (((0,), (0,)), ((), ())), preferred_element_type=F32)


def dot_back(a, b):
    return lax.dot_general(a, b, (((1,), (1,)), ((), ())), preferred_element_type=F32)


def column_sum(a):
    return jnp.sum(a, axis=0, keepdims=True)


def split_refs(refs, counts):
    out, at = [], 0
    for n in counts:
        out.append(refs[at : at + n])
        at += n
    return out


def layers_kernel(
    species, emb, cot, *refs
):
    own_p, own_w = refs[:6], refs[6:10]
    lo4, dx4, g_out, r1, full_x, full_y, small_out = refs[10:17]
    (
        (qkv_w, out_w, up_w, down_w, pk),
        (S, A1, Q, K, V, LSE, O, R, A2, G, SL, LO, DX, DR, DZ, DO, PB, DS, X, Y),
        (GS, PAD, SM, SMR, s1, s2, s2f, s3, r2, r2f, r3),
        (load_sem, x_send, x_recv, out_local, out_send, out_recv, g_sem, w_send, w_recv, pull_sem, keep_sem),
    ) = split_refs(refs[17:], (5, 20, 11, 11))
    x, y, z, c = place()
    t = z // 2
    zl = lax.rem(z, 2)
    sibling = device(x, y, z, 1 - c)
    far = device(x, y, lax.rem(z + 2, 4), c)
    cross = device(x, y, 3 - z, 1 - c)
    pair = device(x, y, 2 * t + 1 - zl, c)
    along_x = [device(wrap(x + k), y, z, c) for k in (1, 2, 3)]
    along_y = [device(x, wrap(y + k), z, c) for k in (1, 2, 3)]
    barrier = pltpu.get_barrier_semaphore()
    for p in (sibling, far, cross, pair, *along_x, *along_y):
        pl.semaphore_signal(barrier, inc=1, device_id=p, device_id_type=MESH)
    weights = (qkv_w, out_w, up_w, down_w)

    def load(src, dst, i):
        cp = pltpu.make_async_copy(src, dst, load_sem.at[i])
        cp.start()
        return cp

    w_loads = [load(own_w[i], w.at[c], i) for i, w in enumerate(weights)]
    start = [load(emb.at[pl.ds(2 * t, 2)], DZ, 4)]
    p_loads = [load(own_p[i], pk.at[c, i], 7 + i) for i in range(4)]
    for i in range(2):
        p_loads.append(load(own_p[4].at[:, pl.ds(i * 768, 768)], pk.at[c, 6 + i], 11 + i))
        p_loads.append(load(own_p[5].at[:, i], pk.at[c, 4 + i], 13 + i))
    cot_load = load(cot.at[pl.ds(2 * t, 2)], DR, 6)
    pl.semaphore_wait(barrier, 10)
    near_x, wrap_x = device(flip(x), y, z, c), device(3 - x, y, z, c)
    near_y, wrap_y = device(x, flip(y), z, c), device(x, 3 - y, z, c)

    moves = []

    def move(src, dst, peer):
        i = len(moves)
        cp = pltpu.make_async_remote_copy(
            src_ref=src, dst_ref=dst, send_sem=w_send.at[i], recv_sem=w_recv.at[i], device_id=peer, device_id_type=MESH
        )
        moves.append(cp)
        return cp

    def start_all(copies):
        for cp in copies:
            cp.start()

    def arrived(copies):
        for cp in copies:
            cp.wait_recv()

    def sent(copies):
        for cp in copies:
            cp.wait_send()

    pk_move = move(pk.at[c], pk.at[c], cross)
    up_hop = move(own_w[2].at[pl.ds(x * 192 + y * 48, 48)], up_w.at[c, pl.ds(x * 192 + y * 48, 48)], cross)
    down_hop = move(own_w[3].at[pl.ds(y * 384 + x * 96, 96)], down_w.at[c, pl.ds(y * 384 + x * 96, 96)], cross)
    pl.when(c == 0)(lambda: start_all((up_hop, down_hop)))
    for cp in p_loads:
        cp.wait()
    pk_move.start()
    direct = [
        move(own_w[0].at[i, pl.ds((1 - zl) * 384, 384)], qkv_w.at[c, i, pl.ds((1 - zl) * 384, 384)], cross) for i in range(3)
    ]
    direct.append(move(own_w[1].at[pl.ds((1 - zl) * 192, 192)], out_w.at[c, pl.ds((1 - zl) * 192, 192)], cross))
    pl.when(c == 0)(lambda: start_all(direct))

    def onward(ref, rows, count, peers):
        part = ref.at[1 - c, pl.ds(rows, count)]
        return [move(part, part, p) for p in peers]

    up_y = onward(up_w, x * 192 + y * 48, 48, along_y)
    down_x = onward(down_w, y * 384 + x * 96, 96, along_x)
    up_x = onward(up_w, x * 192, 192, along_x)
    down_y = onward(down_w, y * 384, 384, along_y)
    trade = []
    for i in range(3):
        part = qkv_w.at[1 - c, i, pl.ds(zl * 384, 384)]
        trade.append(move(part, part, pair))
    part = out_w.at[1 - c, pl.ds(zl * 192, 192)]
    trade.append(move(part, part, pair))

    w_count = len(moves)

    def gather_hops():
        arrived([up_hop])
        start_all(up_y)
        arrived([down_hop])
        start_all(down_x)

    def gather_rest():
        arrived(up_y)
        start_all(up_x)
        arrived(down_x)
        start_all(down_y)

    def hand_on(*which):
        for i in which:
            arrived([direct[i]])
            trade[i].start()

    @pl.when(c == 1)
    def _():
        gather_hops()
        hand_on(0)
        gather_rest()
        hand_on(1, 2)
        start_all((up_hop, down_hop))
        start_all(direct)
        hand_on(3)

    arrived([pk_move])
    for cp in start:
        cp.wait()

    def need(l, i):
        incoming = ([*trade[:3]], [trade[3]], up_x, down_y)[i]
        if l == 0:
            w_loads[i].wait()
        pl.when(c == 1 - l)(lambda: arrived(incoming))

    flying = {}

    def push(kind, b):
        cp = pltpu.make_async_remote_copy(
            src_ref=X.at[kind, b],
            dst_ref=Y.at[kind, b],
            send_sem=x_send.at[kind, b],
            recv_sem=x_recv.at[kind, b],
            device_id=sibling,
            device_id_type=MESH,
        )
        cp.start()
        flying[kind, b] = cp

    def both(kind, b):
        flying.pop((kind, b)).wait()
        return X[kind, b].astype(F32) + Y[kind, b].astype(F32)

    def flag(b):
        return species[2 * t + b]

    def heads_forward(l, b):
        if l == 0:
            xin = DZ[b].astype(F32)
        else:
            low = (R[0, b] + both(1, b)).astype(BF)
            LO[0, b] = low
            xin = low.astype(F32)
        s = xin + jnp.where(flag(b) == 0, pk[l, 4], pk[l, 5])
        S[l, b] = s
        n1, _ = norm(s)
        a1 = (n1 * pk[l, 0] + pk[l, 1]).astype(BF)
        A1[l, b] = a1
        if b == 0:
            need(l, 0)
        for i, part in enumerate((Q, K, V)):
            part[l, b] = dot(a1, qkv_w[l, i]).astype(BF)
        for h in range(6):
            hs = slice(h * HEAD, h * HEAD + HEAD)
            sc = dot_back(K[l, b, :, hs], Q[l, b, :, hs]) * HEAD**-0.5
            top = jnp.max(sc, axis=0, keepdims=True)
            e = jnp.exp(sc - top)
            total = jnp.sum(e, axis=0, keepdims=True)
            PB[h] = (e * (1.0 / total)).astype(BF)
            LSE[l, b, h : h + 1] = top + jnp.log(total)
        for h in range(6):
            hs = slice(h * HEAD, h * HEAD + HEAD)
            O[l, b, :, hs] = dot_rows(PB[h], V[l, b, :, hs]).astype(BF)
        if b == 0:
            need(l, 1)
        X[0, b] = dot(O[l, b], out_w[l]).astype(BF)
        push(0, b)

    def units_forward(l, b):
        r = S[l, b] + both(0, b)
        R[l, b] = r
        n2, _ = norm(r)
        a2 = (n2 * pk[l, 2] + pk[l, 3]).astype(BF)
        A2[l, b] = a2
        if b == 0:
            need(l, 2)
        for j in range(2):
            cols = slice(j * 768, j * 768 + 768)
            u = dot(a2, up_w[l, :, cols]) + pk[l, 6 + j]
            cdf = 0.5 * (1.0 + lax.erf(u * root_half))
            G[l, b, :, cols] = (u * cdf).astype(BF)
            SL[l, b, :, cols] = (cdf + u * density_scale * jnp.exp(-0.5 * u * u)).astype(BF)
        if b == 0:
            need(l, 3)
        X[1, b] = dot(G[l, b], down_w[l]).astype(BF)
        push(1, b)

    def rows(ref, *lead):
        a = ref[lead] if lead else ref[...]
        return a.reshape(512, a.shape[-1])

    def put(slot, half, value, numbers):
        for i, number in enumerate(numbers):
            GS[slot, half, number] = value[i * UR : (i + 1) * UR]

    g_copies = {}

    def flush(l, m):
        cp = pltpu.make_async_copy(GS.at[m % 2], g_out.at[l, m], g_sem.at[m % 2])
        cp.start()
        g_copies[m % 2] = cp

    def free(slot):
        if slot in g_copies:
            g_copies.pop(slot).wait()

    def dy(l, b):
        return DR[b] if l == 1 else DX[1, b].astype(F32)

    def share(i, l):
        src, dst = ((LO, lo4), (DX, dx4))[i]
        part = dst.at[pl.ds(2 * t, 2)]
        here = pltpu.make_async_copy(src.at[l], part, out_local.at[i])
        there = pltpu.make_async_remote_copy(
            src_ref=src.at[l], dst_ref=part, send_sem=out_send.at[i], recv_sem=out_recv.at[i], device_id=far, device_id_type=MESH
        )
        return here, there

    def share_own(i, l):
        pl.when(c == l)(lambda: start_all(share(i, l)))


    def add_up(jobs, stored=False):
        if stored:
            pulls = []
            for dst, pieces in jobs:
                for i, piece in enumerate(pieces):
                    k = len(pulls)
                    cp = pltpu.make_async_copy(piece, PAD.at[k], pull_sem.at[k])
                    cp.start()
                    pulls.append(cp)
                    pieces[i] = PAD.at[k]
            for cp in pulls:
                cp.wait()
        for dst, pieces in jobs:
            total = pieces[0][...].astype(F32)
            for piece in pieces[1:]:
                total += piece[...].astype(F32)
            dst[...] = total.astype(BF)

    class Ring:
        def __init__(self, i, near_dev, wrap_dev, low_of, high_of, got, low, high):
            near, other, opposite = flip(i), 3 - i, 3 - flip(i)
            self.first = [
                move(low_of(near), got(0), near_dev),
                move(high_of(other), got(2), wrap_dev),
                move(low_of(opposite), got(1), near_dev),
                move(high_of(opposite), got(3), wrap_dev),
            ]
            self.second = [move(low, got(4), wrap_dev), move(high, got(5), near_dev)]
            self.mid_jobs = lambda: [(low, [low_of(other), got(1)]), (high, [high_of(near), got(3)])]
            self.end_jobs = lambda: [(low, [low_of(i), got(0), got(4)]), (high, [high_of(i), got(2), got(5)])]

        def start(self):
            start_all(self.first[2:])
            start_all(self.first[:2])

        def mid_wait(self):
            arrived(self.first[2:])

        def end_wait(self):
            arrived(self.first[:2])
            arrived(self.second)
            sent(self.second)

        def close(self):
            sent(self.first)

    class Column:
        def __init__(self, l, of, got, kept, out, passed):
            self.l = l
            low, high = out.at[pl.ds(0, 2)], out.at[pl.ds(2, 2)]
            self.own_pair = move(of(1 - zl, 0), got(0), pair)
            self.far_pair = move(of(zl, 0), kept, pair)
            self.far_cross = [move(of(0, 1), got(1), cross), move(of(1, 1), got(2), cross)]
            self.own_second = move(high, got(4), pair)
            self.far_second = move(passed, got(3), cross)
            self.own_mid = lambda: [(high, [of(1 - zl, 1), got(2 - zl)])]
            self.far_mid = lambda: [(passed, [of(1 - zl, 0), kept])]
            self.own_end = lambda: [(low, [of(zl, 0), got(0), got(3)]), (high, [of(zl, 1), got(1 + zl), got(4)])]

        def start(self):
            @pl.when(c == self.l)
            def _():
                self.own_pair.start()

            @pl.when(c != self.l)
            def _():
                start_all((self.far_pair, *self.far_cross))

        def mid(self):
            @pl.when(c == self.l)
            def _():
                arrived(self.far_cross)
                add_up(self.own_mid())
                self.own_second.start()

            @pl.when(c != self.l)
            def _():
                arrived([self.far_pair])
                add_up(self.far_mid())
                self.far_second.start()

        def end(self):
            arrived((self.own_pair, self.own_second, self.far_second))
            sent([self.own_second])
            add_up(self.own_end())

        def close(self):
            @pl.when(c == self.l)
            def _():
                sent([self.own_pair])

            @pl.when(c != self.l)
            def _():
                sent((self.far_pair, *self.far_cross, self.far_second))

    by_x, by_y = (x, near_x, wrap_x), (y, near_y, wrap_y)

    pairs = [(m, a) for m in range(3) for a in range(2)]

    def matrix_ring(l, m, a):
        g, got, out = g_out.at[l, m, a], r1.at[l, m, a], s1.at[l, m, a]
        return Ring(
            *(by_x, by_y)[a],
            lambda k: g.at[pl.ds(k * 8, 4)],
            lambda k: g.at[pl.ds(k * 8 + 4, 4)],
            lambda j: got.at[j],
            out.at[0],
            out.at[1],
        )

    def z_column(l, m, a):
        return Column(
            l,
            lambda k, half: s1.at[l, m, a, k, pl.ds(half * 2, 2)],
            lambda j: r2.at[m, a, j],
            r2f.at[m, a],
            s2.at[m, a],
            s2f.at[m, a],
        )

    first = [[[matrix_ring(l, m, a) for a in range(2)] for m in range(3)] for l in range(2)]
    column = [[[z_column(l, m, a) for a in range(2)] for m in range(3)] for l in range(2)]


    class Spread:
        def __init__(self, full, n, i, near_dev, wrap_dev):
            h = n // 2
            near, other = flip(i), 3 - i
            low = lambda k: full.at[pl.ds(k * n, h)]
            high = lambda k: full.at[pl.ds(k * n + h, h)]
            self.first = [move(low(i), low(i), wrap_dev), move(high(i), high(i), near_dev)]
            self.second = [
                move(low(i), low(i), near_dev),
                move(high(i), high(i), wrap_dev),
                move(low(other), low(other), near_dev),
                move(high(near), high(near), wrap_dev),
            ]

        def start(self):
            start_all(self.first)
            start_all(self.second[:2])

        def mid(self):
            arrived(self.first)
            start_all(self.second[2:])

    class Tail:
        def __init__(self, m, a):
            i, j = ((x, y), (y, x))[a]
            peers = (along_y, along_x)[a]
            whole = (full_x, full_y)[a].at[m]
            number = i * 8 + zl * 4 + j
            own = whole.at[pl.ds(number, 1)]
            out = s3.at[m, a]
            self.sums = [move(s2.at[m, a, pl.ds(wrap(j + k), 1)], r3.at[m, a, k - 1], peers[k - 1]) for k in (1, 2, 3)]
            self.job = (out, [s2.at[m, a, pl.ds(j, 1)]] + [r3.at[m, a, k] for k in range(3)])
            self.keep = pltpu.make_async_copy(out, own, keep_sem.at[m, a])
            self.near = [move(out, own, p) for p in peers]
            group = whole.at[pl.ds(i * 8 + zl * 4, 4)]
            self.trade = move(group, group, pair)
            self.ring = Spread(whole, 8, *(by_x, by_y)[a])

    tail = [[Tail(m, a) for a in range(2)] for m in range(3)]

    def on_core(l):
        return pl.when(c == l)

    def launch(l, m):
        free(m % 2)
        for ring in first[l][m]:
            ring.start()

    def sum1_mid(l, m):
        for ring in first[l][m]:
            ring.mid_wait()
        add_up([job for ring in first[l][m] for job in ring.mid_jobs()], True)
        for ring in first[l][m]:
            start_all(ring.second)

    def sum1_end(l, m):
        for ring in first[l][m]:
            ring.end_wait()
        add_up([job for ring in first[l][m] for job in ring.end_jobs()], True)
        for col in column[l][m]:
            col.start()

    def sum2_mid(l, m):
        for col in column[l][m]:
            col.mid()

    def sum2_end(l, m):
        @on_core(l)
        def _():
            for col, tl in zip(column[l][m], tail[m]):
                col.end()
                start_all(tl.sums)

    def sum3(l, m):
        @on_core(l)
        def _():
            for tl in tail[m]:
                arrived(tl.sums)
                add_up([tl.job])
                tl.keep.start()
                start_all(tl.near)

    def back1(l, m):
        @on_core(l)
        def _():
            for tl in tail[m]:
                arrived(tl.near)
                tl.keep.wait()
                tl.trade.start()

    def back2(l, m):
        @on_core(l)
        def _():
            for tl in tail[m]:
                arrived([tl.trade])
                tl.ring.start()

    def back3(l, m):
        @on_core(l)
        def _():
            for tl in tail[m]:
                tl.ring.mid()

    beside = {
        (1, "grads_up"): [(launch, 1, 0)],
        (1, "units"): [(launch, 1, 1)],
        (1, "cell1"): [(sum1_mid, 1, 0)],
        (1, "heads"): [(launch, 1, 2), (share_own, 1, 1)],
        (0, "pushed"): [(sum1_mid, 1, 1)],
        (0, "grads_down"): [(sum1_end, 1, 0)],
        (0, "grads_up"): [(launch, 0, 0)],
        (0, "units"): [(launch, 0, 1)],
        (0, "cell0"): [(sum1_mid, 1, 2), (sum1_end, 1, 1), (sum2_mid, 1, 0)],
        (0, "cell1"): [(sum1_mid, 0, 0)],
        (0, "heads"): [(launch, 0, 2), (share_own, 1, 0)],
    }

    def meanwhile(l, point):
        for f, *args in beside.get((l, point), ()):
            f(*args)

    def units_backward(l):
        for b in range(2):
            DZ[b] = dy(l, b).astype(BF) if l == 1 else DX[1, b]
            for j in range(2):
                cols = slice(j * 768, j * 768 + 768)
                SL[l, b, :, cols] = (dot_back(DZ[b], down_w[l, cols]) * SL[l, b, :, cols].astype(F32)).astype(BF)
            X[0, b] = dot_back(SL[l, b], up_w[l]).astype(BF)
            push(0, b)
        meanwhile(l, "pushed")
        free(0)
        dz = rows(DZ)
        for j in range(2):
            gd = dot_rows(rows(G, l)[:, j * 768 : j * 768 + 768], dz).astype(BF)
            for h in range(2):
                put(0, h, gd[:, h * UC : (h + 1) * UC], range(j * 16, j * 16 + 16))
        flush(l, 0)
        meanwhile(l, "grads_down")
        free(1)
        a2 = rows(A2, l)
        for j in range(2):
            du = rows(SL, l)[:, j * 768 : j * 768 + 768]
            gu = dot_rows(a2, du).astype(BF)
            for h in range(2):
                put(1, j, gu[:, h * UC : (h + 1) * UC], range(h, 32, 2))
            SM[0, l, 6 + j : 7 + j] = column_sum(du.astype(F32))
        flush(l, 1)
        meanwhile(l, "grads_up")
        gain = bias = 0.0
        for b in range(2):
            da2 = both(0, b)
            n2, inv = norm(R[l, b])
            gain += column_sum(da2 * n2)
            bias += column_sum(da2)
            dr = dy(l, b) + norm_back(da2 * pk[l, 2], n2, inv)
            DR[b] = dr
            DZ[b] = dr.astype(BF)
        SM[0, l, 2:3] = gain
        SM[0, l, 3:4] = bias
        meanwhile(l, "units")

    def heads_backward(l):
        for b in range(2):
            DO[b] = dot_back(DZ[b], out_w[l]).astype(BF)
            for h in range(6):
                hs = slice(h * HEAD, h * HEAD + HEAD)
                sc = dot_back(K[l, b, :, hs], Q[l, b, :, hs]) * HEAD**-0.5
                p = jnp.exp(sc - LSE[l, b, h : h + 1])
                dp = dot_back(V[l, b, :, hs], DO[b, :, hs])
                pdp = p * dp
                PB[h] = p.astype(BF)
                DS[h] = (pdp - p * jnp.sum(pdp, axis=0, keepdims=True)).astype(BF)
            for h in range(6):
                hs = slice(h * HEAD, h * HEAD + HEAD)
                V[l, b, :, hs] = dot(PB[h], DO[b, :, hs]).astype(BF)
                dk = (dot(DS[h], Q[l, b, :, hs]) * HEAD**-0.5).astype(BF)
                dq = (dot_rows(DS[h], K[l, b, :, hs]) * HEAD**-0.5).astype(BF)
                K[l, b, :, hs] = dk
                Q[l, b, :, hs] = dq
            X[1, b] = (
                dot_back(Q[l, b], qkv_w[l, 0]) + dot_back(K[l, b], qkv_w[l, 1]) + dot_back(V[l, b], qkv_w[l, 2])
            ).astype(BF)
            push(1, b)
            meanwhile(l, f"cell{b}")
        free(0)
        go = dot_rows(rows(O, l), rows(DZ)).astype(BF)
        for h in range(2):
            put(0, 1, go[:, h * UC : (h + 1) * UC], range(2 + h, 32, 4))
        a1 = rows(A1, l)
        for i, d in enumerate((Q, K, V)):
            put(0, i // 2, dot_rows(a1, rows(d, l)).astype(BF), [4 * (r // 2) + r % 2 + (2 if i == 1 else 0) for r in range(16)])
        flush(l, 2)
        gain = bias = 0.0
        table = [0.0, 0.0]
        for b in range(2):
            da1 = both(1, b)
            n1, inv = norm(S[l, b])
            gain += column_sum(da1 * n1)
            bias += column_sum(da1)
            dx = DR[b] + norm_back(da1 * pk[l, 0], n1, inv)
            DX[l, b] = dx.astype(BF)
            total = column_sum(dx)
            for k in range(2):
                table[k] += jnp.where(flag(b) == k, total, 0.0)
        SM[0, l, 0:1] = gain
        SM[0, l, 1:2] = bias
        SM[0, l, 4:5] = table[0]
        SM[0, l, 5:6] = table[1]
        meanwhile(l, "heads")

    for l in range(2):
        for b in range(2):
            heads_forward(l, b)
        if l == 0:
            pl.when(c == 0)(gather_hops)
        else:
            share_own(0, 0)
        units_forward(l, 0)
        if l == 0:
            pl.when(c == 0)(gather_rest)
        units_forward(l, 1)
        if l == 0:
            pl.when(c == 0)(lambda: hand_on(0, 1, 2, 3))
    for b in range(2):
        LO[1, b] = (R[1, b] + both(1, b)).astype(BF)
    share_own(0, 1)
    cot_load.wait()
    for l in (1, 0):
        units_backward(l)
        heads_backward(l)

    small_steps = []

    def small_step(k, peer, both_layers=True):
        src = SM.at[k] if both_layers else SM.at[k, pl.ds(1 - c, 1)]
        dst = SMR.at[k] if both_layers else SMR.at[k, pl.ds(1 - c, 1)]
        cp = move(src, dst, peer)

        def begin():
            cp.start()

        def finish_step():
            cp.wait_recv()
            if both_layers:
                SM[k + 1] = SM[k] + SMR[k]
            else:
                small_out[...] = SM[k, pl.ds(c, 1)][0] + SMR[k, pl.ds(c, 1)][0]

        small_steps.append((begin, finish_step))

    small_from = len(moves)
    for k, peer in enumerate((near_x, wrap_x, near_y, wrap_y, pair)):
        small_step(k, peer)
    small_step(5, cross, False)

    def small_next(k):
        if k:
            small_steps[k - 1][1]()
        if k < 6:
            small_steps[k][0]()

    small_next(0)
    sum2_end(1, 0)
    sum2_mid(1, 1)
    sum1_end(1, 2)
    sum1_mid(0, 1)
    sum3(1, 0)
    sum2_end(1, 1)
    small_next(1)
    sum1_end(0, 0)
    sum2_mid(1, 2)
    sum1_mid(0, 2)
    sum3(1, 1)
    back1(1, 0)
    small_next(2)
    sum2_mid(0, 0)
    sum2_end(1, 2)
    sum1_end(0, 1)
    back1(1, 1)
    sum3(1, 2)
    small_next(3)
    sum2_end(0, 0)
    sum2_mid(0, 1)
    sum1_end(0, 2)
    back1(1, 2)
    back2(1, 0)
    sum3(0, 0)
    small_next(4)
    back2(1, 1)
    sum2_end(0, 1)
    back1(0, 0)
    sum2_mid(0, 2)
    back2(1, 2)
    sum3(0, 1)
    back3(1, 0)
    small_next(5)
    back2(0, 0)
    sum2_end(0, 2)
    back1(0, 1)
    back3(1, 1)
    sum3(0, 2)
    small_next(6)
    back2(0, 1)
    back3(1, 2)
    back3(0, 0)
    back1(0, 2)
    back3(0, 1)
    back2(0, 2)
    back3(0, 2)
    for m, a in pairs:
        arrived(tail[m][a].ring.second)

    for i in range(2):
        for cp in share(i, c):
            cp.wait()
    sent(moves[:w_count])
    for l in range(2):
        for m, a in pairs:
            first[l][m][a].close()
            column[l][m][a].close()
    for m, a in pairs:
        tl = tail[m][a]
        for copies in (tl.sums, tl.near, [tl.trade], tl.ring.first, tl.ring.second):
            sent(copies)
    sent(moves[small_from : small_from + 6])


def run_layers(species, emb, cot, own_p, own_w):
    anywhere = pl.BlockSpec(memory_space=pl.ANY)
    dma = pltpu.SemaphoreType.DMA
    vm = lambda *shape: pltpu.VMEM(shape, BF)
    vf = lambda *shape: pltpu.VMEM(shape, F32)
    cells = (2, 256, 768)
    units = lambda *shape: pltpu.VMEM((*shape, UR, UC), BF)
    scratch = [
        vm(2, 3, 768, 384),
        vm(2, 384, 768),
        vm(2, 768, 1536),
        vm(2, 1536, 768),
        vf(2, 8, 1, 768),
        vf(2, *cells),
        vm(2, *cells),
        vm(2, 2, 256, 384),
        vm(2, 2, 256, 384),
        vm(2, 2, 256, 384),
        vf(2, 2, 8, 256),
        vm(2, 2, 256, 384),
        vf(2, *cells),
        vm(2, *cells),
        vm(2, 2, 256, 1536),
        vm(2, 2, 256, 1536),
        vm(2, *cells),
        vm(2, *cells),
        vf(*cells),
        vm(*cells),
        vm(2, 256, 384),
        vm(6, 256, 256),
        vm(6, 256, 256),
        vm(2, *cells),
        vm(2, *cells),
        units(2, 2, 32),
        units(12, 4),
        vf(6, 2, 8, 768),
        vf(6, 2, 8, 768),
        units(2, 3, 2, 2, 4),
        units(3, 2, 4),
        units(3, 2, 2),
        units(3, 2, 1),
        units(3, 2, 5, 2),
        units(3, 2, 2),
        units(3, 2, 3, 1),
        dma((15,)),
        dma((2, 2)),
        dma((2, 2)),
        dma((2,)),
        dma((2,)),
        dma((2,)),
        dma((2,)),
        dma((MOVES,)),
        dma((MOVES,)),
        dma((12,)),
        dma((3, 2)),
    ]
    hbm = lambda *shape: jax.ShapeDtypeStruct((*shape, UR, UC), BF)
    return pl.pallas_call(
        layers_kernel,
        out_shape=(
            jax.ShapeDtypeStruct((4, 256, 768), BF),
            jax.ShapeDtypeStruct((4, 256, 768), BF),
            hbm(2, 3, 2, 32),
            hbm(2, 3, 2, 6, 4),
            hbm(3, 32),
            hbm(3, 32),
            jax.ShapeDtypeStruct((8, 768), F32),
        ),
        in_specs=[pl.BlockSpec(memory_space=pltpu.SMEM)] + [anywhere] * 12,
        out_specs=(*[anywhere] * 6, pl.BlockSpec(memory_space=pltpu.VMEM)),
        scratch_shapes=scratch,
        compiler_params=pltpu.CompilerParams(collective_id=1, has_side_effects=True, vmem_limit_bytes=63 * 2**20),
        name="layers",
    )(species, emb, cot, *own_p, *own_w)


def widen_kernel(gx, gy, lo, dx, small, *out):
    down, up, qkv, attn, layer_out, input_grad, g1, b1, g2, b2, ub, table = out
    for u in range(4):
        rows = slice(u * UR, (u + 1) * UR)
        down[rows, :UC] = gx[0, u].astype(F32)
        down[rows, UC:] = gy[0, u].astype(F32)
    for r in range(2):
        rows = slice(r * UR, (r + 1) * UR)
        for h in range(2):
            up[rows, h * UC : (h + 1) * UC] = gx[1, 2 * r + h].astype(F32)
            up[rows, (2 + h) * UC : (3 + h) * UC] = gy[1, 2 * r + h].astype(F32)
        qkv[0, rows] = gx[2, r].astype(F32)
        qkv[1, rows] = gx[2, 2 + r].astype(F32)
        qkv[2, rows] = gy[2, r].astype(F32)
        attn[:, r * UC : (r + 1) * UC] = gy[2, 2 + r].astype(F32)
    layer_out[...] = lo[...].astype(F32)
    input_grad[...] = dx[...].astype(F32)
    for i, ref in enumerate((g1, b1, g2, b2)):
        ref[...] = small[i : i + 1]
    table[...] = small[4:6]
    ub[:, :768] = small[6:7]
    ub[:, 768:] = small[7:8]


def widen(gx, gy, lo, dx, small):
    whole = lambda *shape: pl.BlockSpec(shape, lambda i: (0,) * len(shape))
    blocks = pl.BlockSpec((3, 4, UR, UC), lambda i: (0, i, 0, 0))
    by_row = lambda *shape: pl.BlockSpec(shape, lambda i: (i,) + (0,) * (len(shape) - 1))
    return pl.pallas_call(
        widen_kernel,
        grid=(8,),
        in_specs=[blocks, blocks, by_row(128, 768), by_row(128, 768), whole(8, 768)],
        out_specs=[
            by_row(192, 768),
            by_row(96, 1536),
            pl.BlockSpec((3, 96, UC), lambda i: (0, i, 0)),
            by_row(48, 768),
            by_row(128, 768),
            by_row(128, 768),
            *[whole(1, 768)] * 4,
            whole(1, 1536),
            whole(2, 768),
        ],
        out_shape=[
            jax.ShapeDtypeStruct(shape, F32)
            for shape in (
                (1536, 768),
                (768, 1536),
                (3, 768, UC),
                (384, 768),
                (1024, 768),
                (1024, 768),
                *[(1, 768)] * 4,
                (1, 1536),
                (2, 768),
            )
        ],
        name="widen",
    )(gx, gy, lo.reshape(1024, 768), dx.reshape(1024, 768), small)


def shards(
    embeddings,
    species,
    ln1_gain,
    ln1_bias,
    qkv_weight,
    out_weight,
    ln2_gain,
    ln2_bias,
    up_weight,
    up_bias,
    down_weight,
    species_bias,
    out_cotangent,
):
    own_w = (qkv_weight[0].transpose(1, 0, 2), out_weight[0], up_weight[0], down_weight[0])
    own_p = (ln1_gain, ln1_bias, ln2_gain, ln2_bias, up_bias, species_bias)
    lo4, dx4, _, _, full_x, full_y, small = run_layers(species, embeddings, out_cotangent, own_p, own_w)
    down, up, qkv, attn, layer_out, input_grad, g1, b1, g2, b2, ub, table = widen(full_x, full_y, lo4, dx4, small)
    return (
        layer_out.reshape(1, 4, 256, 768),
        input_grad.reshape(1, 4, 256, 768),
        g1,
        b1,
        qkv.transpose(1, 0, 2)[None],
        attn[None],
        g2,
        b2,
        up[None],
        ub,
        down[None],
        table[None],
    )


def solution(mesh):
    placed = (
        P("dp", None, None),
        P("dp"),
        P("section", None),
        P("section", None),
        P("section", None, None, "tensor"),
        P("section", "tensor", None),
        P("section", None),
        P("section", None),
        P("section", None, "tensor"),
        P("section", "tensor"),
        P("section", "tensor", None),
        P("section", None, None),
        P("dp", None, None),
    )
    return jax.shard_map(
        shards,
        mesh=mesh,
        in_specs=placed,
        out_specs=(
            P("section", "dp", None, None),
            P("section", "dp", None, None),
            P("section", None),
            P("section", None),
            P("section", None, None, "tensor"),
            P("section", "tensor", None),
            P("section", None),
            P("section", None),
            P("section", None, "tensor"),
            P("section", "tensor"),
            P("section", "tensor", None),
            P("section", None, None),
        ),
        check_vma=False,
    )
```

```python
import functools

import jax
import jax.numpy as jnp
from jax import lax
from jax.experimental import pallas as pl
from jax.experimental.pallas import tpu as pltpu
from jax.sharding import PartitionSpec as P

HEAD = 64
MOVES = 272
UR, UC = 48, 384
MESH = pl.DeviceIdType.MESH
BF = jnp.bfloat16
F32 = jnp.float32

epsilon = 1e-05
root_half = 0.7071067811865476
density_scale = 0.3989422804014327


def place():
    dp = lax.axis_index("dp")
    z = lax.axis_index("tensor") * 2 + lax.rem(dp, 2)
    return dp // 8, lax.rem(dp // 2, 4), z, lax.axis_index("section")


def device(x, y, z, core):
    return (core, (x * 4 + y) * 2 + lax.rem(z, 2), z // 2)


def flip(v):
    return v + 1 - 2 * lax.rem(v, 2)


def wrap(v):
    return lax.rem(v, 4)


def norm(values):
    center = values - jnp.mean(values, axis=-1, keepdims=True)
    inverse = lax.rsqrt(jnp.mean(center * center, axis=-1, keepdims=True) + epsilon)
    return (center * inverse, inverse)


def norm_back(grad_normed, normed, inverse):
    return inverse * (
        grad_normed
        - jnp.mean(grad_normed, axis=-1, keepdims=True)
        - normed * jnp.mean(grad_normed * normed, axis=-1, keepdims=True)
    )


def dot(a, b):
    return jnp.dot(a, b, preferred_element_type=F32)


def dot_rows(a, b):
    return lax.dot_general(a, b, (((0,), (0,)), ((), ())), preferred_element_type=F32)


def dot_back(a, b):
    return lax.dot_general(a, b, (((1,), (1,)), ((), ())), preferred_element_type=F32)


def column_sum(a):
    return jnp.sum(a, axis=0, keepdims=True)


def split_refs(refs, counts):
    out, at = [], 0
    for n in counts:
        out.append(refs[at : at + n])
        at += n
    return out


def layers_kernel(
    species, emb, cot, *refs
):
    own_p, own_w = refs[:6], refs[6:10]
    lo4, dx4, g_out, r1, full_x, full_y, small_out = refs[10:17]
    (
        (qkv_w, out_w, up_w, down_w, pk),
        (S, A1, Q, K, V, LSE, O, R, A2, G, SL, LO, DX, DR, DZ, DO, PB, DS, X, Y),
        (GS, PAD, SM, SMR, s1, s2, s2f, s3, r2, r2f, r3),
        (load_sem, x_send, x_recv, out_local, out_send, out_recv, g_sem, w_send, w_recv, pull_sem, keep_sem),
    ) = split_refs(refs[17:], (5, 20, 11, 11))
    x, y, z, c = place()
    t = z // 2
    zl = lax.rem(z, 2)
    sibling = device(x, y, z, 1 - c)
    far = device(x, y, lax.rem(z + 2, 4), c)
    cross = device(x, y, 3 - z, 1 - c)
    pair = device(x, y, 2 * t + 1 - zl, c)
    along_x = [device(wrap(x + k), y, z, c) for k in (1, 2, 3)]
    along_y = [device(x, wrap(y + k), z, c) for k in (1, 2, 3)]
    barrier = pltpu.get_barrier_semaphore()
    for p in (sibling, far, cross, pair, *along_x, *along_y):
        pl.semaphore_signal(barrier, inc=1, device_id=p, device_id_type=MESH)
    weights = (qkv_w, out_w, up_w, down_w)

    def load(src, dst, i):
        cp = pltpu.make_async_copy(src, dst, load_sem.at[i])
        cp.start()
        return cp

    w_loads = [load(own_w[i], w.at[c], i) for i, w in enumerate(weights)]
    start = [load(emb.at[pl.ds(2 * t, 2)], DZ, 4)]
    p_loads = [load(own_p[i], pk.at[c, i], 7 + i) for i in range(4)]
    for i in range(2):
        p_loads.append(load(own_p[4].at[:, pl.ds(i * 768, 768)], pk.at[c, 6 + i], 11 + i))
        p_loads.append(load(own_p[5].at[:, i], pk.at[c, 4 + i], 13 + i))
    cot_load = load(cot.at[pl.ds(2 * t, 2)], DR, 6)
    pl.semaphore_wait(barrier, 10)
    near_x, wrap_x = device(flip(x), y, z, c), device(3 - x, y, z, c)
    near_y, wrap_y = device(x, flip(y), z, c), device(x, 3 - y, z, c)

    moves = []

    def move(src, dst, peer):
        i = len(moves)
        cp = pltpu.make_async_remote_copy(
            src_ref=src, dst_ref=dst, send_sem=w_send.at[i], recv_sem=w_recv.at[i], device_id=peer, device_id_type=MESH
        )
        moves.append(cp)
        return cp

    def start_all(copies):
        for cp in copies:
            cp.start()

    def arrived(copies):
        for cp in copies:
            cp.wait_recv()

    def sent(copies):
        for cp in copies:
            cp.wait_send()

    pk_move = move(pk.at[c], pk.at[c], cross)
    def piece_out(ref):
        return ref.at[pl.ds(x * 96 + (y // 2) * 48, 48), pl.ds(lax.rem(y, 2) * 384, 384)]

    def piece_up(ref):
        return ref.at[pl.ds(x * 192 + y * 48, 48)]

    def piece_down(ref):
        return ref.at[pl.ds(y * 384 + x * 96, 96)]

    pieces = ((1, out_w, piece_out), (2, up_w, piece_up), (3, down_w, piece_down))
    hops = [move(f(own_w[i]), f(w.at[c]), cross) for i, w, f in pieces]
    pl.when(c == 0)(lambda: start_all(hops))
    for cp in p_loads:
        cp.wait()
    pk_move.start()
    direct = [
        move(own_w[0].at[i, pl.ds((1 - zl) * 384, 384)], qkv_w.at[c, i, pl.ds((1 - zl) * 384, 384)], cross) for i in range(3)
    ]
    pl.when(c == 0)(lambda: start_all(direct))

    second = [
        [move(f(w.at[1 - c]), f(w.at[1 - c]), p) for p in (along_y, along_y, along_x)[k]]
        for k, (i, w, f) in enumerate(pieces)
    ]

    class Spread:
        def __init__(self, low, high, i, near_dev, wrap_dev):
            near, other = flip(i), 3 - i
            self.first = [move(low(i), low(i), wrap_dev), move(high(i), high(i), near_dev)]
            self.second = [
                move(low(i), low(i), near_dev),
                move(high(i), high(i), wrap_dev),
                move(low(other), low(other), near_dev),
                move(high(near), high(near), wrap_dev),
            ]

        def start(self):
            start_all(self.first)
            start_all(self.second[:2])

        def mid(self):
            arrived(self.first)
            start_all(self.second[2:])

    by_x, by_y = (x, near_x, wrap_x), (y, near_y, wrap_y)

    def spread_rows(w, n, axis):
        ref, h = w.at[1 - c], n // 2
        return Spread(lambda k: ref.at[pl.ds(k * n, h)], lambda k: ref.at[pl.ds(k * n + h, h)], *axis)

    third = [spread_rows(out_w, 96, by_x), spread_rows(up_w, 192, by_x), spread_rows(down_w, 384, by_y)]
    trade = []
    for i in range(3):
        part = qkv_w.at[1 - c, i, pl.ds(zl * 384, 384)]
        trade.append(move(part, part, pair))
    w_count = len(moves)

    def gather_hops():
        for k in range(3):
            arrived([hops[k]])
            start_all(second[k])

    def gather_rest():
        for k in range(3):
            arrived(second[k])
            third[k].start()

    def gather_mids():
        for k in range(3):
            third[k].mid()

    def hand_on(*which):
        for i in which:
            arrived([direct[i]])
            trade[i].start()

    @pl.when(c == 1)
    def _():
        gather_hops()
        hand_on(0)
        gather_rest()
        hand_on(1)
        start_all(hops)
        hand_on(2)
        start_all(direct)
        gather_mids()

    arrived([pk_move])
    for cp in start:
        cp.wait()

    def need(l, i):
        incoming = (trade, *[ring.second for ring in third])[i]
        if l == 0:
            w_loads[i].wait()
        pl.when(c == 1 - l)(lambda: arrived(incoming))

    flying = {}

    def push(kind, b):
        cp = pltpu.make_async_remote_copy(
            src_ref=X.at[kind, b],
            dst_ref=Y.at[kind, b],
            send_sem=x_send.at[kind, b],
            recv_sem=x_recv.at[kind, b],
            device_id=sibling,
            device_id_type=MESH,
        )
        cp.start()
        flying[kind, b] = cp

    def both(kind, b):
        flying.pop((kind, b)).wait()
        return X[kind, b].astype(F32) + Y[kind, b].astype(F32)

    def flag(b):
        return species[2 * t + b]

    def heads_forward(l, b):
        if l == 0:
            xin = DZ[b].astype(F32)
        else:
            low = (R[0, b] + both(1, b)).astype(BF)
            LO[0, b] = low
            xin = low.astype(F32)
        s = xin + jnp.where(flag(b) == 0, pk[l, 4], pk[l, 5])
        S[l, b] = s
        n1, _ = norm(s)
        a1 = (n1 * pk[l, 0] + pk[l, 1]).astype(BF)
        A1[l, b] = a1
        if b == 0:
            need(l, 0)
        for i, part in enumerate((Q, K, V)):
            part[l, b] = dot(a1, qkv_w[l, i]).astype(BF)
        for h in range(6):
            hs = slice(h * HEAD, h * HEAD + HEAD)
            sc = dot_back(K[l, b, :, hs], Q[l, b, :, hs]) * HEAD**-0.5
            top = jnp.max(sc, axis=0, keepdims=True)
            e = jnp.exp(sc - top)
            total = jnp.sum(e, axis=0, keepdims=True)
            PB[h] = (e * (1.0 / total)).astype(BF)
            LSE[l, b, h : h + 1] = top + jnp.log(total)
        for h in range(6):
            hs = slice(h * HEAD, h * HEAD + HEAD)
            O[l, b, :, hs] = dot_rows(PB[h], V[l, b, :, hs]).astype(BF)
        if b == 0:
            need(l, 1)
        X[0, b] = dot(O[l, b], out_w[l]).astype(BF)
        push(0, b)

    def units_forward(l, b):
        r = S[l, b] + both(0, b)
        R[l, b] = r
        n2, _ = norm(r)
        a2 = (n2 * pk[l, 2] + pk[l, 3]).astype(BF)
        A2[l, b] = a2
        if b == 0:
            need(l, 2)
        for j in range(2):
            cols = slice(j * 768, j * 768 + 768)
            u = dot(a2, up_w[l, :, cols]) + pk[l, 6 + j]
            cdf = 0.5 * (1.0 + lax.erf(u * root_half))
            G[l, b, :, cols] = (u * cdf).astype(BF)
            SL[l, b, :, cols] = (cdf + u * density_scale * jnp.exp(-0.5 * u * u)).astype(BF)
        if b == 0:
            need(l, 3)
        X[1, b] = dot(G[l, b], down_w[l]).astype(BF)
        push(1, b)

    def rows(ref, *lead):
        a = ref[lead] if lead else ref[...]
        return a.reshape(512, a.shape[-1])

    def put(slot, half, value, numbers):
        for i, number in enumerate(numbers):
            GS[slot, half, number] = value[i * UR : (i + 1) * UR]

    g_copies = {}

    def flush(l, m):
        cp = pltpu.make_async_copy(GS.at[m % 2], g_out.at[l, m], g_sem.at[m % 2])
        cp.start()
        g_copies[m % 2] = cp

    def free(slot):
        if slot in g_copies:
            g_copies.pop(slot).wait()

    def dy(l, b):
        return DR[b] if l == 1 else DX[1, b].astype(F32)

    def share(i, l):
        src, dst = ((LO, lo4), (DX, dx4))[i]
        part = dst.at[pl.ds(2 * t, 2)]
        here = pltpu.make_async_copy(src.at[l], part, out_local.at[i])
        there = pltpu.make_async_remote_copy(
            src_ref=src.at[l], dst_ref=part, send_sem=out_send.at[i], recv_sem=out_recv.at[i], device_id=far, device_id_type=MESH
        )
        return here, there

    def share_own(i, l):
        on_core(l)(lambda: start_all(share(i, l)))


    def add_up(jobs):
        for dst, pieces in jobs:
            total = pieces[0][...].astype(F32)
            for piece in pieces[1:]:
                total += piece[...].astype(F32)
            dst[...] = total.astype(BF)

    pulled = {}
    turn = [0]
    known = [None]

    def on_core(l, other=False):
        def run(step):
            if known[0] is None:
                pl.when((c != l) if other else (c == l))(step)
            elif (known[0] == l) != other:
                step()

        return run


    def pull(key, jobs):
        pad = turn[0] % 2
        turn[0] += 1
        copies, local = [], []
        for dst, pieces in jobs:
            for piece in pieces:
                k = len(copies)
                copies.append(pltpu.make_async_copy(piece, PAD.at[pad, k], pull_sem.at[pad, k]))
            local.append((dst, [PAD.at[pad, k] for k in range(len(copies) - len(pieces), len(copies))]))
        start_all(copies)
        pulled[key] = (copies, local)

    def add_pulled(key):
        copies, local = pulled[key]
        for cp in copies:
            cp.wait()
        add_up(local)

    class Ring:
        def __init__(self, i, near_dev, wrap_dev, low_of, high_of, got, low, high):
            near, other, opposite = flip(i), 3 - i, 3 - flip(i)
            self.first = [
                move(low_of(near), got(0), near_dev),
                move(high_of(other), got(2), wrap_dev),
                move(low_of(opposite), got(1), near_dev),
                move(high_of(opposite), got(3), wrap_dev),
            ]
            self.second = [move(low, got(4), wrap_dev), move(high, got(5), near_dev)]
            self.mid_jobs = lambda: [(low, [low_of(other), got(1)]), (high, [high_of(near), got(3)])]
            self.end_jobs = lambda: [(low, [low_of(i), got(0), got(4)]), (high, [high_of(i), got(2), got(5)])]

        def start(self):
            start_all(self.first[2:])
            start_all(self.first[:2])

        def mid_wait(self):
            arrived(self.first[2:])

        def end_wait(self):
            arrived(self.first[:2])
            arrived(self.second)
            sent(self.second)

        def close(self):
            sent(self.first)

    class Column:
        def __init__(self, l, of, got, kept, out, passed):
            self.l = l
            low, high = out.at[pl.ds(0, 2)], out.at[pl.ds(2, 2)]
            self.own_pair = move(of(1 - zl, 0), got(0), pair)
            self.far_pair = move(of(zl, 0), kept, pair)
            self.far_cross = [move(of(0, 1), got(1), cross), move(of(1, 1), got(2), cross)]
            self.own_second = move(high, got(4), pair)
            self.far_second = move(passed, got(3), cross)
            self.own_mid = lambda: [(high, [of(1 - zl, 1), got(2 - zl)])]
            self.far_mid = lambda: [(passed, [of(1 - zl, 0), kept])]
            self.own_end = lambda: [(low, [of(zl, 0), got(0), got(3)]), (high, [of(zl, 1), got(1 + zl), got(4)])]

        def start(self):
            @on_core(self.l)
            def _():
                self.own_pair.start()

            @on_core(self.l, True)
            def _():
                start_all((self.far_pair, *self.far_cross))

        def mid(self):
            @on_core(self.l)
            def _():
                arrived(self.far_cross)
                add_up(self.own_mid())
                self.own_second.start()

            @on_core(self.l, True)
            def _():
                arrived([self.far_pair])
                add_up(self.far_mid())
                self.far_second.start()

        def end(self):
            arrived((self.own_pair, self.own_second, self.far_second))
            sent([self.own_second])
            add_up(self.own_end())

        def close(self):
            @on_core(self.l)
            def _():
                sent([self.own_pair])

            @on_core(self.l, True)
            def _():
                sent((self.far_pair, *self.far_cross, self.far_second))

    pairs = [(m, a) for m in range(3) for a in range(2)]

    def matrix_ring(l, m, a):
        g, got, out = g_out.at[l, m, a], r1.at[l, m, a], s1.at[l, m, a]
        return Ring(
            *(by_x, by_y)[a],
            lambda k: g.at[pl.ds(k * 8, 4)],
            lambda k: g.at[pl.ds(k * 8 + 4, 4)],
            lambda j: got.at[j],
            out.at[0],
            out.at[1],
        )

    def z_column(l, m, a):
        return Column(
            l,
            lambda k, half: s1.at[l, m, a, k, pl.ds(half * 2, 2)],
            lambda j: r2.at[m, a, j],
            r2f.at[m, a],
            s2.at[m, a],
            s2f.at[m, a],
        )

    first = [[[matrix_ring(l, m, a) for a in range(2)] for m in range(3)] for l in range(2)]
    column = [[[z_column(l, m, a) for a in range(2)] for m in range(3)] for l in range(2)]


    class Tail:
        def __init__(self, m, a):
            i, j = ((x, y), (y, x))[a]
            peers = (along_y, along_x)[a]
            whole = (full_x, full_y)[a].at[m]
            number = i * 8 + zl * 4 + j
            own = whole.at[pl.ds(number, 1)]
            out = s3.at[m, a]
            self.sums = [move(s2.at[m, a, pl.ds(wrap(j + k), 1)], r3.at[m, a, k - 1], peers[k - 1]) for k in (1, 2, 3)]
            self.job = (out, [s2.at[m, a, pl.ds(j, 1)]] + [r3.at[m, a, k] for k in range(3)])
            self.keep = pltpu.make_async_copy(out, own, keep_sem.at[m, a])
            self.near = [move(out, own, p) for p in peers]
            group = whole.at[pl.ds(i * 8 + zl * 4, 4)]
            self.trade = move(group, group, pair)
            self.ring = Spread(
                lambda k: whole.at[pl.ds(k * 8, 4)], lambda k: whole.at[pl.ds(k * 8 + 4, 4)], *(by_x, by_y)[a]
            )

    tail = [[Tail(m, a) for a in range(2)] for m in range(3)]

    def launch(l, m):
        free(m % 2)
        for ring in first[l][m]:
            ring.start()

    def mid_pull(l, m):
        for ring in first[l][m]:
            ring.mid_wait()
        pull(("mid", l, m), [job for ring in first[l][m] for job in ring.mid_jobs()])

    def mid_send(l, m):
        add_pulled(("mid", l, m))
        for ring in first[l][m]:
            start_all(ring.second)

    def end_pull(l, m):
        for ring in first[l][m]:
            ring.end_wait()
        pull(("end", l, m), [job for ring in first[l][m] for job in ring.end_jobs()])

    def end_send(l, m):
        add_pulled(("end", l, m))
        for col in column[l][m]:
            col.start()

    def sum1_mid(l, m):
        mid_pull(l, m)
        mid_send(l, m)

    def sum1_end(l, m):
        end_pull(l, m)
        end_send(l, m)

    def sum2_mid(l, m):
        for col in column[l][m]:
            col.mid()

    def sum2_end(l, m):
        @on_core(l)
        def _():
            for col, tl in zip(column[l][m], tail[m]):
                col.end()
                start_all(tl.sums)

    def sum3(l, m):
        @on_core(l)
        def _():
            for tl in tail[m]:
                arrived(tl.sums)
                add_up([tl.job])
                tl.keep.start()
                start_all(tl.near)

    def back1(l, m):
        @on_core(l)
        def _():
            for tl in tail[m]:
                arrived(tl.near)
                tl.keep.wait()
                tl.trade.start()

    def back2(l, m):
        @on_core(l)
        def _():
            for tl in tail[m]:
                arrived([tl.trade])
                tl.ring.start()

    def back3(l, m):
        @on_core(l)
        def _():
            for tl in tail[m]:
                tl.ring.mid()

    beside = {
        (1, "units"): [(launch, 1, 1)],
        (1, "cell0"): [(mid_pull, 1, 0)],
        (1, "cell1"): [(mid_send, 1, 0), (mid_pull, 1, 1)],
        (1, "heads"): [(mid_send, 1, 1), (launch, 1, 2), (share_own, 1, 1)],
        (0, "pushed"): [(end_pull, 1, 0)],
        (0, "grads_down"): [(end_send, 1, 0)],
        (0, "grads_up"): [(launch, 0, 0), (end_pull, 1, 1)],
        (0, "units"): [(end_send, 1, 1), (mid_pull, 1, 2), (launch, 0, 1)],
        (0, "cell0"): [(mid_send, 1, 2), (sum2_mid, 1, 0), (mid_pull, 0, 0)],
        (0, "cell1"): [(mid_send, 0, 0), (sum2_mid, 1, 1), (sum2_end, 1, 0)],
        (0, "heads"): [(launch, 0, 2), (mid_pull, 0, 1)],
    }

    def meanwhile(l, point):
        for f, *args in beside.get((l, point), ()):
            f(*args)

    def grads_down(l):
        free(0)
        dz = rows(DZ)
        for j in range(2):
            gd = dot_rows(rows(G, l)[:, j * 768 : j * 768 + 768], dz).astype(BF)
            for h in range(2):
                put(0, h, gd[:, h * UC : (h + 1) * UC], range(j * 16, j * 16 + 16))
        flush(l, 0)

    def units_backward(l):
        for b in range(2):
            if l == 0:
                DZ[b] = DX[1, b]
            for j in range(2):
                cols = slice(j * 768, j * 768 + 768)
                SL[l, b, :, cols] = (dot_back(DZ[b], down_w[l, cols]) * SL[l, b, :, cols].astype(F32)).astype(BF)
            X[0, b] = dot_back(SL[l, b], up_w[l]).astype(BF)
            push(0, b)
        meanwhile(l, "pushed")
        if l == 0:
            grads_down(l)
        meanwhile(l, "grads_down")
        free(1)
        a2 = rows(A2, l)
        for j in range(2):
            du = rows(SL, l)[:, j * 768 : j * 768 + 768]
            gu = dot_rows(a2, du).astype(BF)
            for h in range(2):
                put(1, j, gu[:, h * UC : (h + 1) * UC], range(h, 32, 2))
            SM[0, l, 6 + j : 7 + j] = column_sum(du.astype(F32))
        flush(l, 1)
        meanwhile(l, "grads_up")
        gain = bias = 0.0
        for b in range(2):
            da2 = both(0, b)
            n2, inv = norm(R[l, b])
            gain += column_sum(da2 * n2)
            bias += column_sum(da2)
            dr = dy(l, b) + norm_back(da2 * pk[l, 2], n2, inv)
            DR[b] = dr
            DZ[b] = dr.astype(BF)
        SM[0, l, 2:3] = gain
        SM[0, l, 3:4] = bias
        meanwhile(l, "units")

    def heads_backward(l):
        for b in range(2):
            DO[b] = dot_back(DZ[b], out_w[l]).astype(BF)
            for h in range(6):
                hs = slice(h * HEAD, h * HEAD + HEAD)
                sc = dot_back(K[l, b, :, hs], Q[l, b, :, hs]) * HEAD**-0.5
                p = jnp.exp(sc - LSE[l, b, h : h + 1])
                dp = dot_back(V[l, b, :, hs], DO[b, :, hs])
                pdp = p * dp
                PB[h] = p.astype(BF)
                DS[h] = (pdp - p * jnp.sum(pdp, axis=0, keepdims=True)).astype(BF)
            for h in range(6):
                hs = slice(h * HEAD, h * HEAD + HEAD)
                V[l, b, :, hs] = dot(PB[h], DO[b, :, hs]).astype(BF)
                dk = (dot(DS[h], Q[l, b, :, hs]) * HEAD**-0.5).astype(BF)
                dq = (dot_rows(DS[h], K[l, b, :, hs]) * HEAD**-0.5).astype(BF)
                K[l, b, :, hs] = dk
                Q[l, b, :, hs] = dq
            X[1, b] = (
                dot_back(Q[l, b], qkv_w[l, 0]) + dot_back(K[l, b], qkv_w[l, 1]) + dot_back(V[l, b], qkv_w[l, 2])
            ).astype(BF)
            push(1, b)
            meanwhile(l, f"cell{b}")
        free(0)
        go = dot_rows(rows(O, l), rows(DZ)).astype(BF)
        for h in range(2):
            put(0, 1, go[:, h * UC : (h + 1) * UC], range(2 + h, 32, 4))
        a1 = rows(A1, l)
        for i, d in enumerate((Q, K, V)):
            put(0, i // 2, dot_rows(a1, rows(d, l)).astype(BF), [4 * (r // 2) + r % 2 + (2 if i == 1 else 0) for r in range(16)])
        flush(l, 2)
        gain = bias = 0.0
        table = [0.0, 0.0]
        for b in range(2):
            da1 = both(1, b)
            n1, inv = norm(S[l, b])
            gain += column_sum(da1 * n1)
            bias += column_sum(da1)
            dx = DR[b] + norm_back(da1 * pk[l, 0], n1, inv)
            DX[l, b] = dx.astype(BF)
            total = column_sum(dx)
            for k in range(2):
                table[k] += jnp.where(flag(b) == k, total, 0.0)
        SM[0, l, 0:1] = gain
        SM[0, l, 1:2] = bias
        SM[0, l, 4:5] = table[0]
        SM[0, l, 5:6] = table[1]
        meanwhile(l, "heads")

    for l in range(2):
        for b in range(2):
            heads_forward(l, b)
        if l == 0:

            @pl.when(c == 0)
            def _():
                gather_hops()
                hand_on(0, 1)
                gather_rest()
                hand_on(2)

        else:
            share_own(0, 0)
        units_forward(l, 0)
        units_forward(l, 1)
        if l == 0:
            pl.when(c == 0)(gather_mids)
    cot_load.wait()
    for b in range(2):
        DZ[b] = DR[b].astype(BF)
    grads_down(1)
    for b in range(2):
        LO[1, b] = (R[1, b] + both(1, b)).astype(BF)
    launch(1, 0)
    share_own(0, 1)
    for l in (1, 0):
        units_backward(l)
        heads_backward(l)

    small_steps = []

    def small_step(k, peer, both_layers=True):
        src = SM.at[k] if both_layers else SM.at[k, pl.ds(1 - c, 1)]
        dst = SMR.at[k] if both_layers else SMR.at[k, pl.ds(1 - c, 1)]
        cp = move(src, dst, peer)

        def begin():
            cp.start()

        def finish_step():
            cp.wait_recv()
            if both_layers:
                SM[k + 1] = SM[k] + SMR[k]
            else:
                small_out[...] = SM[k, pl.ds(c, 1)][0] + SMR[k, pl.ds(c, 1)][0]

        small_steps.append((begin, finish_step))

    small_from = len(moves)
    for k, peer in enumerate((near_x, wrap_x, near_y, wrap_y, pair)):
        small_step(k, peer)
    small_step(5, cross, False)

    def small_next(k):
        if k:
            small_steps[k - 1][1]()
        if k < 6:
            small_steps[k][0]()

    steps = (
        [
            (mid_send, 0, 1),
            (end_pull, 1, 2),
            (end_send, 1, 2),
            (end_pull, 0, 0),
            (end_send, 0, 0),
            (sum2_mid, 1, 2),
            (mid_pull, 0, 2),
            (mid_send, 0, 2),
            (sum2_mid, 0, 0),
            (small_next, 0),
            (end_pull, 0, 1),
            (end_send, 0, 1),
            (sum2_end, 0, 0),
            (end_pull, 0, 2),
            (end_send, 0, 2),
            (small_next, 1),
            (sum2_mid, 0, 1),
            (sum3, 0, 0),
            (sum2_end, 0, 1),
            (sum2_mid, 0, 2),
            (small_next, 2),
            (back1, 0, 0),
            (sum3, 0, 1),
            (sum2_end, 0, 2),
            (small_next, 3),
            (back1, 0, 1),
            (sum3, 0, 2),
            (back2, 0, 0),
            (small_next, 4),
            (back1, 0, 2),
            (back2, 0, 1),
            (small_next, 5),
            (small_next, 6),
            (share_own, 1, 0),
            (back3, 0, 0),
            (back2, 0, 2),
            (back3, 0, 1),
            (back3, 0, 2),
        ],
        [
            (mid_send, 0, 1),
            (end_pull, 1, 2),
            (end_send, 1, 2),
            (end_pull, 0, 0),
            (end_send, 0, 0),
            (sum3, 1, 0),
            (sum2_end, 1, 1),
            (mid_pull, 0, 2),
            (mid_send, 0, 2),
            (sum2_mid, 1, 2),
            (sum2_mid, 0, 0),
            (small_next, 0),
            (back1, 1, 0),
            (sum3, 1, 1),
            (sum2_end, 1, 2),
            (end_pull, 0, 1),
            (end_send, 0, 1),
            (end_pull, 0, 2),
            (end_send, 0, 2),
            (small_next, 1),
            (sum2_mid, 0, 1),
            (back2, 1, 0),
            (back1, 1, 1),
            (sum3, 1, 2),
            (sum2_mid, 0, 2),
            (small_next, 2),
            (back2, 1, 1),
            (back1, 1, 2),
            (small_next, 3),
            (back3, 1, 0),
            (back2, 1, 2),
            (small_next, 4),
            (back3, 1, 1),
            (small_next, 5),
            (back3, 1, 2),
            (small_next, 6),
        ],
    )
    pulls_so_far = turn[0]

    def finish_on(core):
        def run():
            known[0], turn[0] = core, pulls_so_far
            for f, *args in steps[core]:
                f(*args)
            known[0] = None

        pl.when(c == core)(run)

    finish_on(0)
    finish_on(1)
    for m, a in pairs:
        arrived(tail[m][a].ring.second)

    for i in range(2):
        for cp in share(i, c):
            cp.wait()
    sent(moves[:w_count])
    for l in range(2):
        for m, a in pairs:
            first[l][m][a].close()
            column[l][m][a].close()
    for m, a in pairs:
        tl = tail[m][a]
        for copies in (tl.sums, tl.near, [tl.trade], tl.ring.first, tl.ring.second):
            sent(copies)
    sent(moves[small_from : small_from + 6])
    assert len(moves) <= MOVES


def run_layers(species, emb, cot, own_p, own_w):
    anywhere = pl.BlockSpec(memory_space=pl.ANY)
    dma = pltpu.SemaphoreType.DMA
    vm = lambda *shape: pltpu.VMEM(shape, BF)
    vf = lambda *shape: pltpu.VMEM(shape, F32)
    cells = (2, 256, 768)
    units = lambda *shape: pltpu.VMEM((*shape, UR, UC), BF)
    scratch = [
        vm(2, 3, 768, 384),
        vm(2, 384, 768),
        vm(2, 768, 1536),
        vm(2, 1536, 768),
        vf(2, 8, 1, 768),
        vf(2, *cells),
        vm(2, *cells),
        vm(2, 2, 256, 384),
        vm(2, 2, 256, 384),
        vm(2, 2, 256, 384),
        vf(2, 2, 8, 256),
        vm(2, 2, 256, 384),
        vf(2, *cells),
        vm(2, *cells),
        vm(2, 2, 256, 1536),
        vm(2, 2, 256, 1536),
        vm(2, *cells),
        vm(2, *cells),
        vf(*cells),
        vm(*cells),
        vm(2, 256, 384),
        vm(6, 256, 256),
        vm(6, 256, 256),
        vm(2, *cells),
        vm(2, *cells),
        units(2, 2, 32),
        units(2, 12, 4),
        vf(6, 2, 8, 768),
        vf(6, 2, 8, 768),
        units(2, 3, 2, 2, 4),
        units(3, 2, 4),
        units(3, 2, 2),
        units(3, 2, 1),
        units(3, 2, 5, 2),
        units(3, 2, 2),
        units(3, 2, 3, 1),
        dma((15,)),
        dma((2, 2)),
        dma((2, 2)),
        dma((2,)),
        dma((2,)),
        dma((2,)),
        dma((2,)),
        dma((MOVES,)),
        dma((MOVES,)),
        dma((2, 12)),
        dma((3, 2)),
    ]
    hbm = lambda *shape: jax.ShapeDtypeStruct((*shape, UR, UC), BF)
    return pl.pallas_call(
        layers_kernel,
        out_shape=(
            jax.ShapeDtypeStruct((4, 256, 768), BF),
            jax.ShapeDtypeStruct((4, 256, 768), BF),
            hbm(2, 3, 2, 32),
            hbm(2, 3, 2, 6, 4),
            hbm(3, 32),
            hbm(3, 32),
            jax.ShapeDtypeStruct((8, 768), F32),
        ),
        in_specs=[pl.BlockSpec(memory_space=pltpu.SMEM)] + [anywhere] * 12,
        out_specs=(*[anywhere] * 6, pl.BlockSpec(memory_space=pltpu.VMEM)),
        scratch_shapes=scratch,
        compiler_params=pltpu.CompilerParams(collective_id=1, has_side_effects=True, vmem_limit_bytes=63 * 2**20),
        name="layers",
    )(species, emb, cot, *own_p, *own_w)


def widen_kernel(gx, gy, lo, dx, small, *out):
    down, up, qkv, attn, layer_out, input_grad, g1, b1, g2, b2, ub, table = out
    for u in range(4):
        rows = slice(u * UR, (u + 1) * UR)
        down[rows, :UC] = gx[0, u].astype(F32)
        down[rows, UC:] = gy[0, u].astype(F32)
    for r in range(2):
        rows = slice(r * UR, (r + 1) * UR)
        for h in range(2):
            up[rows, h * UC : (h + 1) * UC] = gx[1, 2 * r + h].astype(F32)
            up[rows, (2 + h) * UC : (3 + h) * UC] = gy[1, 2 * r + h].astype(F32)
        qkv[0, rows] = gx[2, r].astype(F32)
        qkv[1, rows] = gx[2, 2 + r].astype(F32)
        qkv[2, rows] = gy[2, r].astype(F32)
        attn[:, r * UC : (r + 1) * UC] = gy[2, 2 + r].astype(F32)
    layer_out[...] = lo[...].astype(F32)
    input_grad[...] = dx[...].astype(F32)
    for i, ref in enumerate((g1, b1, g2, b2)):
        ref[...] = small[i : i + 1]
    table[...] = small[4:6]
    ub[:, :768] = small[6:7]
    ub[:, 768:] = small[7:8]


def widen(gx, gy, lo, dx, small):
    whole = lambda *shape: pl.BlockSpec(shape, lambda i: (0,) * len(shape))
    blocks = pl.BlockSpec((3, 4, UR, UC), lambda i: (0, i, 0, 0))
    by_row = lambda *shape: pl.BlockSpec(shape, lambda i: (i,) + (0,) * (len(shape) - 1))
    return pl.pallas_call(
        widen_kernel,
        grid=(8,),
        in_specs=[blocks, blocks, by_row(128, 768), by_row(128, 768), whole(8, 768)],
        out_specs=[
            by_row(192, 768),
            by_row(96, 1536),
            pl.BlockSpec((3, 96, UC), lambda i: (0, i, 0)),
            by_row(48, 768),
            by_row(128, 768),
            by_row(128, 768),
            *[whole(1, 768)] * 4,
            whole(1, 1536),
            whole(2, 768),
        ],
        out_shape=[
            jax.ShapeDtypeStruct(shape, F32)
            for shape in (
                (1536, 768),
                (768, 1536),
                (3, 768, UC),
                (384, 768),
                (1024, 768),
                (1024, 768),
                *[(1, 768)] * 4,
                (1, 1536),
                (2, 768),
            )
        ],
        name="widen",
    )(gx, gy, lo.reshape(1024, 768), dx.reshape(1024, 768), small)


def shards(
    embeddings,
    species,
    ln1_gain,
    ln1_bias,
    qkv_weight,
    out_weight,
    ln2_gain,
    ln2_bias,
    up_weight,
    up_bias,
    down_weight,
    species_bias,
    out_cotangent,
):
    own_w = (qkv_weight[0].transpose(1, 0, 2), out_weight[0], up_weight[0], down_weight[0])
    own_p = (ln1_gain, ln1_bias, ln2_gain, ln2_bias, up_bias, species_bias)
    lo4, dx4, _, _, full_x, full_y, small = run_layers(species, embeddings, out_cotangent, own_p, own_w)
    down, up, qkv, attn, layer_out, input_grad, g1, b1, g2, b2, ub, table = widen(full_x, full_y, lo4, dx4, small)
    return (
        layer_out.reshape(1, 4, 256, 768),
        input_grad.reshape(1, 4, 256, 768),
        g1,
        b1,
        qkv.transpose(1, 0, 2)[None],
        attn[None],
        g2,
        b2,
        up[None],
        ub,
        down[None],
        table[None],
    )


def solution(mesh):
    placed = (
        P("dp", None, None),
        P("dp"),
        P("section", None),
        P("section", None),
        P("section", None, None, "tensor"),
        P("section", "tensor", None),
        P("section", None),
        P("section", None),
        P("section", None, "tensor"),
        P("section", "tensor"),
        P("section", "tensor", None),
        P("section", None, None),
        P("dp", None, None),
    )
    return jax.shard_map(
        shards,
        mesh=mesh,
        in_specs=placed,
        out_specs=(
            P("section", "dp", None, None),
            P("section", "dp", None, None),
            P("section", None),
            P("section", None),
            P("section", None, None, "tensor"),
            P("section", "tensor", None),
            P("section", None),
            P("section", None),
            P("section", None, "tensor"),
            P("section", "tensor"),
            P("section", "tensor", None),
            P("section", None, None),
        ),
        check_vma=False,
    )
```

```python
import functools

import jax
import jax.numpy as jnp
from jax import lax
from jax.experimental import pallas as pl
from jax.experimental.pallas import tpu as pltpu
from jax.sharding import PartitionSpec as P

HEAD = 64
MOVES = 320
UR, UC = 48, 384
MESH = pl.DeviceIdType.MESH
BF = jnp.bfloat16
F32 = jnp.float32

epsilon = 1e-05
root_half = 0.7071067811865476
density_scale = 0.3989422804014327


def place():
    dp = lax.axis_index("dp")
    z = lax.axis_index("tensor") * 2 + lax.rem(dp, 2)
    return dp // 8, lax.rem(dp // 2, 4), z, lax.axis_index("section")


def device(x, y, z, core):
    return (core, (x * 4 + y) * 2 + lax.rem(z, 2), z // 2)


def flip(v):
    return v + 1 - 2 * lax.rem(v, 2)


def wrap(v):
    return lax.rem(v, 4)


def norm(values):
    center = values - jnp.mean(values, axis=-1, keepdims=True)
    inverse = lax.rsqrt(jnp.mean(center * center, axis=-1, keepdims=True) + epsilon)
    return (center * inverse, inverse)


def norm_back(grad_normed, normed, inverse):
    return inverse * (
        grad_normed
        - jnp.mean(grad_normed, axis=-1, keepdims=True)
        - normed * jnp.mean(grad_normed * normed, axis=-1, keepdims=True)
    )


def dot(a, b):
    return jnp.dot(a, b, preferred_element_type=F32)


def dot_rows(a, b):
    return lax.dot_general(a, b, (((0,), (0,)), ((), ())), preferred_element_type=F32)


def dot_back(a, b):
    return lax.dot_general(a, b, (((1,), (1,)), ((), ())), preferred_element_type=F32)


def column_sum(a):
    return jnp.sum(a, axis=0, keepdims=True)


def split_refs(refs, counts):
    out, at = [], 0
    for n in counts:
        out.append(refs[at : at + n])
        at += n
    return out


def layers_kernel(
    species, emb, cot, *refs
):
    own_p, own_w = refs[:6], refs[6:10]
    lo4, dx4, g_out, r1, full_x, full_y, small_out = refs[10:17]
    (
        (qkv_w, out_w, up_w, down_w, pk),
        (S, A1, Q, K, V, LSE, O, R, A2, G, SL, LO, DX, DR, DZ, DO, PB, DS, X, Y),
        (GS, PAD, SM, SMR, s1, s2, s2f, s3, r2, r2f, r3, s3c, r3c),
        (load_sem, x_send, x_recv, out_local, out_send, out_recv, g_sem, w_send, w_recv, pull_sem, keep_sem),
    ) = split_refs(refs[17:], (5, 20, 13, 11))
    x, y, z, c = place()
    t = z // 2
    zl = lax.rem(z, 2)
    sibling = device(x, y, z, 1 - c)
    far = device(x, y, lax.rem(z + 2, 4), c)
    cross = device(x, y, 3 - z, 1 - c)
    pair = device(x, y, 2 * t + 1 - zl, c)
    along_x = [device(wrap(x + k), y, z, c) for k in (1, 2, 3)]
    along_y = [device(x, wrap(y + k), z, c) for k in (1, 2, 3)]
    barrier = pltpu.get_barrier_semaphore()
    for p in (sibling, far, cross, pair, *along_x, *along_y):
        pl.semaphore_signal(barrier, inc=1, device_id=p, device_id_type=MESH)
    weights = (qkv_w, out_w, up_w, down_w)

    def load(src, dst, i):
        cp = pltpu.make_async_copy(src, dst, load_sem.at[i])
        cp.start()
        return cp

    w_loads = [load(own_w[i], w.at[c], i) for i, w in enumerate(weights)]
    start = [load(emb.at[pl.ds(2 * t, 2)], DZ, 4)]
    p_loads = [load(own_p[i], pk.at[c, i], 7 + i) for i in range(4)]
    for i in range(2):
        p_loads.append(load(own_p[4].at[:, pl.ds(i * 768, 768)], pk.at[c, 6 + i], 11 + i))
        p_loads.append(load(own_p[5].at[:, i], pk.at[c, 4 + i], 13 + i))
    cot_load = load(cot.at[pl.ds(2 * t, 2)], DR, 6)
    pl.semaphore_wait(barrier, 10)
    near_x, wrap_x = device(flip(x), y, z, c), device(3 - x, y, z, c)
    near_y, wrap_y = device(x, flip(y), z, c), device(x, 3 - y, z, c)

    moves = []

    def move(src, dst, peer):
        i = len(moves)
        cp = pltpu.make_async_remote_copy(
            src_ref=src, dst_ref=dst, send_sem=w_send.at[i], recv_sem=w_recv.at[i], device_id=peer, device_id_type=MESH
        )
        moves.append(cp)
        return cp

    def start_all(copies):
        for cp in copies:
            cp.start()

    def arrived(copies):
        for cp in copies:
            cp.wait_recv()

    def sent(copies):
        for cp in copies:
            cp.wait_send()

    pk_move = move(pk.at[c], pk.at[c], cross)
    def rows_of(part, n, last_x):
        h = n // 4
        return lambda w: part(w).at[pl.ds(x * n + y * h if last_x else y * n + x * h, h)]

    def piece_out(w):
        return w[1].at[pl.ds(y * 96 + (x // 2) * 48, 48), pl.ds(lax.rem(x, 2) * 384, 384)]

    def piece_down(w):
        return w[3].at[pl.ds(1152 + x * 96 + (y // 2) * 48, 48), pl.ds(lax.rem(y, 2) * 384, 384)]

    qkv_part = [lambda w, i=i: w[0].at[i] for i in range(3)]
    up_part = [lambda w, i=i: w[2].at[:, pl.ds(i * 768, 768)] for i in range(2)]
    pieces = (
        (qkv_part[0], 192, True, None),
        (qkv_part[1], 192, False, None),
        (qkv_part[2], 192, True, None),
        (lambda w: w[1], 96, False, piece_out),
        (up_part[0], 192, False, None),
        (up_part[1], 192, True, None),
        (lambda w: w[3].at[pl.ds(1152, 384)], 96, True, piece_down),
    )
    cut = [f or rows_of(part, n, last_x) for part, n, last_x, f in pieces]
    mine = [w.at[c] for w in weights]
    hops = [move(f(own_w), f(mine), cross) for f in cut]
    pl.when(c == 0)(lambda: start_all(hops))
    for cp in p_loads:
        cp.wait()
    pk_move.start()
    theirs = [w.at[1 - c] for w in weights]
    down_rows = lambda k, i: pl.ds(k * 576 + i * 192, 192)
    direct = [move(own_w[3].at[down_rows(1 - zl, i)], mine[3].at[down_rows(1 - zl, i)], cross) for i in range(3)]
    pl.when(c == 0)(lambda: start_all(direct))

    second = [
        [move(f(theirs), f(theirs), p) for p in (along_y if last_x else along_x)]
        for f, (_, _, last_x, _) in zip(cut, pieces)
    ]

    class Spread:
        def __init__(self, low, high, i, near_dev, wrap_dev):
            near, other = flip(i), 3 - i
            self.first = [move(low(i), low(i), wrap_dev), move(high(i), high(i), near_dev)]
            self.second = [
                move(low(i), low(i), near_dev),
                move(high(i), high(i), wrap_dev),
                move(low(other), low(other), near_dev),
                move(high(near), high(near), wrap_dev),
            ]

        def start(self):
            start_all(self.first)
            start_all(self.second[:2])

        def mid(self):
            arrived(self.first)
            start_all(self.second[2:])

    by_x, by_y = (x, near_x, wrap_x), (y, near_y, wrap_y)

    def spread_rows(ref, n, axis):
        h = n // 2
        return Spread(lambda k: ref.at[pl.ds(k * n, h)], lambda k: ref.at[pl.ds(k * n + h, h)], *axis)

    third = [spread_rows(part(theirs), n, by_x if last_x else by_y) for part, n, last_x, _ in pieces]
    trade = [move(theirs[3].at[down_rows(zl, i)], theirs[3].at[down_rows(zl, i)], pair) for i in range(3)]
    w_count = len(moves)

    def gather_hops():
        for k in range(7):
            arrived([hops[k]])
            start_all(second[k])

    def gather_rest(*which):
        for k in which:
            arrived(second[k])
            third[k].start()

    def gather_mids(*which):
        for k in which:
            third[k].mid()

    def hand_on(*which):
        for i in which:
            arrived([direct[i]])
            trade[i].start()

    @pl.when(c == 1)
    def _():
        gather_hops()
        gather_rest(0, 1, 2, 3)
        hand_on(0)
        gather_mids(0, 1, 2, 3)
        gather_rest(4, 5, 6)
        hand_on(1)
        start_all(hops)

    arrived([pk_move])
    for cp in start:
        cp.wait()

    def need(l, i):
        took = [cp for k in ((0, 1, 2), (3,), (4, 5), (6,))[i] for cp in third[k].second]
        incoming = took + trade if i == 3 else took
        if l == 0:
            w_loads[i].wait()
        pl.when(c == 1 - l)(lambda: arrived(incoming))

    flying = {}

    def push(kind, b):
        cp = pltpu.make_async_remote_copy(
            src_ref=X.at[kind, b],
            dst_ref=Y.at[kind, b],
            send_sem=x_send.at[kind, b],
            recv_sem=x_recv.at[kind, b],
            device_id=sibling,
            device_id_type=MESH,
        )
        cp.start()
        flying[kind, b] = cp

    def both(kind, b):
        flying.pop((kind, b)).wait()
        return X[kind, b].astype(F32) + Y[kind, b].astype(F32)

    def flag(b):
        return species[2 * t + b]

    def heads_forward(l, b):
        if l == 0:
            xin = DZ[b].astype(F32)
        else:
            low = (R[0, b] + both(1, b)).astype(BF)
            LO[0, b] = low
            xin = low.astype(F32)
        s = xin + jnp.where(flag(b) == 0, pk[l, 4], pk[l, 5])
        S[l, b] = s
        n1, _ = norm(s)
        a1 = (n1 * pk[l, 0] + pk[l, 1]).astype(BF)
        A1[l, b] = a1
        if b == 0:
            need(l, 0)
        for i, part in enumerate((Q, K, V)):
            part[l, b] = dot(a1, qkv_w[l, i]).astype(BF)
        for h in range(6):
            hs = slice(h * HEAD, h * HEAD + HEAD)
            sc = dot_back(K[l, b, :, hs], Q[l, b, :, hs]) * HEAD**-0.5
            top = jnp.max(sc, axis=0, keepdims=True)
            e = jnp.exp(sc - top)
            total = jnp.sum(e, axis=0, keepdims=True)
            PB[h] = (e * (1.0 / total)).astype(BF)
            LSE[l, b, h : h + 1] = top + jnp.log(total)
        for h in range(6):
            hs = slice(h * HEAD, h * HEAD + HEAD)
            O[l, b, :, hs] = dot_rows(PB[h], V[l, b, :, hs]).astype(BF)
        if b == 0:
            need(l, 1)
        X[0, b] = dot(O[l, b], out_w[l]).astype(BF)
        push(0, b)

    def units_forward(l, b):
        r = S[l, b] + both(0, b)
        R[l, b] = r
        n2, _ = norm(r)
        a2 = (n2 * pk[l, 2] + pk[l, 3]).astype(BF)
        A2[l, b] = a2
        if b == 0:
            need(l, 2)
        for j in range(2):
            cols = slice(j * 768, j * 768 + 768)
            u = dot(a2, up_w[l, :, cols]) + pk[l, 6 + j]
            cdf = 0.5 * (1.0 + lax.erf(u * root_half))
            G[l, b, :, cols] = (u * cdf).astype(BF)
            SL[l, b, :, cols] = (cdf + u * density_scale * jnp.exp(-0.5 * u * u)).astype(BF)
        if b == 0:
            need(l, 3)
        X[1, b] = dot(G[l, b], down_w[l]).astype(BF)
        push(1, b)

    def rows(ref, *lead):
        a = ref[lead] if lead else ref[...]
        return a.reshape(512, a.shape[-1])

    def put(slot, half, value, numbers):
        for i, number in enumerate(numbers):
            GS[slot, half, number] = value[i * UR : (i + 1) * UR]

    g_copies = {}

    def flush(l, m):
        cp = pltpu.make_async_copy(GS.at[m % 2], g_out.at[l, m], g_sem.at[m % 2])
        cp.start()
        g_copies[m % 2] = cp

    def free(slot):
        if slot in g_copies:
            g_copies.pop(slot).wait()

    def dy(l, b):
        return DR[b] if l == 1 else DX[1, b].astype(F32)

    def share(i, l):
        src, dst = ((LO, lo4), (DX, dx4))[i]
        part = dst.at[pl.ds(2 * t, 2)]
        here = pltpu.make_async_copy(src.at[l], part, out_local.at[i])
        there = pltpu.make_async_remote_copy(
            src_ref=src.at[l], dst_ref=part, send_sem=out_send.at[i], recv_sem=out_recv.at[i], device_id=far, device_id_type=MESH
        )
        return here, there

    def share_own(i, l):
        on_core(l)(lambda: start_all(share(i, l)))


    def add_up(jobs):
        for dst, pieces in jobs:
            total = pieces[0][...].astype(F32)
            for piece in pieces[1:]:
                total += piece[...].astype(F32)
            dst[...] = total.astype(BF)

    pulled = {}
    turn = [0]
    known = [None]

    def on_core(l, other=False):
        def run(step):
            if known[0] is None:
                pl.when((c != l) if other else (c == l))(step)
            elif (known[0] == l) != other:
                step()

        return run


    def pull(key, jobs):
        pad = turn[0] % 2
        turn[0] += 1
        copies, local = [], []
        for dst, pieces in jobs:
            for piece in pieces:
                k = len(copies)
                copies.append(pltpu.make_async_copy(piece, PAD.at[pad, k], pull_sem.at[pad, k]))
            local.append((dst, [PAD.at[pad, k] for k in range(len(copies) - len(pieces), len(copies))]))
        start_all(copies)
        pulled[key] = (copies, local)

    def add_pulled(key):
        copies, local = pulled[key]
        for cp in copies:
            cp.wait()
        add_up(local)

    class Ring:
        def __init__(self, i, near_dev, wrap_dev, low_of, high_of, got, low, high):
            near, other, opposite = flip(i), 3 - i, 3 - flip(i)
            self.first = [
                move(low_of(near), got(0), near_dev),
                move(high_of(other), got(2), wrap_dev),
                move(low_of(opposite), got(1), near_dev),
                move(high_of(opposite), got(3), wrap_dev),
            ]
            self.second = [move(low, got(4), wrap_dev), move(high, got(5), near_dev)]
            self.mid_jobs = lambda: [(low, [low_of(other), got(1)]), (high, [high_of(near), got(3)])]
            self.end_jobs = lambda: [(low, [low_of(i), got(0), got(4)]), (high, [high_of(i), got(2), got(5)])]

        def start(self):
            start_all(self.first[2:])
            start_all(self.first[:2])

        def mid_wait(self):
            arrived(self.first[2:])

        def end_wait(self):
            arrived(self.first[:2])
            arrived(self.second)
            sent(self.second)

        def close(self):
            sent(self.first)

    class Column:
        def __init__(self, l, of, got, kept, out, passed):
            self.l = l
            low, high = out.at[pl.ds(0, 2)], out.at[pl.ds(2, 2)]
            self.own_pair = move(of(1 - zl, 0), got(0), pair)
            self.far_pair = move(of(zl, 0), kept, pair)
            self.far_cross = [move(of(0, 1), got(1), cross), move(of(1, 1), got(2), cross)]
            self.own_second = move(high, got(4), pair)
            self.far_second = move(passed, got(3), cross)
            self.own_mid = lambda: [(high, [of(1 - zl, 1), got(2 - zl)])]
            self.far_mid = lambda: [(passed, [of(1 - zl, 0), kept])]
            self.own_end = lambda: [(low, [of(zl, 0), got(0), got(3)]), (high, [of(zl, 1), got(1 + zl), got(4)])]

        def start(self):
            @on_core(self.l)
            def _():
                self.own_pair.start()

            @on_core(self.l, True)
            def _():
                start_all((self.far_pair, *self.far_cross))

        def mid(self):
            @on_core(self.l)
            def _():
                arrived(self.far_cross)
                add_up(self.own_mid())
                self.own_second.start()

            @on_core(self.l, True)
            def _():
                arrived([self.far_pair])
                add_up(self.far_mid())
                self.far_second.start()

        def end(self):
            arrived((self.own_pair, self.own_second, self.far_second))
            sent([self.own_second])
            add_up(self.own_end())

        def close(self):
            @on_core(self.l)
            def _():
                sent([self.own_pair])

            @on_core(self.l, True)
            def _():
                sent((self.far_pair, *self.far_cross, self.far_second))

    pairs = [(m, a) for m in range(3) for a in range(2)]

    def matrix_ring(l, m, a):
        g, got, out = g_out.at[l, m, a], r1.at[l, m, a], s1.at[l, m, a]
        return Ring(
            *(by_x, by_y)[a],
            lambda k: g.at[pl.ds(k * 8, 4)],
            lambda k: g.at[pl.ds(k * 8 + 4, 4)],
            lambda j: got.at[j],
            out.at[0],
            out.at[1],
        )

    def z_column(l, m, a):
        return Column(
            l,
            lambda k, half: s1.at[l, m, a, k, pl.ds(half * 2, 2)],
            lambda j: r2.at[m, a, j],
            r2f.at[m, a],
            s2.at[m, a],
            s2f.at[m, a],
        )

    first = [[[matrix_ring(l, m, a) for a in range(2)] for m in range(3)] for l in range(2)]
    column = [[[z_column(l, m, a) for a in range(2)] for m in range(3)] for l in range(2)]


    class Tail:
        def __init__(self, m, a):
            i, j = ((x, y), (y, x))[a]
            peers = (along_y, along_x)[a]
            whole = (full_x, full_y)[a].at[m]
            group = whole.at[pl.ds(i * 8 + zl * 4, 4)]
            self.near = []
            if m < 2:
                own = whole.at[pl.ds(i * 8 + zl * 4 + j, 1)]
                out = s3.at[m, a]
                self.sums = [move(s2.at[m, a, pl.ds(wrap(j + k), 1)], r3.at[m, a, k - 1], peers[k - 1]) for k in (1, 2, 3)]
                self.job = (out, [s2.at[m, a, pl.ds(j, 1)]] + [r3.at[m, a, k] for k in range(3)])
                self.keep = pltpu.make_async_copy(out, own, keep_sem.at[m, a])
                self.near = [move(out, own, p) for p in peers]
                self.trade = move(group, group, pair)
            else:
                out = s3c.at[a]
                self.share = (r3c.at[a, j], s2.at[m, a])
                self.sums = [move(s2.at[m, a], r3c.at[a, j], p) for p in peers]
                self.job = (out, [r3c.at[a, k] for k in range(4)])
                self.keep = pltpu.make_async_copy(out, group, keep_sem.at[m, a])
                self.trade = move(out, group, pair)
            self.ring = Spread(
                lambda k: whole.at[pl.ds(k * 8 + zl * 4, 4)],
                lambda k: whole.at[pl.ds(k * 8 + (1 - zl) * 4, 4)],
                *(by_x, by_y)[a],
            )

        def own_half(self):
            self.ring.first[0].start()
            self.ring.second[0].start()

    tail = [[Tail(m, a) for a in range(2)] for m in range(3)]

    def launch(l, m):
        free(m % 2)
        for ring in first[l][m]:
            ring.start()

    def mid_pull(l, m):
        for ring in first[l][m]:
            ring.mid_wait()
        pull(("mid", l, m), [job for ring in first[l][m] for job in ring.mid_jobs()])

    def mid_send(l, m):
        add_pulled(("mid", l, m))
        for ring in first[l][m]:
            start_all(ring.second)

    def end_pull(l, m):
        for ring in first[l][m]:
            ring.end_wait()
        pull(("end", l, m), [job for ring in first[l][m] for job in ring.end_jobs()])

    def end_send(l, m):
        add_pulled(("end", l, m))
        for col in column[l][m]:
            col.start()

    def sum1_mid(l, m):
        mid_pull(l, m)
        mid_send(l, m)

    def sum1_end(l, m):
        end_pull(l, m)
        end_send(l, m)

    def sum2_mid(l, m):
        for col in column[l][m]:
            col.mid()

    def sum2_end(l, m):
        @on_core(l)
        def _():
            for col, tl in zip(column[l][m], tail[m]):
                col.end()
                start_all(tl.sums)

    def sum3(l, m):
        @on_core(l)
        def _():
            for tl in tail[m]:
                if m == 2:
                    mine, partial = tl.share
                    mine[...] = partial[...]
                arrived(tl.sums)
                add_up([tl.job])
                tl.keep.start()
                if m < 2:
                    start_all(tl.near)
                else:
                    tl.trade.start()
            if m == 2:
                for tl in tail[m]:
                    tl.keep.wait()
                    tl.own_half()

    def back1(l, m):
        @on_core(l)
        def _():
            for tl in tail[m]:
                arrived(tl.near)
                tl.keep.wait()
                tl.trade.start()
                tl.own_half()

    def back2(l, m):
        @on_core(l)
        def _():
            for tl in tail[m]:
                arrived([tl.trade])
                tl.ring.first[1].start()
                tl.ring.second[1].start()
            for tl in tail[m]:
                arrived([tl.ring.first[0]])
                tl.ring.second[2].start()

    def back3(l, m):
        @on_core(l)
        def _():
            for tl in tail[m]:
                arrived([tl.ring.first[1]])
                tl.ring.second[3].start()

    beside = {
        (1, "units"): [(launch, 1, 1)],
        (1, "cell0"): [(mid_pull, 1, 0)],
        (1, "cell1"): [(mid_send, 1, 0), (mid_pull, 1, 1)],
        (1, "heads"): [(mid_send, 1, 1), (launch, 1, 2), (share_own, 1, 1)],
        (0, "pushed"): [(end_pull, 1, 0)],
        (0, "grads_down"): [(end_send, 1, 0)],
        (0, "grads_up"): [(launch, 0, 0), (end_pull, 1, 1)],
        (0, "units"): [(end_send, 1, 1), (mid_pull, 1, 2), (launch, 0, 1)],
        (0, "cell0"): [(mid_send, 1, 2), (sum2_mid, 1, 0), (mid_pull, 0, 0)],
        (0, "cell1"): [(mid_send, 0, 0), (sum2_mid, 1, 1), (sum2_end, 1, 0)],
        (0, "heads"): [(launch, 0, 2), (mid_pull, 0, 1)],
    }

    def meanwhile(l, point):
        for f, *args in beside.get((l, point), ()):
            f(*args)

    def grads_down(l):
        free(0)
        dz = rows(DZ)
        for j in range(2):
            gd = dot_rows(rows(G, l)[:, j * 768 : j * 768 + 768], dz).astype(BF)
            for h in range(2):
                put(0, h, gd[:, h * UC : (h + 1) * UC], range(j * 16, j * 16 + 16))
        flush(l, 0)

    def units_backward(l):
        for b in range(2):
            if l == 0:
                DZ[b] = DX[1, b]
            for j in range(2):
                cols = slice(j * 768, j * 768 + 768)
                SL[l, b, :, cols] = (dot_back(DZ[b], down_w[l, cols]) * SL[l, b, :, cols].astype(F32)).astype(BF)
            X[0, b] = dot_back(SL[l, b], up_w[l]).astype(BF)
            push(0, b)
        meanwhile(l, "pushed")
        if l == 0:
            grads_down(l)
        meanwhile(l, "grads_down")
        free(1)
        du = rows(SL, l)
        gu = dot_rows(rows(A2, l), du).astype(BF)
        total = column_sum(du.astype(F32))
        for j in range(2):
            for h in range(2):
                start = j * 768 + h * UC
                put(1, j, gu[:, start : start + UC], range(h, 32, 2))
            SM[0, l, 6 + j : 7 + j] = total[:, j * 768 : j * 768 + 768]
        flush(l, 1)
        meanwhile(l, "grads_up")
        gain = bias = 0.0
        for b in range(2):
            da2 = both(0, b)
            n2, inv = norm(R[l, b])
            gain += column_sum(da2 * n2)
            bias += column_sum(da2)
            dr = dy(l, b) + norm_back(da2 * pk[l, 2], n2, inv)
            DR[b] = dr
            DZ[b] = dr.astype(BF)
        SM[0, l, 2:3] = gain
        SM[0, l, 3:4] = bias
        meanwhile(l, "units")

    def heads_backward(l):
        for b in range(2):
            DO[b] = dot_back(DZ[b], out_w[l]).astype(BF)
            for h in range(6):
                hs = slice(h * HEAD, h * HEAD + HEAD)
                sc = dot_back(K[l, b, :, hs], Q[l, b, :, hs]) * HEAD**-0.5
                p = jnp.exp(sc - LSE[l, b, h : h + 1])
                dp = dot_back(V[l, b, :, hs], DO[b, :, hs])
                pdp = p * dp
                PB[h] = p.astype(BF)
                DS[h] = (pdp - p * jnp.sum(pdp, axis=0, keepdims=True)).astype(BF)
            for h in range(6):
                hs = slice(h * HEAD, h * HEAD + HEAD)
                V[l, b, :, hs] = dot(PB[h], DO[b, :, hs]).astype(BF)
                dk = (dot(DS[h], Q[l, b, :, hs]) * HEAD**-0.5).astype(BF)
                dq = (dot_rows(DS[h], K[l, b, :, hs]) * HEAD**-0.5).astype(BF)
                K[l, b, :, hs] = dk
                Q[l, b, :, hs] = dq
            X[1, b] = (
                dot_back(Q[l, b], qkv_w[l, 0]) + dot_back(K[l, b], qkv_w[l, 1]) + dot_back(V[l, b], qkv_w[l, 2])
            ).astype(BF)
            push(1, b)
            meanwhile(l, f"cell{b}")
        free(0)
        go = dot_rows(rows(O, l), rows(DZ)).astype(BF)
        for h in range(2):
            put(0, 1, go[:, h * UC : (h + 1) * UC], range(2 + h, 32, 4))
        a1 = rows(A1, l)
        for i, d in enumerate((Q, K, V)):
            put(0, i // 2, dot_rows(a1, rows(d, l)).astype(BF), [4 * (r // 2) + r % 2 + (2 if i == 1 else 0) for r in range(16)])
        flush(l, 2)
        gain = bias = 0.0
        table = [0.0, 0.0]
        for b in range(2):
            da1 = both(1, b)
            n1, inv = norm(S[l, b])
            gain += column_sum(da1 * n1)
            bias += column_sum(da1)
            dx = DR[b] + norm_back(da1 * pk[l, 0], n1, inv)
            DX[l, b] = dx.astype(BF)
            total = column_sum(dx)
            for k in range(2):
                table[k] += jnp.where(flag(b) == k, total, 0.0)
        SM[0, l, 0:1] = gain
        SM[0, l, 1:2] = bias
        SM[0, l, 4:5] = table[0]
        SM[0, l, 5:6] = table[1]
        meanwhile(l, "heads")

    def on_first(*steps):
        def run():
            for f, *args in steps:
                f(*args)

        return run

    heads_forward(0, 0)
    pl.when(c == 1)(on_first((hand_on, 2), (gather_mids, 4, 5, 6), (start_all, direct)))
    heads_forward(0, 1)
    pl.when(c == 0)(on_first((gather_hops,), (gather_rest, 0, 1, 2, 3)))
    units_forward(0, 0)
    pl.when(c == 0)(on_first((hand_on, 0), (gather_mids, 0, 1, 2, 3), (gather_rest, 4, 5, 6)))
    units_forward(0, 1)
    pl.when(c == 0)(on_first((hand_on, 1, 2)))
    heads_forward(1, 0)
    pl.when(c == 0)(on_first((gather_mids, 4, 5, 6)))
    heads_forward(1, 1)
    share_own(0, 0)
    units_forward(1, 0)
    units_forward(1, 1)
    cot_load.wait()
    for b in range(2):
        DZ[b] = DR[b].astype(BF)
    grads_down(1)
    for b in range(2):
        LO[1, b] = (R[1, b] + both(1, b)).astype(BF)
    launch(1, 0)
    share_own(0, 1)
    for l in (1, 0):
        units_backward(l)
        heads_backward(l)

    small_steps = []

    def small_step(k, peer, both_layers=True):
        src = SM.at[k] if both_layers else SM.at[k, pl.ds(1 - c, 1)]
        dst = SMR.at[k] if both_layers else SMR.at[k, pl.ds(1 - c, 1)]
        cp = move(src, dst, peer)

        def begin():
            cp.start()

        def finish_step():
            cp.wait_recv()
            if both_layers:
                SM[k + 1] = SM[k] + SMR[k]
            else:
                small_out[...] = SM[k, pl.ds(c, 1)][0] + SMR[k, pl.ds(c, 1)][0]

        small_steps.append((begin, finish_step))

    small_from = len(moves)
    for k, peer in enumerate((near_x, wrap_x, near_y, wrap_y, pair)):
        small_step(k, peer)
    small_step(5, cross, False)

    def small_next(k):
        if k:
            small_steps[k - 1][1]()
        if k < 6:
            small_steps[k][0]()

    steps = (
        [
            (mid_send, 0, 1),
            (end_pull, 1, 2),
            (end_send, 1, 2),
            (end_pull, 0, 0),
            (end_send, 0, 0),
            (sum2_mid, 1, 2),
            (mid_pull, 0, 2),
            (mid_send, 0, 2),
            (sum2_mid, 0, 0),
            (small_next, 0),
            (end_pull, 0, 1),
            (end_send, 0, 1),
            (sum2_end, 0, 0),
            (end_pull, 0, 2),
            (end_send, 0, 2),
            (small_next, 1),
            (sum2_mid, 0, 1),
            (sum3, 0, 0),
            (sum2_end, 0, 1),
            (sum2_mid, 0, 2),
            (small_next, 2),
            (back1, 0, 0),
            (sum3, 0, 1),
            (sum2_end, 0, 2),
            (small_next, 3),
            (back1, 0, 1),
            (back2, 0, 0),
            (sum3, 0, 2),
            (small_next, 4),
            (back2, 0, 1),
            (back3, 0, 0),
            (small_next, 5),
            (back2, 0, 2),
            (small_next, 6),
            (share_own, 1, 0),
            (back3, 0, 1),
            (back3, 0, 2),
        ],
        [
            (mid_send, 0, 1),
            (end_pull, 1, 2),
            (end_send, 1, 2),
            (end_pull, 0, 0),
            (end_send, 0, 0),
            (sum3, 1, 0),
            (sum2_end, 1, 1),
            (mid_pull, 0, 2),
            (mid_send, 0, 2),
            (sum2_mid, 1, 2),
            (sum2_mid, 0, 0),
            (small_next, 0),
            (back1, 1, 0),
            (sum3, 1, 1),
            (sum2_end, 1, 2),
            (end_pull, 0, 1),
            (end_send, 0, 1),
            (end_pull, 0, 2),
            (end_send, 0, 2),
            (small_next, 1),
            (sum2_mid, 0, 1),
            (back2, 1, 0),
            (back1, 1, 1),
            (sum3, 1, 2),
            (sum2_mid, 0, 2),
            (small_next, 2),
            (back2, 1, 1),
            (small_next, 3),
            (back3, 1, 0),
            (back2, 1, 2),
            (small_next, 4),
            (back3, 1, 1),
            (small_next, 5),
            (back3, 1, 2),
            (small_next, 6),
        ],
    )
    pulls_so_far = turn[0]

    def finish_on(core):
        def run():
            known[0], turn[0] = core, pulls_so_far
            for f, *args in steps[core]:
                f(*args)
            known[0] = None

        pl.when(c == core)(run)

    finish_on(0)
    finish_on(1)
    for m, a in pairs:
        arrived(tail[m][a].ring.second)

    for i in range(2):
        for cp in share(i, c):
            cp.wait()
    sent(moves[:w_count])
    for l in range(2):
        for m, a in pairs:
            first[l][m][a].close()
            column[l][m][a].close()
    for m, a in pairs:
        tl = tail[m][a]
        for copies in (tl.sums, tl.near, [tl.trade], tl.ring.first, tl.ring.second):
            sent(copies)
    sent(moves[small_from : small_from + 6])
    assert len(moves) <= MOVES


def run_layers(species, emb, cot, own_p, own_w):
    anywhere = pl.BlockSpec(memory_space=pl.ANY)
    dma = pltpu.SemaphoreType.DMA
    vm = lambda *shape: pltpu.VMEM(shape, BF)
    vf = lambda *shape: pltpu.VMEM(shape, F32)
    cells = (2, 256, 768)
    units = lambda *shape: pltpu.VMEM((*shape, UR, UC), BF)
    scratch = [
        vm(2, 3, 768, 384),
        vm(2, 384, 768),
        vm(2, 768, 1536),
        vm(2, 1536, 768),
        vf(2, 8, 1, 768),
        vf(2, *cells),
        vm(2, *cells),
        vm(2, 2, 256, 384),
        vm(2, 2, 256, 384),
        vm(2, 2, 256, 384),
        vf(2, 2, 8, 256),
        vm(2, 2, 256, 384),
        vf(2, *cells),
        vm(2, *cells),
        vm(2, 2, 256, 1536),
        vm(2, 2, 256, 1536),
        vm(2, *cells),
        vm(2, *cells),
        vf(*cells),
        vm(*cells),
        vm(2, 256, 384),
        vm(6, 256, 256),
        vm(6, 256, 256),
        vm(2, *cells),
        vm(2, *cells),
        units(2, 2, 32),
        units(2, 12, 4),
        vf(6, 2, 8, 768),
        vf(6, 2, 8, 768),
        units(2, 3, 2, 2, 4),
        units(3, 2, 4),
        units(3, 2, 2),
        units(3, 2, 1),
        units(3, 2, 5, 2),
        units(3, 2, 2),
        units(3, 2, 3, 1),
        units(2, 4),
        units(2, 4, 4),
        dma((15,)),
        dma((2, 2)),
        dma((2, 2)),
        dma((2,)),
        dma((2,)),
        dma((2,)),
        dma((2,)),
        dma((MOVES,)),
        dma((MOVES,)),
        dma((2, 12)),
        dma((3, 2)),
    ]
    hbm = lambda *shape: jax.ShapeDtypeStruct((*shape, UR, UC), BF)
    return pl.pallas_call(
        layers_kernel,
        out_shape=(
            jax.ShapeDtypeStruct((4, 256, 768), BF),
            jax.ShapeDtypeStruct((4, 256, 768), BF),
            hbm(2, 3, 2, 32),
            hbm(2, 3, 2, 6, 4),
            hbm(3, 32),
            hbm(3, 32),
            jax.ShapeDtypeStruct((8, 768), F32),
        ),
        in_specs=[pl.BlockSpec(memory_space=pltpu.SMEM)] + [anywhere] * 12,
        out_specs=(*[anywhere] * 6, pl.BlockSpec(memory_space=pltpu.VMEM)),
        scratch_shapes=scratch,
        compiler_params=pltpu.CompilerParams(collective_id=1, has_side_effects=True, vmem_limit_bytes=63 * 2**20),
        name="layers",
    )(species, emb, cot, *own_p, *own_w)


def widen_kernel(gx, gy, lo, dx, small, *out):
    down, up, qkv, attn, layer_out, input_grad, g1, b1, g2, b2, ub, table = out
    for u in range(4):
        rows = slice(u * UR, (u + 1) * UR)
        down[rows, :UC] = gx[0, u].astype(F32)
        down[rows, UC:] = gy[0, u].astype(F32)
    for r in range(2):
        rows = slice(r * UR, (r + 1) * UR)
        for h in range(2):
            up[rows, h * UC : (h + 1) * UC] = gx[1, 2 * r + h].astype(F32)
            up[rows, (2 + h) * UC : (3 + h) * UC] = gy[1, 2 * r + h].astype(F32)
        qkv[0, rows] = gx[2, r].astype(F32)
        qkv[1, rows] = gx[2, 2 + r].astype(F32)
        qkv[2, rows] = gy[2, r].astype(F32)
        attn[:, r * UC : (r + 1) * UC] = gy[2, 2 + r].astype(F32)
    layer_out[...] = lo[...].astype(F32)
    input_grad[...] = dx[...].astype(F32)
    for i, ref in enumerate((g1, b1, g2, b2)):
        ref[...] = small[i : i + 1]
    table[...] = small[4:6]
    ub[:, :768] = small[6:7]
    ub[:, 768:] = small[7:8]


def widen(gx, gy, lo, dx, small):
    whole = lambda *shape: pl.BlockSpec(shape, lambda i: (0,) * len(shape))
    blocks = pl.BlockSpec((3, 4, UR, UC), lambda i: (0, i, 0, 0))
    by_row = lambda *shape: pl.BlockSpec(shape, lambda i: (i,) + (0,) * (len(shape) - 1))
    return pl.pallas_call(
        widen_kernel,
        grid=(8,),
        in_specs=[blocks, blocks, by_row(128, 768), by_row(128, 768), whole(8, 768)],
        out_specs=[
            by_row(192, 768),
            by_row(96, 1536),
            pl.BlockSpec((3, 96, UC), lambda i: (0, i, 0)),
            by_row(48, 768),
            by_row(128, 768),
            by_row(128, 768),
            *[whole(1, 768)] * 4,
            whole(1, 1536),
            whole(2, 768),
        ],
        out_shape=[
            jax.ShapeDtypeStruct(shape, F32)
            for shape in (
                (1536, 768),
                (768, 1536),
                (3, 768, UC),
                (384, 768),
                (1024, 768),
                (1024, 768),
                *[(1, 768)] * 4,
                (1, 1536),
                (2, 768),
            )
        ],
        name="widen",
    )(gx, gy, lo.reshape(1024, 768), dx.reshape(1024, 768), small)


def shards(
    embeddings,
    species,
    ln1_gain,
    ln1_bias,
    qkv_weight,
    out_weight,
    ln2_gain,
    ln2_bias,
    up_weight,
    up_bias,
    down_weight,
    species_bias,
    out_cotangent,
):
    own_w = (qkv_weight[0].transpose(1, 0, 2), out_weight[0], up_weight[0], down_weight[0])
    own_p = (ln1_gain, ln1_bias, ln2_gain, ln2_bias, up_bias, species_bias)
    lo4, dx4, _, _, full_x, full_y, small = run_layers(species, embeddings, out_cotangent, own_p, own_w)
    down, up, qkv, attn, layer_out, input_grad, g1, b1, g2, b2, ub, table = widen(full_x, full_y, lo4, dx4, small)
    return (
        layer_out.reshape(1, 4, 256, 768),
        input_grad.reshape(1, 4, 256, 768),
        g1,
        b1,
        qkv.transpose(1, 0, 2)[None],
        attn[None],
        g2,
        b2,
        up[None],
        ub,
        down[None],
        table[None],
    )


def solution(mesh):
    placed = (
        P("dp", None, None),
        P("dp"),
        P("section", None),
        P("section", None),
        P("section", None, None, "tensor"),
        P("section", "tensor", None),
        P("section", None),
        P("section", None),
        P("section", None, "tensor"),
        P("section", "tensor"),
        P("section", "tensor", None),
        P("section", None, None),
        P("dp", None, None),
    )
    return jax.shard_map(
        shards,
        mesh=mesh,
        in_specs=placed,
        out_specs=(
            P("section", "dp", None, None),
            P("section", "dp", None, None),
            P("section", None),
            P("section", None),
            P("section", None, None, "tensor"),
            P("section", "tensor", None),
            P("section", None),
            P("section", None),
            P("section", None, "tensor"),
            P("section", "tensor"),
            P("section", "tensor", None),
            P("section", None, None),
        ),
        check_vma=False,
    )
```
